128 devices in a mesh: dt: 8 (over x, y_lo), tmpl: 16 (over y_hi, z, core).
Axes of the slice: x: 4, y: 4 (y_hi: 2, y_lo: 2; y = y_hi * 2 + y_lo), z: 4, core: 2. Of those that a mesh axis runs over, the one named last changes fastest.
Arguments:
- strain: bfloat16 [8, 3, 2, 96, 256], P('dt', None, None, 'tmpl'), may hold values from -6 to 6
- templates: bfloat16 [1536, 2, 96, 256], P(('dt', 'tmpl')), may hold values from -6 to 6
- live_count: int32 [8, 16], P('dt', 'tmpl'), may hold values from 0 to 12, as said below
- chi_edges: int32 [1536, 15], P(('dt', 'tmpl')), may hold values from 1 to 95, as said below
- shifts: int32 [8, 3], replicated, may hold values from -41 to 41
Outputs:
- best: float32 [8, 8, 8], P(None, 'dt')
The draws below stay inside these ranges and needn't reach their ends.
Inputs may be any that keep to these rules, and one draw needn't show every extreme that they name: `live_count`: in each row the counts sum to 96; every row has a device with 12 templates and one with none. `chi_edges`: each row is strictly increasing.
All inputs are finite; a program needn't handle non-finite values.
Results may differ from the reference program's by a relative error of at most 0.00081.
Values may be sent and summed in bfloat16 or wider, within the bound.
No kernel may reach another device: no remote copies, remote signals or barrier semaphores. Data moves between devices by JAX's collectives and lax.ppermute only.
A program may use at most 64 MiB of HBM per device.

```python
import math
import jax
import jax.numpy as jnp
from jax import lax

NDET = 3
FB = 256
NBLK = 96
NFFT = 1048576
FLOW = 5120
NBIN = 16
TW = 128
TX = 256
WIN = 16
SLIDE = 41
KAVG = 6
SEGS = 8
TEMPLATES = 1536
N_DT = 8
N_TMPL = 16


def draw_live_count(key, part):
    key = jax.random.fold_in(key, 11)
    row_keys = jax.random.split(key, N_DT)

    def one_row(row_key):
        order_key, delta_key = jax.random.split(row_key)
        order = jax.random.permutation(order_key, N_TMPL)
        delta = jax.random.randint(delta_key, (N_TMPL // 2,), 0, KAVG + 1)
        delta = delta.at[0].set(KAVG)
        paired = jnp.stack([KAVG + delta, KAVG - delta], axis=1).reshape(-1)
        return jnp.zeros((N_TMPL,), jnp.int32).at[order].set(paired.astype(jnp.int32))
    return jax.vmap(one_row)(row_keys)


def draw_chi_edges(key, part):
    key = jax.random.fold_in(key, 23)
    row_keys = jax.random.split(key, TEMPLATES)

    def one_row(row_key):
        picked = jax.random.permutation(row_key, NBLK - 1)[:NBIN - 1] + 1
        return jnp.sort(picked).astype(jnp.int32)
    return jax.vmap(one_row)(row_keys)


def set_ends(drawn, rng, smallest, largest):
    longest = drawn.shape.index(max(drawn.shape))
    spots = []
    for shift in (0, 1):
        where = [jax.random.randint(jax.random.fold_in(rng, axis), (), 0, length) for axis, length in enumerate(drawn.shape)]
        where[longest] = (where[longest] + shift) % drawn.shape[longest]
        spots.append(tuple(where))
    return drawn.at[spots[0]].set(smallest).at[spots[1]].set(largest)


def levels(rng, dims, cuts, least, top_value):
    loudness = 1.0
    for position, shards_of in cuts:
        heights = jax.random.uniform(jax.random.fold_in(jax.random.fold_in(rng, 6), position), (shards_of,), jnp.float32, least / len(cuts), top_value / len(cuts))
        loudness = loudness * jnp.repeat(jnp.exp(heights), dims[position] // shards_of).reshape((-1,) + (1,) * (len(dims) - 1 - position))
    return loudness


def normal_values(key, extent, spread, bound, shards=(), held_as=jnp.bfloat16):
    loudness = levels(key, extent, shards, -0.22, 0.18) if shards else 1.0
    drawn = jax.random.normal(key, extent, jnp.float32) * spread * loudness
    return jnp.minimum(jnp.maximum(drawn, -bound), bound).astype(held_as)


def setup_inputs(seed: int = 0) -> dict:
    key_of = jax.random.split(jax.random.key(seed), 6)
    strain = normal_values(key_of[0], (SEGS, NDET, 2, NBLK, FB), 1.0, 6.0, ((0, 8), (3, 16)))
    templates = normal_values(key_of[1], (TEMPLATES, 2, NBLK, FB), 1.0, 6.0, ((0, 128),))
    live_count = draw_live_count(jax.random.fold_in(key_of[5], 71), 0)
    chi_edges = draw_chi_edges(jax.random.fold_in(key_of[5], 71), 0)
    shifts = set_ends(jax.random.randint(key_of[4], (SEGS, NDET), 0 - SLIDE, SLIDE + 1), jax.random.fold_in(key_of[4], 1), 0 - SLIDE, SLIDE).astype(jnp.int32)
    return dict(strain=strain, templates=templates, live_count=live_count, chi_edges=chi_edges, shifts=shifts)


TWO_PI = 2.0 * math.pi
EPSILON = 1e-05

def stride_turns(values):
    spacing = NFFT // FB
    return (values % FB * spacing + values % NFFT) % NFFT

def local_table():
    bins = jnp.arange(FB, dtype=jnp.int32)
    times = jnp.arange(TX, dtype=jnp.int32)
    turns = stride_turns((bins[:, None] * times[None, :]).astype(jnp.int32))
    angle = turns.astype(jnp.float32) * jnp.float32(TWO_PI / NFFT)
    cosine = jnp.cos(angle)
    sine = jnp.sin(angle)
    upper = jnp.concatenate([cosine, sine], axis=1)
    lower = jnp.concatenate([-sine, cosine], axis=1)
    return jnp.concatenate([upper, lower], axis=0).astype(jnp.bfloat16)

def twiddle(blocks):
    times = jnp.arange(TX, dtype=jnp.int32)
    base = (FLOW + blocks.astype(jnp.int32) * FB).astype(jnp.int32)
    turns = stride_turns((base[:, None] * times[None, :]).astype(jnp.int32))
    angle = turns.astype(jnp.float32) * jnp.float32(TWO_PI / NFFT)
    return (jnp.cos(angle), jnp.sin(angle))

def edge_onehot(edges):
    blocks = jnp.arange(NBLK, dtype=jnp.int32)
    bin_of = lax.optimization_barrier(jnp.sum((edges[:, :, None] <= blocks[None, None, :]).astype(jnp.int32), axis=1))
    labels = jnp.arange(NBIN, dtype=jnp.int32)
    return (bin_of[:, None, :] == labels[None, :, None]).astype(jnp.float32)

def prepare(template_set, onehot):
    wide = template_set.astype(jnp.float32)
    block_power = lax.optimization_barrier(jnp.sum(wide * wide, axis=(1, 3)))
    sigma2 = lax.optimization_barrier(jnp.sum(block_power, axis=1)) + EPSILON
    in_bins = jnp.einsum('kbj,kj->kb', onehot, block_power, precision=lax.Precision.HIGHEST)
    return (sigma2, (in_bins + EPSILON) / sigma2[:, None])

def correlate(strain_blocks, template_blocks, blocks, phase_table):
    strain_real = strain_blocks[:, 0].astype(jnp.float32)[:, None]
    strain_imag = strain_blocks[:, 1].astype(jnp.float32)[:, None]
    templ_real = template_blocks[:, 0].astype(jnp.float32)[None]
    templ_imag = template_blocks[:, 1].astype(jnp.float32)[None]
    prod_real = strain_real * templ_real + strain_imag * templ_imag
    prod_imag = strain_imag * templ_real - strain_real * templ_imag
    stacked = jnp.concatenate([prod_real, prod_imag], axis=-1).astype(jnp.bfloat16)
    detectors, count, nblocks = (stacked.shape[0], stacked.shape[1], stacked.shape[2])
    flat = stacked.reshape(-1, 2 * FB)
    raw = jnp.dot(flat.astype(jnp.float32), phase_table.astype(jnp.float32), precision=lax.Precision.HIGHEST)
    raw = raw.reshape(detectors, count, nblocks, 2, TX)
    cos_turn, sin_turn = twiddle(blocks)
    raw_real = raw[:, :, :, 0, :]
    raw_imag = raw[:, :, :, 1, :]
    out_real = cos_turn * raw_real - sin_turn * raw_imag
    out_imag = cos_turn * raw_imag + sin_turn * raw_real
    return jnp.concatenate([out_real, out_imag], axis=-1)

def statistic(partial_value, onehot, fraction, sigma2, shift_row, live):
    binned = jnp.einsum('kbj,dkjt->dkbt', onehot, partial_value, precision=lax.Precision.HIGHEST)
    series = lax.optimization_barrier(jnp.sum(binned, axis=2))
    series_real = series[..., :TX]
    series_imag = series[..., TX:]
    snr = jnp.sqrt(series_real * series_real + series_imag * series_imag) / jnp.sqrt(2.0 * sigma2)[None, :, None]
    frac_full = fraction[None, :, :, None]
    gap_real = binned[..., :TX] - frac_full * series_real[:, :, None, :]
    gap_imag = binned[..., TX:] - frac_full * series_imag[:, :, None, :]
    chi_square = lax.optimization_barrier(jnp.sum((gap_real * gap_real + gap_imag * gap_imag) / (fraction * sigma2[:, None])[None, :, :, None], axis=2))
    reduced = chi_square / (2.0 * NBIN - 2.0)
    factor = jnp.where(reduced > 1.0, ((1.0 + reduced * reduced * reduced) * 0.5) ** (-1.0 / 6.0), 1.0)
    newsnr = snr * factor
    margin = (TX - TW) // 2
    squares = jnp.zeros((newsnr.shape[1], TW), jnp.float32)
    for detector in range(newsnr.shape[0]):
        moved = lax.dynamic_slice_in_dim(newsnr[detector], (margin + shift_row[detector]).astype(jnp.int32), TW, 1)
        squares = squares + moved * moved
    network = jnp.sqrt(squares) * live[:, None]
    windows = lax.optimization_barrier(jnp.max(network.reshape(network.shape[0], TW // WIN, WIN), axis=2))
    return lax.optimization_barrier(jnp.max(windows, axis=0))

def reference(strain, templates, live_count, chi_edges, shifts):
    rows = live_count.shape[0]
    columns = live_count.shape[1]
    slots = templates.shape[0] // (rows * columns)
    phase_table = local_table()
    blocks = jnp.arange(NBLK, dtype=jnp.int32)
    live = (jnp.arange(slots, dtype=jnp.int32)[None, None, :] < live_count[:, :, None]).reshape(rows, columns * slots)
    per_row = KAVG * columns

    def row_best(row):
        mask = lax.dynamic_index_in_dim(live, row, 0, keepdims=False)
        chosen = jnp.nonzero(mask, size=per_row)[0].astype(jnp.int32) + (row * columns * slots).astype(jnp.int32)
        chosen_templates = jnp.take(templates, chosen, axis=0)
        onehot = edge_onehot(jnp.take(chi_edges, chosen, axis=0))
        sigma2, fraction = prepare(chosen_templates, onehot)
        ones = jnp.ones((per_row,), jnp.float32)

        def segment_best(segment):
            strain_segment = lax.dynamic_index_in_dim(strain, segment, 0, keepdims=False)
            partial_value = correlate(strain_segment, chosen_templates, blocks, phase_table)
            shift_row = lax.dynamic_index_in_dim(shifts, segment, 0, keepdims=False)
            return statistic(partial_value, onehot, fraction, sigma2, shift_row, ones)
        return lax.map(segment_best, jnp.arange(SEGS, dtype=jnp.int32))
    results = lax.map(row_best, jnp.arange(rows, dtype=jnp.int32))
    return jnp.transpose(results, (1, 0, 2))
```

```python
import math

import ml_dtypes
import numpy as np

import jax
import jax.numpy as jnp
from jax import lax
from jax.experimental import pallas as pl
from jax.experimental.pallas import tpu as pltpu
from jax.sharding import PartitionSpec as P

FB = 256
NBLK = 96
NFFT = 1048576
FLOW = 5120
STRIDE = 4097
NBIN = 16
TW = 128
MARGIN = 64
WIN = 16
NWIN = TW // WIN
NDET = 3
SEGS = 8
SLOTS = 12
NSL = 16
JS = NBLK // NSL
ROWS = NDET * SEGS
EPSILON = 1e-05
TWO_PI = 2.0 * math.pi
AXES = ("dt", "tmpl")


def place_of(index):
    dt, tm = divmod(index, 16)
    return (dt // 2, (tm // 8) * 2 + dt % 2, (tm // 2) % 4, tm % 2)


def index_of(x, y, z, core):
    return (x * 2 + y % 2) * 16 + (y // 2) * 8 + z * 2 + core


def near(a):
    return a ^ 1


def far(a):
    return 3 - a


def swap_with(value, axis, partner):
    pairs = []
    for index in range(128):
        place = list(place_of(index))
        place[axis] = partner(place[axis])
        pairs.append((index, index_of(*place)))
    return lax.ppermute(value, AXES, pairs)


def tables():
    n = FLOW + np.arange(NBLK * FB, dtype=np.int64)
    tau = np.arange(TW, dtype=np.int64)
    turns = (n[:, None] * tau[None, :] * STRIDE) % NFFT
    angle = turns.astype(np.float64) * (TWO_PI / NFFT)
    cosine, sine = np.cos(angle), np.sin(angle)
    whole = np.concatenate([-sine, cosine, sine], axis=1).astype(ml_dtypes.bfloat16)
    return whole.reshape(NSL, JS, FB, 3 * TW)


def gather_strain(shard):
    x = jnp.transpose(shard[0], (2, 1, 0, 3)).reshape(JS, 2 * NDET, 1, FB)
    for axis, partner in ((0, near), (0, far), (1, near)):
        x = jnp.concatenate([x, swap_with(x, axis, partner)], axis=2)
    x = x[None]
    y = swap_with(x, 1, far)
    y = jnp.concatenate([y[:, :, :, 4:], y[:, :, :, :4]], axis=3)
    x = jnp.concatenate([x, y], axis=0)
    x = x.reshape(2, JS, 2 * ROWS, FB)
    for axis, partner in ((2, near), (2, far), (3, near)):
        x = jnp.concatenate([x, swap_with(x, axis, partner)], axis=0)
    return x


def arrival_order():
    dt = lax.axis_index("dt")
    tm = lax.axis_index("tmpl")
    x, y_lo = dt // 2, dt % 2
    y_hi, z, core = tm // 8, (tm // 2) % 4, tm % 2
    p = jnp.arange(SEGS, dtype=jnp.int32)
    q = jnp.arange(NSL, dtype=jnp.int32)

    def ring(a, first, second):
        a = jnp.where(second == 1, 3 - a, a)
        return a ^ first

    segs = ring(x, p % 2, p // 2 % 2) * 2 + (y_lo ^ (p // 4))
    slices = (y_hi ^ (q % 2)) * 8 + ring(z, q // 2 % 2, q // 4 % 2) * 2 + (core ^ (q // 8))
    return segs, slices


def phase(turns):
    angle = turns.astype(jnp.float32) * jnp.float32(TWO_PI / NFFT)
    return jnp.stack([jnp.cos(angle), jnp.sin(angle)])


def kernel(
    sl_ref, segs_ref, live_ref, bin_ref, frac_ref, inv_ref, half_ref,
    strain_ref, table_ref, templ_ref, start_ref, local_ref, step_ref,
    out_ref, prod_ref, rot_ref, best_ref, *binned,
):
    g = pl.program_id(0)

    @pl.when(g == 0)
    def _():
        for ref in binned:
            ref[...] = jnp.zeros_like(ref)

    sc, ss = start_ref[0, 0], start_ref[0, 1]
    for half in range(2):
        cols = slice(half * 128, half * 128 + 128)
        lc, ls = local_ref[0, :, cols], local_ref[1, :, cols]
        rot_ref[0, :, cols] = sc * lc - ss * ls
        rot_ref[1, :, cols] = sc * ls + ss * lc

    def one_block(jj, slot):
        both = strain_ref[0, jj].astype(jnp.float32)
        raw_r, raw_i = both[:ROWS], both[ROWS:]
        rc, rs = rot_ref[0], rot_ref[1]
        sr = raw_r * rc - raw_i * rs
        si = raw_r * rs + raw_i * rc
        su = sr + si
        pc = jnp.concatenate([step_ref[0], step_ref[0]], axis=1)
        ps = jnp.concatenate([step_ref[1], step_ref[1]], axis=1)
        rot_ref[0] = rc * pc - rs * ps
        rot_ref[1] = rc * ps + rs * pc
        for pair in range(SLOTS // 2):
            real, imag = [], []
            for k in (2 * pair, 2 * pair + 1):
                h = templ_ref[0, jj, k:k + 1, :]
                v = templ_ref[0, jj, SLOTS + k:SLOTS + k + 1, :]
                w = templ_ref[0, jj, 2 * SLOTS + k:2 * SLOTS + k + 1, :]
                k1 = h * su
                real.append(k1 - si * w)
                imag.append(k1 - sr * v)
            rows = slice(2 * ROWS * pair, 2 * ROWS * (pair + 1))
            prod_ref[slot, rows, :FB] = jnp.concatenate(real, axis=0).astype(jnp.bfloat16)
            prod_ref[slot, rows, FB:] = jnp.concatenate(imag, axis=0).astype(jnp.bfloat16)
        weights = jnp.concatenate([table_ref[0, jj, :, TW:], table_ref[0, jj, :, :2 * TW]], axis=0)
        series = jnp.dot(prod_ref[slot], weights, preferred_element_type=jnp.float32)
        j = sl_ref[g] * JS + jj
        for k in range(SLOTS):
            b = bin_ref[k, j]
            binned[k][b] += series[k * ROWS:(k + 1) * ROWS]

    def two_blocks(m, carry):
        one_block(2 * m, 0)
        one_block(2 * m + 1, 1)
        return carry

    lax.fori_loop(0, JS // 2, two_blocks, 0)

    @pl.when(g == NSL - 1)
    def _():
        best = jnp.zeros((SEGS, TW), jnp.float32)
        for k in range(SLOTS):
            total = binned[k][0]
            for b in range(1, NBIN):
                total = total + binned[k][b]
            chi = jnp.zeros((ROWS, TW), jnp.float32)
            for b in range(NBIN):
                gap = binned[k][b] - frac_ref[k, b] * total
                gap = gap * gap
                chi = chi + (gap[:, :TW] + gap[:, TW:]) * inv_ref[k, b]
            power = total * total
            snr2 = (power[:, :TW] + power[:, TW:]) * half_ref[k]
            reduced = chi / (2.0 * NBIN - 2.0)
            cube = (1.0 + reduced * reduced * reduced) * 0.5
            factor = jnp.where(reduced > 1.0, jnp.exp(jnp.log(cube) * (-1.0 / 3.0)), 1.0)
            new2 = snr2 * factor
            net2 = new2[:SEGS] + new2[SEGS:2 * SEGS] + new2[2 * SEGS:]
            best = jnp.where(k < live_ref[0], jnp.maximum(best, net2), best)
        best = jnp.sqrt(best)
        best_ref[...] = jnp.concatenate(
            [jnp.max(best[:, w * WIN:(w + 1) * WIN], axis=1, keepdims=True) for w in range(NWIN)], axis=1
        )
        for p in range(SEGS):
            out_ref[pl.ds(segs_ref[p], 1), :] = best_ref[p:p + 1, :]


def search(sl, segs, live, bin_of, frac, inv, half, strain, templ, start, local, step):
    grid_spec = pltpu.PrefetchScalarGridSpec(
        num_scalar_prefetch=7,
        grid=(NSL,),
        in_specs=[
            pl.BlockSpec((1, JS, 2 * ROWS, FB), lambda g, sl, *_: (g, 0, 0, 0)),
            pl.BlockSpec((1, JS, FB, 3 * TW), lambda g, sl, *_: (sl[g], 0, 0, 0)),
            pl.BlockSpec((1, JS, 3 * SLOTS, FB), lambda g, sl, *_: (sl[g], 0, 0, 0)),
            pl.BlockSpec((1, 2, ROWS, TW), lambda g, sl, *_: (g, 0, 0, 0)),
            pl.BlockSpec((2, ROWS, FB), lambda g, sl, *_: (0, 0, 0)),
            pl.BlockSpec((2, ROWS, TW), lambda g, sl, *_: (0, 0, 0)),
        ],
        out_specs=pl.BlockSpec((SEGS, NWIN), lambda g, sl, *_: (0, 0)),
        scratch_shapes=[
            pltpu.VMEM((2, SLOTS * ROWS, 2 * FB), jnp.bfloat16),
            pltpu.VMEM((2, ROWS, FB), jnp.float32),
            pltpu.VMEM((SEGS, NWIN), jnp.float32),
        ] + [pltpu.VMEM((NBIN, ROWS, 2 * TW), jnp.float32) for _ in range(SLOTS)],
    )
    return pl.pallas_call(
        kernel,
        out_shape=jax.ShapeDtypeStruct((SEGS, NWIN), jnp.float32),
        grid_spec=grid_spec,
        compiler_params=pltpu.CompilerParams(
            dimension_semantics=("arbitrary",), vmem_limit_bytes=40 * 1024 * 1024
        ),
        name="search",
    )(sl, segs, live, bin_of, frac, inv, half, strain, tables(), templ, start, local, step)


def per_device(strain, templates, live_count, chi_edges, shifts):
    segs, slices = arrival_order()
    gathered = gather_strain(strain)

    blocks = jnp.arange(NBLK, dtype=jnp.int32)
    bin_of = jnp.sum((chi_edges[:, :, None] <= blocks[None, None, :]).astype(jnp.int32), axis=1)
    labels = jnp.arange(NBIN, dtype=jnp.int32)
    onehot = (bin_of[:, None, :] == labels[None, :, None]).astype(jnp.float32)
    wide = templates.astype(jnp.float32)
    block_power = jnp.sum(wide * wide, axis=(1, 3))
    sigma2 = jnp.sum(block_power, axis=1) + EPSILON
    in_bins = jnp.sum(onehot * block_power[:, None, :], axis=2)
    frac = (in_bins + EPSILON) / sigma2[:, None]
    inv = 1.0 / (frac * sigma2[:, None])
    half = 1.0 / (2.0 * sigma2)

    real, imag = wide[:, 0], wide[:, 1]
    templ = jnp.concatenate([real, real + imag, real - imag], axis=0)
    templ = jnp.transpose(templ, (1, 0, 2)).reshape(NSL, JS, 3 * SLOTS, FB)

    first = (MARGIN + jnp.take(shifts, segs, axis=0)).T.reshape(ROWS)
    bins = jnp.arange(FB, dtype=jnp.int32)
    local = phase((first[:, None] * bins[None, :] * STRIDE) % NFFT)
    starts = (FLOW // FB + slices * JS) * FB
    start = phase((first[None, :] * starts[:, None]) % NFFT)
    start = jnp.broadcast_to(jnp.transpose(start, (1, 0, 2))[..., None], (NSL, 2, ROWS, TW))
    step = phase(first * FB)
    step = jnp.broadcast_to(step[..., None], (2, ROWS, TW))

    best = search(
        slices, segs, live_count[0], bin_of, frac, inv, half, gathered, templ, start, local, step
    )
    for axis, partner in ((3, near), (2, near), (2, far), (1, lambda y: y ^ 2)):
        best = jnp.maximum(best, swap_with(best, axis, partner))
    return best[:, None, :]


def solution(mesh):
    in_specs = (
        P("dt", None, None, "tmpl", None),
        P(("dt", "tmpl"), None, None, None),
        P("dt", "tmpl"),
        P(("dt", "tmpl"), None),
        P(),
    )
    out_specs = P(None, "dt", None)
    return jax.shard_map(
        per_device, mesh=mesh, in_specs=in_specs, out_specs=out_specs, check_vma=False
    )
```

```python
import math

import ml_dtypes
import numpy as np

import jax
import jax.numpy as jnp
from jax import lax
from jax.experimental import pallas as pl
from jax.experimental.pallas import tpu as pltpu
from jax.sharding import PartitionSpec as P

FB = 256
NBLK = 96
NFFT = 1048576
FLOW = 5120
STRIDE = 4097
NBIN = 16
TW = 128
MARGIN = 64
WIN = 16
NWIN = TW // WIN
NDET = 3
SEGS = 8
SLOTS = 12
NSL = 16
JS = NBLK // NSL
ROWS = NDET * SEGS
EPSILON = 1e-05
TWO_PI = 2.0 * math.pi
AXES = ("dt", "tmpl")


def place_of(index):
    dt, tm = divmod(index, 16)
    return (dt // 2, (tm // 8) * 2 + dt % 2, (tm // 2) % 4, tm % 2)


def index_of(x, y, z, core):
    return (x * 2 + y % 2) * 16 + (y // 2) * 8 + z * 2 + core


def near(a):
    return a ^ 1


def far(a):
    return 3 - a


def swap_with(value, move):
    pairs = [(index, index_of(*move(*place_of(index)))) for index in range(128)]
    return lax.ppermute(value, AXES, pairs)


def x_near(x, y, z, core):
    return (near(x), y, z, core)


def x_far(x, y, z, core):
    return (far(x), y, z, core)


def y_near(x, y, z, core):
    return (x, near(y), z, core)


def y_far(x, y, z, core):
    return (x, far(y), z, core)


def z_near(x, y, z, core):
    return (x, y, near(z), core)


def z_far(x, y, z, core):
    return (x, y, far(z), core)


def y_across(x, y, z, core):
    return (x, y ^ 2, z, core)


def other_core(x, y, z, core):
    return (x, y, z, core ^ 1)


def by_core(first, second):
    return lambda x, y, z, core: (second if core else first)(x, y, z, core)


def tables():
    tau = np.arange(TW, dtype=np.int64)
    bins = np.arange(FB, dtype=np.int64)
    angle = ((bins[:, None] * tau[None, :] * STRIDE) % NFFT).astype(np.float64) * (TWO_PI / NFFT)
    cosine, sine = np.cos(angle), np.sin(angle)
    local = np.block([[cosine, sine], [-sine, cosine]]).astype(ml_dtypes.bfloat16)
    base = FLOW + np.arange(NBLK, dtype=np.int64) * FB
    angle = ((base[:, None] * tau[None, :] * STRIDE) % NFFT).astype(np.float64) * (TWO_PI / NFFT)
    turn = np.stack([np.cos(angle), np.sin(angle)], axis=1).astype(np.float32)
    return local, turn.reshape(NSL, JS, 2, TW)


def gather_strain(shard):
    core = lax.axis_index("tmpl") % 2
    x = jnp.transpose(shard[0], (2, 1, 0, 3)).reshape(JS, 2 * NDET, 1, FB)
    for move in (x_near, x_far, y_near):
        x = jnp.concatenate([x, swap_with(x, move)], axis=2)
    x = x[None]
    for moves, turned in (((y_far, z_near), 0), ((z_near, z_far), None), ((z_far, y_far), 1)):
        y = swap_with(x, by_core(*moves))
        if turned is not None:
            other = jnp.concatenate([y[:, :, :, 4:], y[:, :, :, :4]], axis=3)
            y = jnp.where(core == turned, other, y)
        x = jnp.concatenate([x, y], axis=0)
    x = x.reshape(NSL // 2, JS, 2 * ROWS, FB)
    return jnp.concatenate([x, swap_with(x, other_core)], axis=0)


def arrival_order():
    dt = lax.axis_index("dt")
    tm = lax.axis_index("tmpl")
    x, y_lo = dt // 2, dt % 2
    y_hi, z, core = tm // 8, (tm // 2) % 4, tm % 2
    p = jnp.arange(SEGS, dtype=jnp.int32)
    q = jnp.arange(NSL, dtype=jnp.int32)

    def ring(a, first, second):
        a = jnp.where(second == 1, 3 - a, a)
        return a ^ first

    segs = ring(x, p % 2, p // 2 % 2) * 2 + (y_lo ^ (p // 4))
    bits = (q % 2, q // 2 % 2, q // 4 % 2)
    from_core = core ^ (q // 8)
    even = (y_hi ^ bits[0]) * 8 + ring(z, bits[1], bits[2]) * 2
    odd = (y_hi ^ bits[2]) * 8 + ring(z, bits[0], bits[1]) * 2 + 1
    return segs, jnp.where(from_core == 0, even, odd)


def phase(turns):
    angle = turns.astype(jnp.float32) * jnp.float32(TWO_PI / NFFT)
    return jnp.stack([jnp.cos(angle), jnp.sin(angle)])


def kernel(
    sl_ref, segs_ref, live_ref, bin_ref, frac_ref, inv_ref, half_ref,
    strain_ref, table_ref, turn_ref, templ_ref, start_ref, local_ref, step_ref,
    out_ref, prod_ref, rot_ref, best_ref, *binned,
):
    g = pl.program_id(0)

    @pl.when(g == 0)
    def _():
        for ref in binned:
            ref[...] = jnp.zeros_like(ref)

    sc, ss = start_ref[0, 0], start_ref[0, 1]
    for half in range(2):
        cols = slice(half * 128, half * 128 + 128)
        lc, ls = local_ref[0, :, cols], local_ref[1, :, cols]
        rot_ref[0, :, cols] = sc * lc - ss * ls
        rot_ref[1, :, cols] = sc * ls + ss * lc

    def product(jj):
        both = strain_ref[0, jj].astype(jnp.float32)
        raw_r, raw_i = both[:ROWS], both[ROWS:]
        rc, rs = rot_ref[0], rot_ref[1]
        sr = raw_r * rc - raw_i * rs
        si = raw_r * rs + raw_i * rc
        su = sr + si
        pc = jnp.concatenate([step_ref[0], step_ref[0]], axis=1)
        ps = jnp.concatenate([step_ref[1], step_ref[1]], axis=1)
        rot_ref[0] = rc * pc - rs * ps
        rot_ref[1] = rc * ps + rs * pc
        for pair in range(SLOTS // 2):
            real, imag = [], []
            for k in (2 * pair, 2 * pair + 1):
                h = templ_ref[0, jj, k:k + 1, :]
                v = templ_ref[0, jj, SLOTS + k:SLOTS + k + 1, :]
                w = templ_ref[0, jj, 2 * SLOTS + k:2 * SLOTS + k + 1, :]
                k1 = h * su
                real.append(k1 - si * w)
                imag.append(k1 - sr * v)
            rows = slice(jj * SLOTS * ROWS + 2 * ROWS * pair, jj * SLOTS * ROWS + 2 * ROWS * (pair + 1))
            prod_ref[rows, :FB] = jnp.concatenate(real, axis=0).astype(jnp.bfloat16)
            prod_ref[rows, FB:] = jnp.concatenate(imag, axis=0).astype(jnp.bfloat16)

    def post(jj, series):
        j = sl_ref[g] * JS + jj
        c = turn_ref[0, jj, 0:1, :]
        s = turn_ref[0, jj, 1:2, :]
        for k in range(SLOTS):
            b = bin_ref[k, j]
            re = series[k * ROWS:(k + 1) * ROWS, :TW]
            im = series[k * ROWS:(k + 1) * ROWS, TW:]
            binned[k][b, :, :TW] += c * re - s * im
            binned[k][b, :, TW:] += c * im + s * re

    half = JS // 2 * SLOTS * ROWS
    for jj in range(JS):
        product(jj)
    for h in range(2):
        series = jnp.dot(prod_ref[h * half:(h + 1) * half], table_ref[...], preferred_element_type=jnp.float32)
        for m in range(JS // 2):
            post(h * (JS // 2) + m, series[m * SLOTS * ROWS:(m + 1) * SLOTS * ROWS])

    @pl.when(g == NSL - 1)
    def _():
        best = jnp.zeros((SEGS, TW), jnp.float32)
        for k in range(SLOTS):
            total = binned[k][0]
            for b in range(1, NBIN):
                total = total + binned[k][b]
            chi = jnp.zeros((ROWS, TW), jnp.float32)
            for b in range(NBIN):
                gap = binned[k][b] - frac_ref[k, b] * total
                gap = gap * gap
                chi = chi + (gap[:, :TW] + gap[:, TW:]) * inv_ref[k, b]
            power = total * total
            snr2 = (power[:, :TW] + power[:, TW:]) * half_ref[k]
            reduced = chi / (2.0 * NBIN - 2.0)
            cube = (1.0 + reduced * reduced * reduced) * 0.5
            factor = jnp.where(reduced > 1.0, jnp.exp(jnp.log(cube) * (-1.0 / 3.0)), 1.0)
            new2 = snr2 * factor
            net2 = new2[:SEGS] + new2[SEGS:2 * SEGS] + new2[2 * SEGS:]
            best = jnp.where(k < live_ref[0], jnp.maximum(best, net2), best)
        best = jnp.sqrt(best)
        best_ref[...] = jnp.concatenate(
            [jnp.max(best[:, w * WIN:(w + 1) * WIN], axis=1, keepdims=True) for w in range(NWIN)], axis=1
        )
        for p in range(SEGS):
            out_ref[pl.ds(segs_ref[p], 1), :] = best_ref[p:p + 1, :]


def search(sl, segs, live, bin_of, frac, inv, half, strain, templ, start, local, step):
    grid_spec = pltpu.PrefetchScalarGridSpec(
        num_scalar_prefetch=7,
        grid=(NSL,),
        in_specs=[
            pl.BlockSpec((1, JS, 2 * ROWS, FB), lambda g, sl, *_: (g, 0, 0, 0)),
            pl.BlockSpec((2 * FB, 2 * TW), lambda g, sl, *_: (0, 0)),
            pl.BlockSpec((1, JS, 2, TW), lambda g, sl, *_: (sl[g], 0, 0, 0)),
            pl.BlockSpec((1, JS, 3 * SLOTS, FB), lambda g, sl, *_: (sl[g], 0, 0, 0)),
            pl.BlockSpec((1, 2, ROWS, TW), lambda g, sl, *_: (g, 0, 0, 0)),
            pl.BlockSpec((2, ROWS, FB), lambda g, sl, *_: (0, 0, 0)),
            pl.BlockSpec((2, ROWS, TW), lambda g, sl, *_: (0, 0, 0)),
        ],
        out_specs=pl.BlockSpec((SEGS, NWIN), lambda g, sl, *_: (0, 0)),
        scratch_shapes=[
            pltpu.VMEM((JS * SLOTS * ROWS, 2 * FB), jnp.bfloat16),
            pltpu.VMEM((2, ROWS, FB), jnp.float32),
            pltpu.VMEM((SEGS, NWIN), jnp.float32),
        ] + [pltpu.VMEM((NBIN, ROWS, 2 * TW), jnp.float32) for _ in range(SLOTS)],
    )
    return pl.pallas_call(
        kernel,
        out_shape=jax.ShapeDtypeStruct((SEGS, NWIN), jnp.float32),
        grid_spec=grid_spec,
        compiler_params=pltpu.CompilerParams(
            dimension_semantics=("arbitrary",), vmem_limit_bytes=40 * 1024 * 1024
        ),
        name="search",
    )(sl, segs, live, bin_of, frac, inv, half, strain, *tables(), templ, start, local, step)


def per_device(strain, templates, live_count, chi_edges, shifts):
    segs, slices = arrival_order()
    gathered = gather_strain(strain)

    blocks = jnp.arange(NBLK, dtype=jnp.int32)
    bin_of = jnp.sum((chi_edges[:, :, None] <= blocks[None, None, :]).astype(jnp.int32), axis=1)
    labels = jnp.arange(NBIN, dtype=jnp.int32)
    onehot = (bin_of[:, None, :] == labels[None, :, None]).astype(jnp.float32)
    wide = templates.astype(jnp.float32)
    block_power = jnp.sum(wide * wide, axis=(1, 3))
    sigma2 = jnp.sum(block_power, axis=1) + EPSILON
    in_bins = jnp.sum(onehot * block_power[:, None, :], axis=2)
    frac = (in_bins + EPSILON) / sigma2[:, None]
    inv = 1.0 / (frac * sigma2[:, None])
    half = 1.0 / (2.0 * sigma2)

    real, imag = wide[:, 0], wide[:, 1]
    templ = jnp.concatenate([real, real + imag, real - imag], axis=0)
    templ = jnp.transpose(templ, (1, 0, 2)).reshape(NSL, JS, 3 * SLOTS, FB)

    first = (MARGIN + jnp.take(shifts, segs, axis=0)).T.reshape(ROWS)
    bins = jnp.arange(FB, dtype=jnp.int32)
    local = phase((first[:, None] * bins[None, :] * STRIDE) % NFFT)
    starts = (FLOW // FB + slices * JS) * FB
    start = phase((first[None, :] * starts[:, None]) % NFFT)
    start = jnp.broadcast_to(jnp.transpose(start, (1, 0, 2))[..., None], (NSL, 2, ROWS, TW))
    step = phase(first * FB)
    step = jnp.broadcast_to(step[..., None], (2, ROWS, TW))

    best = search(
        slices, segs, live_count[0], bin_of, frac, inv, half, gathered, templ, start, local, step
    )
    for move in (other_core, z_near, z_far, y_across):
        best = jnp.maximum(best, swap_with(best, move))
    return best[:, None, :]


def solution(mesh):
    in_specs = (
        P("dt", None, None, "tmpl", None),
        P(("dt", "tmpl"), None, None, None),
        P("dt", "tmpl"),
        P(("dt", "tmpl"), None),
        P(),
    )
    out_specs = P(None, "dt", None)
    return jax.shard_map(
        per_device, mesh=mesh, in_specs=in_specs, out_specs=out_specs, check_vma=False
    )
```

```python
import math

import ml_dtypes
import numpy as np

import jax
import jax.numpy as jnp
from jax import lax
from jax.experimental import pallas as pl
from jax.experimental.pallas import tpu as pltpu
from jax.sharding import PartitionSpec as P

FB = 256
NBLK = 96
NFFT = 1048576
FLOW = 5120
STRIDE = 4097
NBIN = 16
TW = 128
MARGIN = 64
WIN = 16
NWIN = TW // WIN
NDET = 3
SEGS = 8
SLOTS = 12
NSL = 16
JS = NBLK // NSL
ROWS = NDET * SEGS
EPSILON = 1e-05
TWO_PI = 2.0 * math.pi
AXES = ("dt", "tmpl")


def place_of(index):
    dt, tm = divmod(index, 16)
    return (dt // 2, (tm // 8) * 2 + dt % 2, (tm // 2) % 4, tm % 2)


def index_of(x, y, z, core):
    return (x * 2 + y % 2) * 16 + (y // 2) * 8 + z * 2 + core


def across(dx=0, dy=0, dz=0, dcore=0):
    return lambda x, y, z, core: (x ^ dx, y ^ dy, z ^ dz, core ^ dcore)


def swap_with(value, move):
    pairs = [(index, index_of(*move(*place_of(index)))) for index in range(128)]
    return lax.ppermute(value, AXES, pairs)


def tables():
    tau = np.arange(TW, dtype=np.int64)
    bins = np.arange(FB, dtype=np.int64)
    angle = ((bins[:, None] * tau[None, :] * STRIDE) % NFFT).astype(np.float64) * (TWO_PI / NFFT)
    cosine, sine = np.cos(angle), np.sin(angle)
    local = np.block([[cosine, sine], [-sine, cosine]]).astype(ml_dtypes.bfloat16)
    base = FLOW + np.arange(NBLK, dtype=np.int64) * FB
    angle = ((base[:, None] * tau[None, :] * STRIDE) % NFFT).astype(np.float64) * (TWO_PI / NFFT)
    turn = np.stack([np.cos(angle), np.sin(angle)], axis=1).astype(np.float32)
    return local, turn.reshape(NSL, JS, 2, TW)


def gather_strain(shard):
    x = jnp.transpose(shard[0], (2, 1, 0, 3)).reshape(JS, 2 * NDET, 1, FB)
    got = {0: x}
    for dx in (2, 3, 1):
        got[dx] = swap_with(x, across(dx=dx))
    x = jnp.concatenate([got[dx] for dx in range(4)], axis=2)
    x = jnp.concatenate([x, swap_with(x, across(dy=1))], axis=2)
    x = x.reshape(1, JS, 2 * ROWS, FB)
    got = {(0, 0): x}
    for dy, dz in ((0, 2), (2, 0), (2, 2), (0, 3), (2, 3), (2, 1), (0, 1)):
        got[dy, dz] = swap_with(x, across(dy=dy, dz=dz))
    x = jnp.concatenate([got[dy, dz] for dy in (0, 2) for dz in range(4)], axis=0)
    return jnp.concatenate([x, swap_with(x, across(dcore=1))], axis=0)


def arrival_order():
    dt = lax.axis_index("dt")
    tm = lax.axis_index("tmpl")
    p = jnp.arange(SEGS, dtype=jnp.int32)
    q = jnp.arange(NSL, dtype=jnp.int32)
    segs = ((dt // 2) ^ (p % 4)) * 2 + ((dt % 2) ^ (p // 4))
    slices = ((tm // 8) ^ (q // 4 % 2)) * 8 + ((tm // 2 % 4) ^ (q % 4)) * 2 + ((tm % 2) ^ (q // 8))
    return segs, slices


def phase(turns):
    angle = turns.astype(jnp.float32) * jnp.float32(TWO_PI / NFFT)
    return jnp.stack([jnp.cos(angle), jnp.sin(angle)])


def kernel(
    sl_ref, segs_ref, live_ref, bin_ref, frac_ref, inv_ref, half_ref,
    strain_ref, table_ref, turn_ref, templ_ref, start_ref, local_ref, step_ref,
    out_ref, prod_ref, rot_ref, best_ref, wide_ref, *binned,
):
    g = pl.program_id(0)

    @pl.when(g == 0)
    def _():
        for ref in binned:
            ref[...] = jnp.zeros_like(ref)
        for k in range(SLOTS):
            h = templ_ref[k, 0].astype(jnp.float32)
            i = templ_ref[k, 1].astype(jnp.float32)
            wide_ref[k, 0] = h
            wide_ref[k, 1] = h + i
            wide_ref[k, 2] = h - i

    sc, ss = start_ref[0, 0], start_ref[0, 1]
    for half in range(2):
        cols = slice(half * 128, half * 128 + 128)
        lc, ls = local_ref[0, :, cols], local_ref[1, :, cols]
        rot_ref[0, :, cols] = sc * lc - ss * ls
        rot_ref[1, :, cols] = sc * ls + ss * lc

    def product(jj):
        j = sl_ref[g] * JS + jj
        both = strain_ref[0, jj].astype(jnp.float32)
        raw_r, raw_i = both[:ROWS], both[ROWS:]
        rc, rs = rot_ref[0], rot_ref[1]
        sr = raw_r * rc - raw_i * rs
        si = raw_r * rs + raw_i * rc
        su = sr + si
        pc = jnp.concatenate([step_ref[0], step_ref[0]], axis=1)
        ps = jnp.concatenate([step_ref[1], step_ref[1]], axis=1)
        rot_ref[0] = rc * pc - rs * ps
        rot_ref[1] = rc * ps + rs * pc
        for pair in range(SLOTS // 2):
            real, imag = [], []
            for k in (2 * pair, 2 * pair + 1):
                h = wide_ref[k, 0, pl.ds(j, 1), :]
                v = wide_ref[k, 1, pl.ds(j, 1), :]
                w = wide_ref[k, 2, pl.ds(j, 1), :]
                k1 = h * su
                real.append(k1 - si * w)
                imag.append(k1 - sr * v)
            rows = slice(jj * SLOTS * ROWS + 2 * ROWS * pair, jj * SLOTS * ROWS + 2 * ROWS * (pair + 1))
            prod_ref[rows, :FB] = jnp.concatenate(real, axis=0).astype(jnp.bfloat16)
            prod_ref[rows, FB:] = jnp.concatenate(imag, axis=0).astype(jnp.bfloat16)

    def post(jj, series):
        j = sl_ref[g] * JS + jj
        c = turn_ref[0, jj, 0:1, :]
        s = turn_ref[0, jj, 1:2, :]
        for k in range(SLOTS):
            b = bin_ref[k, j]
            re = series[k * ROWS:(k + 1) * ROWS, :TW]
            im = series[k * ROWS:(k + 1) * ROWS, TW:]
            binned[k][b, :, :TW] += c * re - s * im
            binned[k][b, :, TW:] += c * im + s * re

    half = JS // 2 * SLOTS * ROWS
    for jj in range(JS):
        product(jj)
    for h in range(2):
        series = jnp.dot(prod_ref[h * half:(h + 1) * half], table_ref[...], preferred_element_type=jnp.float32)
        for m in range(JS // 2):
            post(h * (JS // 2) + m, series[m * SLOTS * ROWS:(m + 1) * SLOTS * ROWS])

    @pl.when(g == NSL - 1)
    def _():
        best = jnp.zeros((SEGS, TW), jnp.float32)
        for k in range(SLOTS):
            total = binned[k][0]
            for b in range(1, NBIN):
                total = total + binned[k][b]
            chi = jnp.zeros((ROWS, TW), jnp.float32)
            for b in range(NBIN):
                gap = binned[k][b] - frac_ref[k, b] * total
                gap = gap * gap
                chi = chi + (gap[:, :TW] + gap[:, TW:]) * inv_ref[k, b]
            power = total * total
            snr2 = (power[:, :TW] + power[:, TW:]) * half_ref[k]
            reduced = chi / (2.0 * NBIN - 2.0)
            cube = (1.0 + reduced * reduced * reduced) * 0.5
            factor = jnp.where(reduced > 1.0, jnp.exp(jnp.log(cube) * (-1.0 / 3.0)), 1.0)
            new2 = snr2 * factor
            net2 = new2[:SEGS] + new2[SEGS:2 * SEGS] + new2[2 * SEGS:]
            best = jnp.where(k < live_ref[0], jnp.maximum(best, net2), best)
        best = jnp.sqrt(best)
        best_ref[...] = jnp.concatenate(
            [jnp.max(best[:, w * WIN:(w + 1) * WIN], axis=1, keepdims=True) for w in range(NWIN)], axis=1
        )
        for p in range(SEGS):
            out_ref[pl.ds(segs_ref[p], 1), :] = best_ref[p:p + 1, :]


def search(sl, segs, live, bin_of, frac, inv, half, strain, templ, start, local, step):
    grid_spec = pltpu.PrefetchScalarGridSpec(
        num_scalar_prefetch=7,
        grid=(NSL,),
        in_specs=[
            pl.BlockSpec((1, JS, 2 * ROWS, FB), lambda g, sl, *_: (g, 0, 0, 0)),
            pl.BlockSpec((2 * FB, 2 * TW), lambda g, sl, *_: (0, 0)),
            pl.BlockSpec((1, JS, 2, TW), lambda g, sl, *_: (sl[g], 0, 0, 0)),
            pl.BlockSpec((SLOTS, 2, NBLK, FB), lambda g, sl, *_: (0, 0, 0, 0)),
            pl.BlockSpec((1, 2, ROWS, TW), lambda g, sl, *_: (g, 0, 0, 0)),
            pl.BlockSpec((2, ROWS, FB), lambda g, sl, *_: (0, 0, 0)),
            pl.BlockSpec((2, ROWS, TW), lambda g, sl, *_: (0, 0, 0)),
        ],
        out_specs=pl.BlockSpec((SEGS, NWIN), lambda g, sl, *_: (0, 0)),
        scratch_shapes=[
            pltpu.VMEM((JS * SLOTS * ROWS, 2 * FB), jnp.bfloat16),
            pltpu.VMEM((2, ROWS, FB), jnp.float32),
            pltpu.VMEM((SEGS, NWIN), jnp.float32),
            pltpu.VMEM((SLOTS, 3, NBLK, FB), jnp.float32),
        ] + [pltpu.VMEM((NBIN, ROWS, 2 * TW), jnp.float32) for _ in range(SLOTS)],
    )
    return pl.pallas_call(
        kernel,
        out_shape=jax.ShapeDtypeStruct((SEGS, NWIN), jnp.float32),
        grid_spec=grid_spec,
        compiler_params=pltpu.CompilerParams(
            dimension_semantics=("arbitrary",), vmem_limit_bytes=24 * 1024 * 1024
        ),
        name="search",
    )(sl, segs, live, bin_of, frac, inv, half, strain, *tables(), templ, start, local, step)


def per_device(strain, templates, live_count, chi_edges, shifts):
    segs, slices = arrival_order()
    gathered = gather_strain(strain)

    blocks = jnp.arange(NBLK, dtype=jnp.int32)
    bin_of = jnp.sum((chi_edges[:, :, None] <= blocks[None, None, :]).astype(jnp.int32), axis=1)
    labels = jnp.arange(NBIN, dtype=jnp.int32)
    onehot = (bin_of[:, None, :] == labels[None, :, None]).astype(jnp.float32)
    wide = templates.astype(jnp.float32)
    block_power = jnp.sum(wide * wide, axis=(1, 3))
    sigma2 = jnp.sum(block_power, axis=1) + EPSILON
    in_bins = jnp.sum(onehot * block_power[:, None, :], axis=2)
    frac = (in_bins + EPSILON) / sigma2[:, None]
    inv = 1.0 / (frac * sigma2[:, None])
    half = 1.0 / (2.0 * sigma2)

    first = (MARGIN + jnp.take(shifts, segs, axis=0)).T.reshape(ROWS)
    bins = jnp.arange(FB, dtype=jnp.int32)
    local = phase((first[:, None] * bins[None, :] * STRIDE) % NFFT)
    starts = (FLOW // FB + slices * JS) * FB
    start = phase((first[None, :] * starts[:, None]) % NFFT)
    start = jnp.broadcast_to(jnp.transpose(start, (1, 0, 2))[..., None], (NSL, 2, ROWS, TW))
    step = phase(first * FB)
    step = jnp.broadcast_to(step[..., None], (2, ROWS, TW))

    best = search(
        slices, segs, live_count[0], bin_of, frac, inv, half, gathered, templates, start, local, step
    )
    for move in (across(dcore=1), across(dz=1), across(dz=3), across(dy=2)):
        best = jnp.maximum(best, swap_with(best, move))
    return best[:, None, :]


def solution(mesh):
    in_specs = (
        P("dt", None, None, "tmpl", None),
        P(("dt", "tmpl"), None, None, None),
        P("dt", "tmpl"),
        P(("dt", "tmpl"), None),
        P(),
    )
    out_specs = P(None, "dt", None)
    return jax.shard_map(
        per_device, mesh=mesh, in_specs=in_specs, out_specs=out_specs, check_vma=False
    )
```

```python
import functools
import math

import ml_dtypes
import numpy as np

import jax
import jax.numpy as jnp
from jax import lax
from jax.experimental import pallas as pl
from jax.experimental.pallas import tpu as pltpu
from jax.sharding import PartitionSpec as P

FB = 256
NBLK = 96
NFFT = 1048576
FLOW = 5120
STRIDE = 4097
NBIN = 16
TW = 128
MARGIN = 64
WIN = 16
NWIN = TW // WIN
NDET = 3
SEGS = 8
SLOTS = 12
NSL = 16
JS = NBLK // NSL
ROWS = NDET * SEGS
EPSILON = 1e-05
TWO_PI = 2.0 * math.pi
AXES = ("dt", "tmpl")
VMEM = 16 * 1024 * 1024


def place_of(index):
    dt, tm = divmod(index, 16)
    return (dt // 2, (tm // 8) * 2 + dt % 2, (tm // 2) % 4, tm % 2)


def index_of(x, y, z, core):
    return (x * 2 + y % 2) * 16 + (y // 2) * 8 + z * 2 + core


def across(dx=0, dy=0, dz=0, dcore=0):
    return lambda x, y, z, core: (x ^ dx, y ^ dy, z ^ dz, core ^ dcore)


def swap_with(value, move):
    pairs = [(index, index_of(*move(*place_of(index)))) for index in range(128)]
    return lax.ppermute(value, AXES, pairs)


def tables():
    tau = np.arange(TW, dtype=np.int64)
    bins = np.arange(FB, dtype=np.int64)
    angle = ((bins[:, None] * tau[None, :] * STRIDE) % NFFT).astype(np.float64) * (TWO_PI / NFFT)
    cosine, sine = np.cos(angle), np.sin(angle)
    local = np.block([[cosine, sine], [-sine, cosine]]).astype(ml_dtypes.bfloat16)
    base = FLOW + np.arange(NBLK, dtype=np.int64) * FB
    angle = ((base[:, None] * tau[None, :] * STRIDE) % NFFT).astype(np.float64) * (TWO_PI / NFFT)
    turn = np.stack([np.cos(angle), np.sin(angle)], axis=1).astype(np.float32)
    return local, turn.reshape(NSL, JS, 2, TW)


def phase(turns):
    angle = turns.astype(jnp.float32) * jnp.float32(TWO_PI / NFFT)
    return jnp.stack([jnp.cos(angle), jnp.sin(angle)])


STEPS = (
    ({"dy": 2}, {"dz": 1}),
    ({"dz": 1}, {"dz": 3}),
    ({"dz": 3}, {"dy": 2}),
)


def step_move(step):
    first, second = across(**STEPS[step][0]), across(**STEPS[step][1])
    return lambda x, y, z, core: (second if core else first)(x, y, z, core)


def slice_of(piece, other):
    tm = lax.axis_index("tmpl")
    y_hi, z, core = tm // 8, (tm // 2) % 4, (tm % 2) ^ other
    change = []
    for which in range(2):
        dy = dz = 0
        for step in range(3):
            if piece >> step & 1:
                dy ^= STEPS[step][which].get("dy", 0) // 2
                dz ^= STEPS[step][which].get("dz", 0)
        change.append((dy, dz))
    dy = jnp.where(core == 0, change[0][0], change[1][0])
    dz = jnp.where(core == 0, change[0][1], change[1][1])
    return (y_hi ^ dy) * 8 + (z ^ dz) * 2 + core


def segment_at(place):
    dt = lax.axis_index("dt")
    return ((dt // 2) ^ (place % 4)) * 2 + ((dt % 2) ^ (place // 4))


def widen_kernel(templ_ref, wide_ref, *binned):
    for ref in binned:
        ref[...] = jnp.zeros_like(ref)
    for k in range(SLOTS):
        h = templ_ref[k, 0].astype(jnp.float32)
        i = templ_ref[k, 1].astype(jnp.float32)
        wide_ref[k, 0] = h
        wide_ref[k, 1] = h + i
        wide_ref[k, 2] = h - i


def whole():
    return pl.BlockSpec(memory_space=pltpu.VMEM)


BINNED = [jax.ShapeDtypeStruct((NBIN, ROWS, 2 * TW), jnp.float32)] * SLOTS


def widen(templates):
    outs = pl.pallas_call(
        widen_kernel,
        out_shape=[jax.ShapeDtypeStruct((SLOTS, 3, NBLK, FB), jnp.float32)] + BINNED,
        in_specs=[whole()],
        out_specs=[whole()] * (1 + SLOTS),
        compiler_params=pltpu.CompilerParams(vmem_limit_bytes=VMEM),
        cost_estimate=pl.CostEstimate(flops=10**6, bytes_accessed=10**6, transcendentals=0),
        name="widen",
    )(templates)
    return outs[0], outs[1:]


def bins_kernel(parts, last, *refs):
    count = len(parts)
    pieces, refs = refs[:count], refs[count:]
    bin_vmem, table_ref, turn_ref, wide_ref, start_ref, local_ref, step_ref = refs[:7]
    refs = refs[7:]
    if last:
        stat_vmem, refs = refs[0], refs[1:]
    refs = refs[SLOTS:]
    binned, refs = refs[:SLOTS], refs[SLOTS:]
    if last:
        out_ref, refs = refs[0], refs[1:]
    prod_ref, rot_ref, bin_ref, sems = refs[:4]
    copies = [pltpu.make_async_copy(bin_vmem, bin_ref, sems.at[0])]
    if last:
        stat_ref, best_ref = refs[4:]
        copies.append(pltpu.make_async_copy(stat_vmem, stat_ref, sems.at[1]))
    for copy in copies:
        copy.start()

    def product(piece_ref, c, jj):
        j = c * JS + jj
        both = piece_ref[0, jj].astype(jnp.float32)
        raw_r, raw_i = both[:ROWS], both[ROWS:]
        rc, rs = rot_ref[0], rot_ref[1]
        sr = raw_r * rc - raw_i * rs
        si = raw_r * rs + raw_i * rc
        su = sr + si
        if jj < JS - 1:
            pc = jnp.concatenate([step_ref[0], step_ref[0]], axis=1)
            ps = jnp.concatenate([step_ref[1], step_ref[1]], axis=1)
            rot_ref[0] = rc * pc - rs * ps
            rot_ref[1] = rc * ps + rs * pc
        for pair in range(SLOTS // 2):
            real, imag = [], []
            for k in (2 * pair, 2 * pair + 1):
                h = wide_ref[k, 0, pl.ds(j, 1), :]
                v = wide_ref[k, 1, pl.ds(j, 1), :]
                w = wide_ref[k, 2, pl.ds(j, 1), :]
                k1 = h * su
                real.append(k1 - si * w)
                imag.append(k1 - sr * v)
            base = jj * SLOTS * ROWS + 2 * ROWS * pair
            rows = slice(base, base + 2 * ROWS)
            prod_ref[rows, :FB] = jnp.concatenate(real, axis=0).astype(jnp.bfloat16)
            prod_ref[rows, FB:] = jnp.concatenate(imag, axis=0).astype(jnp.bfloat16)

    def post(c, jj, series):
        j = c * JS + jj
        cos = turn_ref[c, jj, 0:1, :]
        sin = turn_ref[c, jj, 1:2, :]
        for k in range(SLOTS):
            b = bin_ref[k, j]
            re = series[k * ROWS:(k + 1) * ROWS, :TW]
            im = series[k * ROWS:(k + 1) * ROWS, TW:]
            binned[k][b, :, :TW] += cos * re - sin * im
            binned[k][b, :, TW:] += cos * im + sin * re

    for number, (piece_ref, part) in enumerate(zip(pieces, parts)):
        c = slice_of(*part)
        sc, ss = start_ref[c, 0], start_ref[c, 1]
        for half in range(2):
            cols = slice(half * TW, half * TW + TW)
            lc, ls = local_ref[0, :, cols], local_ref[1, :, cols]
            rot_ref[0, :, cols] = sc * lc - ss * ls
            rot_ref[1, :, cols] = sc * ls + ss * lc
        for jj in range(JS):
            product(piece_ref, c, jj)
        if number == 0:
            for copy in copies:
                copy.wait()
        half = JS // 2
        size = half * SLOTS * ROWS
        for h in range(2):
            series = jnp.dot(
                prod_ref[h * size:(h + 1) * size], table_ref[...], preferred_element_type=jnp.float32
            )
            for m in range(half):
                post(c, h * half + m, series[m * SLOTS * ROWS:(m + 1) * SLOTS * ROWS])

    if last:
        best = jnp.zeros((SEGS, TW), jnp.float32)
        for k in range(SLOTS):
            total = binned[k][0]
            for b in range(1, NBIN):
                total = total + binned[k][b]
            chi = jnp.zeros((ROWS, TW), jnp.float32)
            for b in range(NBIN):
                gap = binned[k][b] - stat_ref[k, b] * total
                gap = gap * gap
                chi = chi + (gap[:, :TW] + gap[:, TW:]) * stat_ref[k, NBIN + b]
            power = total * total
            snr2 = (power[:, :TW] + power[:, TW:]) * stat_ref[k, 2 * NBIN]
            reduced = chi / (2.0 * NBIN - 2.0)
            cube = (1.0 + reduced * reduced * reduced) * 0.5
            factor = jnp.where(reduced > 1.0, jnp.exp(jnp.log(cube) * (-1.0 / 3.0)), 1.0)
            new2 = snr2 * factor
            net2 = new2[:SEGS] + new2[SEGS:2 * SEGS] + new2[2 * SEGS:]
            best = jnp.where(stat_ref[k, 2 * NBIN + 1] > 0.5, jnp.maximum(best, net2), best)
        best = jnp.sqrt(best)
        best_ref[...] = jnp.concatenate(
            [jnp.max(best[:, w * WIN:(w + 1) * WIN], axis=1, keepdims=True) for w in range(NWIN)], axis=1
        )
        for place in range(SEGS):
            out_ref[pl.ds(segment_at(place), 1), :] = best_ref[place:place + 1, :]


def add_bins(pieces, parts, shared, binned, stat=None):
    last = stat is not None
    operands = [*pieces, *shared] + ([stat] if last else []) + list(binned)
    first = len(operands) - SLOTS
    out_shape = list(BINNED)
    scratch = [
        pltpu.VMEM((JS * SLOTS * ROWS, 2 * FB), jnp.bfloat16),
        pltpu.VMEM((2, ROWS, FB), jnp.float32),
        pltpu.SMEM((SLOTS, NBLK), jnp.int32),
        pltpu.SemaphoreType.DMA((2,)),
    ]
    if last:
        out_shape.append(jax.ShapeDtypeStruct((SEGS, NWIN), jnp.float32))
        scratch += [pltpu.SMEM((SLOTS, 2 * NBIN + 2), jnp.float32), pltpu.VMEM((SEGS, NWIN), jnp.float32)]
    flops = len(parts) * 2 * JS * SLOTS * ROWS * 2 * FB * 2 * TW
    return pl.pallas_call(
        functools.partial(bins_kernel, parts, last),
        out_shape=out_shape,
        in_specs=[whole()] * len(operands),
        out_specs=[whole()] * len(out_shape),
        scratch_shapes=scratch,
        input_output_aliases={first + k: k for k in range(SLOTS)},
        compiler_params=pltpu.CompilerParams(vmem_limit_bytes=VMEM),
        cost_estimate=pl.CostEstimate(flops=2 * flops, bytes_accessed=10**6, transcendentals=0),
        name="last_bins" if last else "add_bins",
    )(*operands)


def per_device(strain, templates, live_count, chi_edges, shifts):
    wide, binned = widen(templates)

    x = jnp.transpose(strain[0], (2, 1, 0, 3)).reshape(JS, 2 * NDET, 1, FB)
    got = {0: x}
    for dx in (2, 3, 1):
        got[dx] = swap_with(x, across(dx=dx))
    x = jnp.concatenate([got[dx] for dx in range(4)], axis=2)
    x = jnp.concatenate([x, swap_with(x, across(dy=1))], axis=2)
    own = [x.reshape(1, JS, 2 * ROWS, FB)]

    blocks = jnp.arange(NBLK, dtype=jnp.int32)
    bin_of = jnp.sum((chi_edges[:, :, None] <= blocks[None, None, :]).astype(jnp.int32), axis=1)
    labels = jnp.arange(NBIN, dtype=jnp.int32)
    onehot = (bin_of[:, None, :] == labels[None, :, None]).astype(jnp.float32)
    full = templates.astype(jnp.float32)
    block_power = jnp.sum(full * full, axis=(1, 3))
    sigma2 = jnp.sum(block_power, axis=1) + EPSILON
    in_bins = jnp.sum(onehot * block_power[:, None, :], axis=2)
    frac = (in_bins + EPSILON) / sigma2[:, None]
    inv = 1.0 / (frac * sigma2[:, None])
    half = 1.0 / (2.0 * sigma2)
    live = (jnp.arange(SLOTS, dtype=jnp.int32) < live_count[0, 0]).astype(jnp.float32)
    stat = jnp.concatenate([frac, inv, half[:, None], live[:, None]], axis=1)

    order = segment_at(jnp.arange(SEGS, dtype=jnp.int32))
    first = (MARGIN + jnp.take(shifts, order, axis=0)).T.reshape(ROWS)
    bins = jnp.arange(FB, dtype=jnp.int32)
    local = phase((first[:, None] * bins[None, :] * STRIDE) % NFFT)
    starts = (FLOW // FB + jnp.arange(NSL, dtype=jnp.int32) * JS) * FB
    start = phase((first[None, :] * starts[:, None]) % NFFT)
    start = jnp.broadcast_to(jnp.transpose(start, (1, 0, 2))[..., None], (NSL, 2, ROWS, TW))
    step = phase(first * FB)
    step = jnp.broadcast_to(step[..., None], (2, ROWS, TW))
    table, turn = tables()
    shared = (bin_of, table, turn, wide, start, local, step)

    others = [swap_with(own[0], across(dcore=1))]
    for number in range(3):
        fresh = [swap_with(piece, step_move(number)) for piece in own]
        own += fresh
        others += [swap_with(piece, across(dcore=1)) for piece in fresh]
    for p in range(7):
        binned = add_bins((own[p], others[p]), ((p, 0), (p, 1)), shared, binned)
    binned = add_bins((own[7],), ((7, 0),), shared, binned)
    best = add_bins((others[7],), ((7, 1),), shared, binned, stat)[-1]
    for move in (across(dcore=1), across(dz=1), across(dz=3), across(dy=2)):
        best = jnp.maximum(best, swap_with(best, move))
    return best[:, None, :]


def solution(mesh):
    in_specs = (
        P("dt", None, None, "tmpl", None),
        P(("dt", "tmpl"), None, None, None),
        P("dt", "tmpl"),
        P(("dt", "tmpl"), None),
        P(),
    )
    out_specs = P(None, "dt", None)
    return jax.shard_map(
        per_device, mesh=mesh, in_specs=in_specs, out_specs=out_specs, check_vma=False
    )
```

```python
import functools
import math

import ml_dtypes
import numpy as np

import jax
import jax.numpy as jnp
from jax import lax
from jax.experimental import pallas as pl
from jax.experimental.pallas import tpu as pltpu
from jax.sharding import PartitionSpec as P

FB = 256
NBLK = 96
NFFT = 1048576
FLOW = 5120
STRIDE = 4097
NBIN = 16
TW = 128
MARGIN = 64
WIN = 16
LANES = 128
NWIN = TW // WIN
NDET = 3
SEGS = 8
SLOTS = 12
NSL = 16
JS = NBLK // NSL
ROWS = NDET * SEGS
EPSILON = 1e-05
TWO_PI = 2.0 * math.pi
AXES = ("dt", "tmpl")
VMEM = 16 * 1024 * 1024


def place_of(index):
    dt, tm = divmod(index, 16)
    return (dt // 2, (tm // 8) * 2 + dt % 2, (tm // 2) % 4, tm % 2)


def index_of(x, y, z, core):
    return (x * 2 + y % 2) * 16 + (y // 2) * 8 + z * 2 + core


def across(dx=0, dy=0, dz=0, dcore=0):
    return lambda x, y, z, core: (x ^ dx, y ^ dy, z ^ dz, core ^ dcore)


def swap_with(value, move):
    pairs = [(index, index_of(*move(*place_of(index)))) for index in range(128)]
    return lax.ppermute(value, AXES, pairs)


def tables():
    tau = np.arange(TW, dtype=np.int64)
    bins = np.arange(FB, dtype=np.int64)
    angle = ((bins[:, None] * tau[None, :] * STRIDE) % NFFT).astype(np.float64) * (TWO_PI / NFFT)
    cosine, sine = np.cos(angle), np.sin(angle)
    local = np.block([[cosine, sine], [-sine, cosine]]).astype(ml_dtypes.bfloat16)
    base = FLOW + np.arange(NBLK, dtype=np.int64) * FB
    angle = ((base[:, None] * tau[None, :] * STRIDE) % NFFT).astype(np.float64) * (TWO_PI / NFFT)
    turn = np.stack([np.cos(angle), np.sin(angle)], axis=1).astype(np.float32)
    return local, turn.reshape(NSL, JS, 2, TW)


STEPS = (
    ({"dy": 2}, {"dz": 1}),
    ({"dz": 1}, {"dz": 3}),
    ({"dz": 3}, {"dy": 2}),
)


def step_move(step):
    first, second = across(**STEPS[step][0]), across(**STEPS[step][1])
    return lambda x, y, z, core: (second if core else first)(x, y, z, core)


def slice_of(piece, other):
    tm = lax.axis_index("tmpl")
    y_hi, z, core = tm // 8, (tm // 2) % 4, (tm % 2) ^ other
    change = []
    for which in range(2):
        dy = dz = 0
        for step in range(3):
            if piece >> step & 1:
                dy ^= STEPS[step][which].get("dy", 0) // 2
                dz ^= STEPS[step][which].get("dz", 0)
        change.append((dy, dz))
    dy = jnp.where(core == 0, change[0][0], change[1][0])
    dz = jnp.where(core == 0, change[0][1], change[1][1])
    return (y_hi ^ dy) * 8 + (z ^ dz) * 2 + core


def segment_at(place):
    dt = lax.axis_index("dt")
    return ((dt // 2) ^ (place % 4)) * 2 + ((dt % 2) ^ (place // 4))


def widen_kernel(templ_ref, edges_ref, live_ref, wide_ref, bin_ref, stat_ref, *binned):
    for ref in binned:
        ref[...] = jnp.zeros_like(ref)
    lane = lax.broadcasted_iota(jnp.int32, (SLOTS, LANES), 1)
    bin_of = jnp.zeros((SLOTS, LANES), jnp.int32)
    for e in range(NBIN - 1):
        bin_of = bin_of + (edges_ref[:, e:e + 1] <= lane).astype(jnp.int32)
    bin_ref[...] = bin_of
    block = lax.broadcasted_iota(jnp.int32, (NBLK, LANES), 0)
    at_lane = lax.broadcasted_iota(jnp.int32, (1, LANES), 1)
    for k in range(SLOTS):
        h = templ_ref[k, 0].astype(jnp.float32)
        i = templ_ref[k, 1].astype(jnp.float32)
        wide_ref[k, 0] = h
        wide_ref[k, 1] = h + i
        wide_ref[k, 2] = h - i
        power = jnp.sum(h * h + i * i, axis=1, keepdims=True)
        upper = edges_ref[k:k + 1, :]
        lower = jnp.where(at_lane == 0, 0, pltpu.roll(upper, 1, 1))
        inside = jnp.where((block >= lower) & (block < upper), power, 0.0)
        in_bins = jnp.sum(inside, axis=0, keepdims=True)
        sigma2 = jnp.sum(power, axis=0, keepdims=True) + EPSILON
        frac = (in_bins + EPSILON) / sigma2
        inv = pltpu.roll(1.0 / (frac * sigma2), NBIN, 1)
        live = (k < live_ref[...]).astype(jnp.float32)
        row = jnp.where(at_lane == 2 * NBIN, 0.5 / sigma2, live)
        row = jnp.where(at_lane < 2 * NBIN, inv, row)
        stat_ref[k:k + 1, :] = jnp.where(at_lane < NBIN, frac, row)


def whole():
    return pl.BlockSpec(memory_space=pltpu.VMEM)


BINNED = [jax.ShapeDtypeStruct((NBIN, ROWS, 2 * TW), jnp.float32)] * SLOTS


def widen(templates, edges, live_count):
    outs = pl.pallas_call(
        widen_kernel,
        out_shape=[
            jax.ShapeDtypeStruct((SLOTS, 3, NBLK, FB), jnp.float32),
            jax.ShapeDtypeStruct((SLOTS, LANES), jnp.int32),
            jax.ShapeDtypeStruct((SLOTS, LANES), jnp.float32),
        ] + BINNED,
        in_specs=[whole()] * 3,
        out_specs=[whole()] * (3 + SLOTS),
        compiler_params=pltpu.CompilerParams(vmem_limit_bytes=VMEM),
        cost_estimate=pl.CostEstimate(flops=10**6, bytes_accessed=10**6, transcendentals=0),
        name="widen",
    )(templates, edges, live_count)
    return outs[0], outs[1], outs[2], outs[3:]


def bins_kernel(parts, last, *refs):
    count = len(parts)
    pieces, refs = refs[:count], refs[count:]
    bin_vmem, table_ref, turn_ref, wide_ref, phase_ref = refs[:5]
    refs = refs[5:]
    if last:
        stat_vmem, refs = refs[0], refs[1:]
    refs = refs[SLOTS:]
    binned, refs = refs[:SLOTS], refs[SLOTS:]
    if last:
        out_ref, refs = refs[0], refs[1:]
    prod_ref, rot_ref, step_ref, bin_ref, sems = refs[:5]
    copies = [pltpu.make_async_copy(bin_vmem, bin_ref, sems.at[0])]
    if last:
        stat_ref, best_ref = refs[5:]
        copies.append(pltpu.make_async_copy(stat_vmem, stat_ref, sems.at[1]))
    for copy in copies:
        copy.start()

    lane = lax.broadcasted_iota(jnp.int32, (ROWS, LANES), 1)

    def at_lane(part, place):
        return jnp.sum(jnp.where(lane == place, phase_ref[part, :, FB:], 0.0), axis=1, keepdims=True)

    for part in range(2):
        step_ref[part] = jnp.broadcast_to(at_lane(part, NSL), (ROWS, TW))

    def product(piece_ref, which, c, jj):
        j = c * JS + jj
        both = piece_ref[which, jj].astype(jnp.float32)
        raw_r, raw_i = both[:ROWS], both[ROWS:]
        rc, rs = rot_ref[0], rot_ref[1]
        sr = raw_r * rc - raw_i * rs
        si = raw_r * rs + raw_i * rc
        su = sr + si
        if jj < JS - 1:
            pc = jnp.concatenate([step_ref[0], step_ref[0]], axis=1)
            ps = jnp.concatenate([step_ref[1], step_ref[1]], axis=1)
            rot_ref[0] = rc * pc - rs * ps
            rot_ref[1] = rc * ps + rs * pc
        for pair in range(SLOTS // 2):
            real, imag = [], []
            for k in (2 * pair, 2 * pair + 1):
                h = wide_ref[k, 0, pl.ds(j, 1), :]
                v = wide_ref[k, 1, pl.ds(j, 1), :]
                w = wide_ref[k, 2, pl.ds(j, 1), :]
                k1 = h * su
                real.append(k1 - si * w)
                imag.append(k1 - sr * v)
            base = jj * SLOTS * ROWS + 2 * ROWS * pair
            rows = slice(base, base + 2 * ROWS)
            prod_ref[rows, :FB] = jnp.concatenate(real, axis=0).astype(jnp.bfloat16)
            prod_ref[rows, FB:] = jnp.concatenate(imag, axis=0).astype(jnp.bfloat16)

    def post(c, jj, series):
        j = c * JS + jj
        cos = turn_ref[c, jj, 0:1, :]
        sin = turn_ref[c, jj, 1:2, :]
        for k in range(SLOTS):
            b = bin_ref[k, j]
            re = series[k * ROWS:(k + 1) * ROWS, :TW]
            im = series[k * ROWS:(k + 1) * ROWS, TW:]
            binned[k][b, :, :TW] += cos * re - sin * im
            binned[k][b, :, TW:] += cos * im + sin * re

    number = 0
    for piece_ref, (first, amount, other) in zip(pieces, parts):
        for which in range(amount):
            c = slice_of(first + which, other)
            sc, ss = at_lane(0, c), at_lane(1, c)
            lc, ls = phase_ref[0, :, :FB], phase_ref[1, :, :FB]
            rot_ref[0] = sc * lc - ss * ls
            rot_ref[1] = sc * ls + ss * lc
            for jj in range(JS):
                product(piece_ref, which, c, jj)
            if number == 0:
                for copy in copies:
                    copy.wait()
            number += 1
            half = JS // 2
            size = half * SLOTS * ROWS
            for h in range(2):
                series = jnp.dot(
                    prod_ref[h * size:(h + 1) * size], table_ref[...], preferred_element_type=jnp.float32
                )
                for m in range(half):
                    post(c, h * half + m, series[m * SLOTS * ROWS:(m + 1) * SLOTS * ROWS])

    if last:
        best = jnp.zeros((SEGS, TW), jnp.float32)
        for k in range(SLOTS):
            total = binned[k][0]
            for b in range(1, NBIN):
                total = total + binned[k][b]
            chi = jnp.zeros((ROWS, TW), jnp.float32)
            for b in range(NBIN):
                gap = binned[k][b] - stat_ref[k, b] * total
                gap = gap * gap
                chi = chi + (gap[:, :TW] + gap[:, TW:]) * stat_ref[k, NBIN + b]
            power = total * total
            snr2 = (power[:, :TW] + power[:, TW:]) * stat_ref[k, 2 * NBIN]
            reduced = chi / (2.0 * NBIN - 2.0)
            cube = (1.0 + reduced * reduced * reduced) * 0.5
            factor = jnp.where(reduced > 1.0, jnp.exp(jnp.log(cube) * (-1.0 / 3.0)), 1.0)
            new2 = snr2 * factor
            net2 = new2[:SEGS] + new2[SEGS:2 * SEGS] + new2[2 * SEGS:]
            best = jnp.where(stat_ref[k, 2 * NBIN + 1] > 0.5, jnp.maximum(best, net2), best)
        best = jnp.sqrt(best)
        best_ref[...] = jnp.concatenate(
            [jnp.max(best[:, w * WIN:(w + 1) * WIN], axis=1, keepdims=True) for w in range(NWIN)], axis=1
        )
        for place in range(SEGS):
            out_ref[pl.ds(segment_at(place), 1), :] = best_ref[place:place + 1, :]


def add_bins(pieces, parts, shared, binned, stat=None):
    last = stat is not None
    operands = [*pieces, *shared] + ([stat] if last else []) + list(binned)
    first = len(operands) - SLOTS
    out_shape = list(BINNED)
    scratch = [
        pltpu.VMEM((JS * SLOTS * ROWS, 2 * FB), jnp.bfloat16),
        pltpu.VMEM((2, ROWS, FB), jnp.float32),
        pltpu.VMEM((2, ROWS, TW), jnp.float32),
        pltpu.SMEM((SLOTS, LANES), jnp.int32),
        pltpu.SemaphoreType.DMA((2,)),
    ]
    if last:
        out_shape.append(jax.ShapeDtypeStruct((SEGS, NWIN), jnp.float32))
        scratch += [pltpu.SMEM((SLOTS, LANES), jnp.float32), pltpu.VMEM((SEGS, NWIN), jnp.float32)]
    flops = sum(part[1] for part in parts) * 2 * JS * SLOTS * ROWS * 2 * FB * 2 * TW
    return pl.pallas_call(
        functools.partial(bins_kernel, parts, last),
        out_shape=out_shape,
        in_specs=[whole()] * len(operands),
        out_specs=[whole()] * len(out_shape),
        scratch_shapes=scratch,
        input_output_aliases={first + k: k for k in range(SLOTS)},
        compiler_params=pltpu.CompilerParams(vmem_limit_bytes=VMEM),
        cost_estimate=pl.CostEstimate(flops=2 * flops, bytes_accessed=10**6, transcendentals=0),
        name="last_bins" if last else "add_bins",
    )(*operands)


def phases(shifts):
    row = jnp.arange(ROWS, dtype=jnp.int32)
    segment = segment_at(row % SEGS)
    here = (jnp.arange(SEGS, dtype=jnp.int32)[None, :, None] == segment[:, None, None]) & (
        jnp.arange(NDET, dtype=jnp.int32)[None, None, :] == (row // SEGS)[:, None, None]
    )
    first = MARGIN + jnp.sum(jnp.where(here, shifts[None], 0), axis=(1, 2))
    lane = np.arange(FB + LANES, dtype=np.int32)
    starts = (FLOW // FB + (lane - FB) * JS) * FB
    rate = np.where(lane < FB, lane * STRIDE, np.where(lane < FB + NSL, starts, FB)).astype(np.int32)
    angle = ((first[:, None] * rate[None, :]) % NFFT).astype(jnp.float32) * jnp.float32(TWO_PI / NFFT)
    quarter = np.array([0.0, 0.5 * math.pi], np.float32)[:, None, None]
    return jnp.cos(angle[None] - quarter)


def per_device(strain, templates, live_count, chi_edges, shifts):
    edges = jnp.pad(chi_edges, ((0, 0), (0, LANES - NBIN + 1)), constant_values=NBLK)
    wide, bin_of, stat, binned = widen(templates, edges, live_count)
    table, turn = tables()
    turned = phases(shifts)

    x = jnp.transpose(strain[0], (2, 1, 0, 3)).reshape(JS, 2 * NDET, 1, FB)
    got = {0: x}
    for dx in (2, 3, 1):
        got[dx] = swap_with(x, across(dx=dx))
    x = jnp.concatenate([got[dx] for dx in range(4)], axis=2)
    x, wide, turned = lax.optimization_barrier((x, wide, turned))
    x = jnp.concatenate([x, swap_with(x, across(dy=1))], axis=2)
    shared = (bin_of, table, turn, wide, turned)

    def to_core(piece):
        return swap_with(piece, across(dcore=1))

    def after(value, binned):
        value, first = lax.optimization_barrier((value, binned[0]))
        return value, [first, *binned[1:]]

    p0 = x.reshape(1, JS, 2 * ROWS, FB)
    q0 = to_core(p0)
    p1 = swap_with(p0, step_move(0))
    q1 = to_core(p1)
    binned = add_bins((p0, q0), ((0, 1, 0), (0, 1, 1)), shared, binned)
    p01, binned = after(jnp.concatenate([p0, p1], axis=0), binned)
    p23 = swap_with(p01, step_move(1))
    q23 = to_core(p23)
    binned = add_bins((p1, q1), ((1, 1, 0), (1, 1, 1)), shared, binned)
    (p01, p23), binned = after((p01, p23), binned)
    p45 = swap_with(p01, step_move(2))
    p67 = swap_with(p23, step_move(2))
    q45, q67 = to_core(p45), to_core(p67)
    binned = add_bins((p23, q23), ((2, 2, 0), (2, 2, 1)), shared, binned)
    binned = add_bins((p45, q45), ((4, 2, 0), (4, 2, 1)), shared, binned)
    best = add_bins((p67, q67), ((6, 2, 0), (6, 2, 1)), shared, binned, stat)[-1]
    for move in (across(dcore=1), across(dz=1), across(dz=3), across(dy=2)):
        best = jnp.maximum(best, swap_with(best, move))
    return best[:, None, :]


def solution(mesh):
    in_specs = (
        P("dt", None, None, "tmpl", None),
        P(("dt", "tmpl"), None, None, None),
        P("dt", "tmpl"),
        P(("dt", "tmpl"), None),
        P(),
    )
    out_specs = P(None, "dt", None)
    return jax.shard_map(
        per_device, mesh=mesh, in_specs=in_specs, out_specs=out_specs, check_vma=False
    )
```

```python
import functools
import math

import ml_dtypes
import numpy as np

import jax
import jax.numpy as jnp
from jax import lax
from jax.experimental import pallas as pl
from jax.experimental.pallas import tpu as pltpu
from jax.sharding import PartitionSpec as P

FB = 256
NBLK = 96
NFFT = 1048576
FLOW = 5120
STRIDE = 4097
NBIN = 16
TW = 128
MARGIN = 64
WIN = 16
LANES = 128
NWIN = TW // WIN
NDET = 3
SEGS = 8
SLOTS = 12
NSL = 16
JS = NBLK // NSL
ROWS = NDET * SEGS
EPSILON = 1e-05
TWO_PI = 2.0 * math.pi
AXES = ("dt", "tmpl")
VMEM = 16 * 1024 * 1024


def place_of(index):
    dt, tm = divmod(index, 16)
    return (dt // 2, (tm // 8) * 2 + dt % 2, (tm // 2) % 4, tm % 2)


def index_of(x, y, z, core):
    return (x * 2 + y % 2) * 16 + (y // 2) * 8 + z * 2 + core


def across(dx=0, dy=0, dz=0, dcore=0):
    return lambda x, y, z, core: (x ^ dx, y ^ dy, z ^ dz, core ^ dcore)


def swap_with(value, move):
    pairs = [(index, index_of(*move(*place_of(index)))) for index in range(128)]
    return lax.ppermute(value, AXES, pairs)


def tables():
    tau = np.arange(TW, dtype=np.int64)
    bins = np.arange(FB, dtype=np.int64)
    angle = ((bins[:, None] * tau[None, :] * STRIDE) % NFFT).astype(np.float64) * (TWO_PI / NFFT)
    cosine, sine = np.cos(angle), np.sin(angle)
    local = np.block([[cosine, sine], [-sine, cosine]]).astype(ml_dtypes.bfloat16)
    base = FLOW + np.arange(NBLK, dtype=np.int64) * FB
    angle = ((base[:, None] * tau[None, :] * STRIDE) % NFFT).astype(np.float64) * (TWO_PI / NFFT)
    turn = np.stack([np.cos(angle), np.sin(angle)], axis=1).astype(np.float32)
    return local, turn.reshape(NSL, JS, 2, TW)


STEPS = (
    ({"dy": 2}, {"dz": 1}),
    ({"dz": 1}, {"dz": 3}),
    ({"dz": 3}, {"dy": 2}),
)


def step_move(step):
    first, second = across(**STEPS[step][0]), across(**STEPS[step][1])
    return lambda x, y, z, core: (second if core else first)(x, y, z, core)


def slice_of(piece, other):
    tm = lax.axis_index("tmpl")
    y_hi, z, core = tm // 8, (tm // 2) % 4, (tm % 2) ^ other
    change = []
    for which in range(2):
        dy = dz = 0
        for step in range(3):
            if piece >> step & 1:
                dy ^= STEPS[step][which].get("dy", 0) // 2
                dz ^= STEPS[step][which].get("dz", 0)
        change.append((dy, dz))
    dy = jnp.where(core == 0, change[0][0], change[1][0])
    dz = jnp.where(core == 0, change[0][1], change[1][1])
    return (y_hi ^ dy) * 8 + (z ^ dz) * 2 + core


def segment_at(place):
    dt = lax.axis_index("dt")
    return ((dt // 2) ^ (place % 4)) * 2 + ((dt % 2) ^ (place // 4))


def lane_rates():
    lane = np.arange(FB + LANES, dtype=np.int32)
    starts = (FLOW // FB + (lane - FB) * JS) * FB
    return np.where(lane < FB, lane * STRIDE, np.where(lane < FB + NSL, starts, FB)).astype(np.int32)[None]


def prepare_kernel(
    templ_hbm, edges_hbm, live_hbm, shifts_hbm, rate_hbm, table_hbm, turn_hbm,
    wide_ref, bin_ref, stat_ref, phase_ref, table_ref, turn_ref, *refs,
):
    binned, (templ_ref, edges_ref, live_ref, shifts_ref, rate_ref, upper_ref, first_ref, sems) = refs[:SLOTS], refs[SLOTS:]
    moves = [(edges_hbm, edges_ref), (live_hbm, live_ref), (shifts_hbm, shifts_ref), (rate_hbm, rate_ref)]
    moves += [(templ_hbm.at[k], templ_ref.at[k]) for k in range(SLOTS)]
    moves += [(table_hbm, table_ref), (turn_hbm, turn_ref)]
    copies = [pltpu.make_async_copy(a, b, sems.at[n]) for n, (a, b) in enumerate(moves)]
    for copy in copies:
        copy.start()
    for ref in binned:
        ref[...] = jnp.zeros_like(ref)
    for copy in copies[:4]:
        copy.wait()

    for place in range(SEGS):
        first_ref[place:place + 1, :] = shifts_ref[pl.ds(segment_at(place), 1), :]
    ordered = first_ref[...] + MARGIN
    first = jnp.concatenate([ordered[:, d:d + 1] for d in range(NDET)], axis=0)
    turns = (first * rate_ref[...]) & (NFFT - 1)
    angle = turns.astype(jnp.float32) * jnp.float32(TWO_PI / NFFT)
    phase_ref[0] = jnp.cos(angle)
    phase_ref[1] = jnp.sin(angle)

    lane = lax.broadcasted_iota(jnp.int32, (SLOTS, LANES), 1)
    bin_of = jnp.zeros((SLOTS, LANES), jnp.int32)
    for e in range(NBIN - 1):
        bin_of = bin_of + (edges_ref[:, e:e + 1] <= lane).astype(jnp.int32)
    bin_ref[...] = bin_of
    upper_ref[...] = jnp.full((SLOTS, LANES), NBLK, jnp.int32)
    upper_ref[:, :NBIN - 1] = edges_ref[...]
    block = lax.broadcasted_iota(jnp.int32, (NBLK, LANES), 0)
    at_lane = lax.broadcasted_iota(jnp.int32, (1, LANES), 1)
    for k in range(SLOTS):
        copies[4 + k].wait()
        h = templ_ref[k, 0].astype(jnp.float32)
        i = templ_ref[k, 1].astype(jnp.float32)
        wide_ref[k, 0] = h
        wide_ref[k, 1] = h + i
        wide_ref[k, 2] = h - i
        power = jnp.sum(h * h + i * i, axis=1, keepdims=True)
        upper = upper_ref[k:k + 1, :]
        lower = jnp.where(at_lane == 0, 0, pltpu.roll(upper, 1, 1))
        inside = jnp.where((block >= lower) & (block < upper), power, 0.0)
        in_bins = jnp.sum(inside, axis=0, keepdims=True)
        sigma2 = jnp.sum(power, axis=0, keepdims=True) + EPSILON
        frac = (in_bins + EPSILON) / sigma2
        inv = pltpu.roll(1.0 / (frac * sigma2), NBIN, 1)
        live = (k < live_ref[...]).astype(jnp.float32)
        row = jnp.where(at_lane == 2 * NBIN, 0.5 / sigma2, live)
        row = jnp.where(at_lane < 2 * NBIN, inv, row)
        stat_ref[k:k + 1, :] = jnp.where(at_lane < NBIN, frac, row)
    for copy in copies[4 + SLOTS:]:
        copy.wait()


def whole():
    return pl.BlockSpec(memory_space=pltpu.VMEM)


BINNED = [jax.ShapeDtypeStruct((NBIN, ROWS, 2 * TW), jnp.float32)] * SLOTS


def prepare(templates, edges, live_count, shifts):
    table, turn = tables()
    operands = (templates, edges, live_count, shifts, lane_rates(), table, turn)
    outs = pl.pallas_call(
        prepare_kernel,
        out_shape=[
            jax.ShapeDtypeStruct((SLOTS, 3, NBLK, FB), jnp.float32),
            jax.ShapeDtypeStruct((SLOTS, LANES), jnp.int32),
            jax.ShapeDtypeStruct((SLOTS, LANES), jnp.float32),
            jax.ShapeDtypeStruct((2, ROWS, FB + LANES), jnp.float32),
            jax.ShapeDtypeStruct(table.shape, table.dtype),
            jax.ShapeDtypeStruct(turn.shape, turn.dtype),
        ] + BINNED,
        in_specs=[pl.BlockSpec(memory_space=pl.ANY)] * len(operands),
        out_specs=[whole()] * (6 + SLOTS),
        scratch_shapes=[
            pltpu.VMEM(templates.shape, templates.dtype),
            pltpu.VMEM(edges.shape, jnp.int32),
            pltpu.VMEM(live_count.shape, jnp.int32),
            pltpu.VMEM(shifts.shape, jnp.int32),
            pltpu.VMEM((1, FB + LANES), jnp.int32),
            pltpu.VMEM((SLOTS, LANES), jnp.int32),
            pltpu.VMEM(shifts.shape, jnp.int32),
            pltpu.SemaphoreType.DMA((6 + SLOTS,)),
        ],
        compiler_params=pltpu.CompilerParams(vmem_limit_bytes=VMEM),
        cost_estimate=pl.CostEstimate(flops=10**6, bytes_accessed=10**6, transcendentals=0),
        name="prepare",
    )(*operands)
    return outs[:6], outs[6:]


def bins_kernel(parts, last, *refs):
    count = len(parts)
    pieces, refs = refs[:count], refs[count:]
    bin_vmem, table_ref, turn_ref, wide_ref, phase_ref = refs[:5]
    refs = refs[5:]
    if last:
        stat_vmem, refs = refs[0], refs[1:]
    refs = refs[SLOTS:]
    binned, refs = refs[:SLOTS], refs[SLOTS:]
    if last:
        out_ref, refs = refs[0], refs[1:]
    prod_ref, rot_ref, step_ref, bin_ref, sems = refs[:5]
    copies = [pltpu.make_async_copy(bin_vmem, bin_ref, sems.at[0])]
    if last:
        stat_ref, best_ref = refs[5:]
        copies.append(pltpu.make_async_copy(stat_vmem, stat_ref, sems.at[1]))
    for copy in copies:
        copy.start()

    lane = lax.broadcasted_iota(jnp.int32, (ROWS, LANES), 1)

    def at_lane(part, place):
        return jnp.sum(jnp.where(lane == place, phase_ref[part, :, FB:], 0.0), axis=1, keepdims=True)

    for part in range(2):
        step_ref[part] = jnp.broadcast_to(at_lane(part, NSL), (ROWS, TW))

    def product(piece_ref, which, c, jj):
        j = c * JS + jj
        both = piece_ref[which, jj].astype(jnp.float32)
        raw_r, raw_i = both[:ROWS], both[ROWS:]
        rc, rs = rot_ref[0], rot_ref[1]
        sr = raw_r * rc - raw_i * rs
        si = raw_r * rs + raw_i * rc
        su = sr + si
        if jj < JS - 1:
            pc = jnp.concatenate([step_ref[0], step_ref[0]], axis=1)
            ps = jnp.concatenate([step_ref[1], step_ref[1]], axis=1)
            rot_ref[0] = rc * pc - rs * ps
            rot_ref[1] = rc * ps + rs * pc
        for pair in range(SLOTS // 2):
            real, imag = [], []
            for k in (2 * pair, 2 * pair + 1):
                h = wide_ref[k, 0, pl.ds(j, 1), :]
                v = wide_ref[k, 1, pl.ds(j, 1), :]
                w = wide_ref[k, 2, pl.ds(j, 1), :]
                k1 = h * su
                real.append(k1 - si * w)
                imag.append(k1 - sr * v)
            base = jj * SLOTS * ROWS + 2 * ROWS * pair
            rows = slice(base, base + 2 * ROWS)
            prod_ref[rows, :FB] = jnp.concatenate(real, axis=0).astype(jnp.bfloat16)
            prod_ref[rows, FB:] = jnp.concatenate(imag, axis=0).astype(jnp.bfloat16)

    def post(c, jj, series):
        j = c * JS + jj
        cos = turn_ref[c, jj, 0:1, :]
        sin = turn_ref[c, jj, 1:2, :]
        for k in range(SLOTS):
            b = bin_ref[k, j]
            re = series[k * ROWS:(k + 1) * ROWS, :TW]
            im = series[k * ROWS:(k + 1) * ROWS, TW:]
            binned[k][b, :, :TW] += cos * re - sin * im
            binned[k][b, :, TW:] += cos * im + sin * re

    number = 0
    for piece_ref, (first, amount, other) in zip(pieces, parts):
        for which in range(amount):
            c = slice_of(first + which, other)
            sc, ss = at_lane(0, c), at_lane(1, c)
            lc, ls = phase_ref[0, :, :FB], phase_ref[1, :, :FB]
            rot_ref[0] = sc * lc - ss * ls
            rot_ref[1] = sc * ls + ss * lc
            for jj in range(JS):
                product(piece_ref, which, c, jj)
            if number == 0:
                for copy in copies:
                    copy.wait()
            number += 1
            half = JS // 2
            size = half * SLOTS * ROWS
            for h in range(2):
                series = jnp.dot(
                    prod_ref[h * size:(h + 1) * size], table_ref[...], preferred_element_type=jnp.float32
                )
                for m in range(half):
                    post(c, h * half + m, series[m * SLOTS * ROWS:(m + 1) * SLOTS * ROWS])

    if last:
        best = jnp.zeros((SEGS, TW), jnp.float32)
        for k in range(SLOTS):
            total = binned[k][0]
            for b in range(1, NBIN):
                total = total + binned[k][b]
            chi = jnp.zeros((ROWS, TW), jnp.float32)
            for b in range(NBIN):
                gap = binned[k][b] - stat_ref[k, b] * total
                gap = gap * gap
                chi = chi + (gap[:, :TW] + gap[:, TW:]) * stat_ref[k, NBIN + b]
            power = total * total
            snr2 = (power[:, :TW] + power[:, TW:]) * stat_ref[k, 2 * NBIN]
            reduced = chi / (2.0 * NBIN - 2.0)
            cube = (1.0 + reduced * reduced * reduced) * 0.5
            factor = jnp.where(reduced > 1.0, jnp.exp(jnp.log(cube) * (-1.0 / 3.0)), 1.0)
            new2 = snr2 * factor
            net2 = new2[:SEGS] + new2[SEGS:2 * SEGS] + new2[2 * SEGS:]
            best = jnp.where(stat_ref[k, 2 * NBIN + 1] > 0.5, jnp.maximum(best, net2), best)
        best = jnp.sqrt(best)
        best_ref[...] = jnp.concatenate(
            [jnp.max(best[:, w * WIN:(w + 1) * WIN], axis=1, keepdims=True) for w in range(NWIN)], axis=1
        )
        for place in range(SEGS):
            out_ref[pl.ds(segment_at(place), 1), :] = best_ref[place:place + 1, :]


def add_bins(pieces, parts, shared, binned, stat=None):
    last = stat is not None
    operands = [*pieces, *shared] + ([stat] if last else []) + list(binned)
    first = len(operands) - SLOTS
    out_shape = list(BINNED)
    scratch = [
        pltpu.VMEM((JS * SLOTS * ROWS, 2 * FB), jnp.bfloat16),
        pltpu.VMEM((2, ROWS, FB), jnp.float32),
        pltpu.VMEM((2, ROWS, TW), jnp.float32),
        pltpu.SMEM((SLOTS, LANES), jnp.int32),
        pltpu.SemaphoreType.DMA((2,)),
    ]
    if last:
        out_shape.append(jax.ShapeDtypeStruct((SEGS, NWIN), jnp.float32))
        scratch += [pltpu.SMEM((SLOTS, LANES), jnp.float32), pltpu.VMEM((SEGS, NWIN), jnp.float32)]
    flops = sum(part[1] for part in parts) * 2 * JS * SLOTS * ROWS * 2 * FB * 2 * TW
    return pl.pallas_call(
        functools.partial(bins_kernel, parts, last),
        out_shape=out_shape,
        in_specs=[whole()] * len(operands),
        out_specs=[whole()] * len(out_shape),
        scratch_shapes=scratch,
        input_output_aliases={first + k: k for k in range(SLOTS)},
        compiler_params=pltpu.CompilerParams(vmem_limit_bytes=VMEM),
        cost_estimate=pl.CostEstimate(flops=2 * flops, bytes_accessed=10**6, transcendentals=0),
        name="last_bins" if last else "add_bins",
    )(*operands)


def per_device(strain, templates, live_count, chi_edges, shifts):
    (wide, bin_of, stat, turned, table, turn), binned = prepare(templates, chi_edges, live_count, shifts)

    x = jnp.transpose(strain[0], (2, 1, 0, 3)).reshape(JS, 2 * NDET, 1, FB)
    got = {0: x}
    for dx in (2, 3, 1):
        got[dx] = swap_with(x, across(dx=dx))
    x = jnp.concatenate([got[dx] for dx in range(4)], axis=2)
    x, wide = lax.optimization_barrier((x, wide))
    x = jnp.concatenate([x, swap_with(x, across(dy=1))], axis=2)
    shared = (bin_of, table, turn, wide, turned)

    def to_core(piece):
        return swap_with(piece, across(dcore=1))

    def after(value, binned):
        value, first = lax.optimization_barrier((value, binned[0]))
        return value, [first, *binned[1:]]

    p0 = x.reshape(1, JS, 2 * ROWS, FB)
    q0 = to_core(p0)
    p1 = swap_with(p0, step_move(0))
    binned = add_bins((p0, q0), ((0, 1, 0), (0, 1, 1)), shared, binned)
    p1, binned = after(p1, binned)
    q1 = to_core(p1)
    p01 = jnp.concatenate([p0, p1], axis=0)
    p23 = swap_with(p01, step_move(1))
    binned = add_bins((p1, q1), ((1, 1, 0), (1, 1, 1)), shared, binned)
    p23, binned = after(p23, binned)
    q23 = to_core(p23)
    p01, p23 = lax.optimization_barrier((p01, p23))
    p45 = swap_with(p01, step_move(2))
    p67 = swap_with(p23, step_move(2))
    binned = add_bins((p23, q23), ((2, 2, 0), (2, 2, 1)), shared, binned)
    (p45, p67), binned = after((p45, p67), binned)
    q45, q67 = to_core(p45), to_core(p67)
    binned = add_bins((p45, q45), ((4, 2, 0), (4, 2, 1)), shared, binned)
    best = add_bins((p67, q67), ((6, 2, 0), (6, 2, 1)), shared, binned, stat)[-1]
    for move in (across(dcore=1), across(dz=1), across(dz=3), across(dy=2)):
        best = jnp.maximum(best, swap_with(best, move))
    return best[:, None, :]


def solution(mesh):
    in_specs = (
        P("dt", None, None, "tmpl", None),
        P(("dt", "tmpl"), None, None, None),
        P("dt", "tmpl"),
        P(("dt", "tmpl"), None),
        P(),
    )
    out_specs = P(None, "dt", None)
    return jax.shard_map(
        per_device, mesh=mesh, in_specs=in_specs, out_specs=out_specs, check_vma=False
    )
```

```python
import functools
import math

import jax
import jax.numpy as jnp
from jax import lax
from jax.experimental import pallas as pl
from jax.experimental.pallas import tpu as pltpu
from jax.sharding import PartitionSpec as P

FB = 256
NBLK = 96
NFFT = 1048576
FLOW = 5120
STRIDE = 4097
NBIN = 16
TW = 128
MARGIN = 64
WIN = 16
LANES = 128
SPREAD = 40
NWIN = TW // WIN
NDET = 3
SEGS = 8
SLOTS = 12
NSL = 16
JS = NBLK // NSL
ROWS = NDET * SEGS
EPSILON = 1e-05
TWO_PI = 2.0 * math.pi
AXES = ("dt", "tmpl")
VMEM = 16 * 1024 * 1024


def place_of(index):
    dt, tm = divmod(index, 16)
    return (dt // 2, (tm // 8) * 2 + dt % 2, (tm // 2) % 4, tm % 2)


def index_of(x, y, z, core):
    return (x * 2 + y % 2) * 16 + (y // 2) * 8 + z * 2 + core


def across(dx=0, dy=0, dz=0, dcore=0):
    return lambda x, y, z, core: (x ^ dx, y ^ dy, z ^ dz, core ^ dcore)


def swap_with(value, move):
    pairs = [(index, index_of(*move(*place_of(index)))) for index in range(128)]
    return lax.ppermute(value, AXES, pairs)


STEPS = (
    ({"dy": 3}, {"dz": 1}),
    ({"dz": 1}, {"dz": 3}),
    ({"dz": 3}, {"dy": 3}),
)


def step_move(step):
    first, second = across(**STEPS[step][0]), across(**STEPS[step][1])
    return lambda x, y, z, core: (second if core else first)(x, y, z, core)


def slice_of(piece, other):
    tm = lax.axis_index("tmpl")
    y_hi, z, core = tm // 8, (tm // 2) % 4, (tm % 2) ^ other
    change = []
    for which in range(2):
        dy = dz = 0
        for step in range(3):
            if piece >> step & 1:
                dy ^= STEPS[step][which].get("dy", 0) // 2
                dz ^= STEPS[step][which].get("dz", 0)
        change.append((dy, dz))
    dy = jnp.where(core == 0, change[0][0], change[1][0])
    dz = jnp.where(core == 0, change[0][1], change[1][1])
    return (y_hi ^ dy) * 8 + (z ^ dz) * 2 + core


def segment_at(place):
    return ((lax.axis_index("dt") // 2) ^ (place & 3)) * 2 + (place >> 2)


def circle(turns):
    turns = turns + NFFT // 8
    quarter = (turns >> 18) & 3
    rest = (turns & (NFFT // 4 - 1)) - NFFT // 8
    angle = rest.astype(jnp.float32) * jnp.float32(TWO_PI / NFFT)
    square = angle * angle
    cosine = 1.0 + square * (-1 / 2 + square * (1 / 24 + square * (-1 / 720 + square * (1 / 40320))))
    sine = angle * (1.0 + square * (-1 / 6 + square * (1 / 120 + square * (-1 / 5040 + square * (1 / 362880)))))
    odd = (quarter & 1) == 1
    real, imag = jnp.where(odd, -sine, cosine), jnp.where(odd, cosine, sine)
    return jnp.where(quarter >= 2, -real, real), jnp.where(quarter >= 2, -imag, imag)


def counted(shape, axis):
    return lax.broadcasted_iota(jnp.int32, shape, axis)


def tables_kernel(small_ref, bin_ref, phase_ref, table_ref, turn_ref, *binned):
    for ref in binned:
        ref[...] = jnp.zeros_like(ref)

    cosine, sine = circle(counted((FB, TW), 0) * counted((FB, TW), 1) * STRIDE)
    table_ref[:FB, :TW] = cosine.astype(jnp.bfloat16)
    table_ref[:FB, TW:] = sine.astype(jnp.bfloat16)
    table_ref[FB:, :TW] = (-sine).astype(jnp.bfloat16)
    table_ref[FB:, TW:] = cosine.astype(jnp.bfloat16)
    shape = (NSL, 8, TW)
    number = FLOW // FB + counted(shape, 0) * JS + counted(shape, 1)
    turn_ref[0], turn_ref[1] = circle(number * counted(shape, 2) * FB)

    place = counted((ROWS, LANES), 0) & (SEGS - 1)
    here = segment_at(place) == counted((ROWS, LANES), 1)
    spread = [jnp.broadcast_to(small_ref[SLOTS + d:SLOTS + d + 1, :], (SEGS, LANES)) for d in range(NDET)]
    held = jnp.where(here, jnp.concatenate(spread, axis=0), 0).astype(jnp.float32)
    first = MARGIN + jnp.sum(held, axis=1, keepdims=True).astype(jnp.int32)
    lane = counted((1, FB + LANES), 1)
    starts = (FLOW // FB + (lane - FB) * JS) * FB
    rate = jnp.where(lane < FB, lane * STRIDE, jnp.where(lane < FB + NSL, starts, FB))
    phase_ref[0], phase_ref[1] = circle(first * rate)

    lane = counted((SLOTS, LANES), 1)
    bin_of = jnp.zeros((SLOTS, LANES), jnp.int32)
    for e in range(NBIN - 1):
        bin_of = bin_of + (small_ref[:SLOTS, e:e + 1] <= lane).astype(jnp.int32)
    digit = counted((LANES, LANES), 0) - JS * counted((LANES, LANES), 1)
    held = (digit >= 0) & (digit < JS)
    weight = jnp.where(held, 1 << (4 * jnp.where(held, digit, 0)), 0).astype(jnp.float32)
    digits = bin_of.astype(jnp.float32).astype(jnp.bfloat16)
    bin_ref[...] = jnp.dot(digits, weight.astype(jnp.bfloat16), preferred_element_type=jnp.float32)


def templates_kernel(templ_ref, small_ref, wide_ref, spread_ref, stat_ref):
    stat_ref[...] = jnp.zeros_like(stat_ref)
    block = counted((NBLK, LANES), 0)
    at_lane = counted((1, LANES), 1)
    live_count = small_ref[SLOTS + NDET:SLOTS + NDET + 1, :]
    for k in range(SLOTS):
        h = templ_ref[k, 0].astype(jnp.float32)
        i = templ_ref[k, 1].astype(jnp.float32)
        wide_ref[k, 0] = h
        wide_ref[k, 1] = h + i
        wide_ref[k, 2] = h - i
        power = jnp.sum(h * h + i * i, axis=1, keepdims=True)
        upper = small_ref[k:k + 1, :]
        lower = jnp.where(at_lane == 0, 0, pltpu.roll(upper, 1, 1))
        inside = jnp.where((block >= lower) & (block < upper), power, 0.0)
        in_bins = jnp.sum(inside, axis=0, keepdims=True)
        sigma2 = jnp.sum(power, axis=0, keepdims=True) + EPSILON
        frac = (in_bins + EPSILON) / sigma2
        inv = pltpu.roll(1.0 / (frac * sigma2), NBIN, 1)
        live = (k < live_count).astype(jnp.float32)
        row = jnp.where(at_lane == 2 * NBIN, 0.5 / sigma2, live)
        row = jnp.where(at_lane < 2 * NBIN, inv, row)
        stat_ref[k:k + 1, :] = jnp.where(at_lane < NBIN, frac, row)
    columns = stat_ref[...].T
    for k in range(SLOTS):
        spread_ref[k] = jnp.broadcast_to(columns[:SPREAD, k:k + 1], (SPREAD, LANES))


def whole():
    return pl.BlockSpec(memory_space=pltpu.VMEM)


BINNED = [jax.ShapeDtypeStruct((NBIN, ROWS, 2 * TW), jnp.float32)] * SLOTS


def small_numbers(edges, live_count, shifts):
    return jnp.concatenate([
        jnp.pad(edges, ((0, 0), (0, LANES - NBIN + 1)), constant_values=NBLK),
        jnp.pad(shifts.T, ((0, 0), (0, LANES - SEGS))),
        jnp.broadcast_to(live_count, (1, LANES)),
    ], axis=0)


def prepare_tables(small):
    outs = pl.pallas_call(
        tables_kernel,
        out_shape=[
            jax.ShapeDtypeStruct((SLOTS, LANES), jnp.float32),
            jax.ShapeDtypeStruct((2, ROWS, FB + LANES), jnp.float32),
            jax.ShapeDtypeStruct((2 * FB, 2 * TW), jnp.bfloat16),
            jax.ShapeDtypeStruct((2, NSL, 8, TW), jnp.float32),
        ] + BINNED,
        in_specs=[whole()],
        out_specs=[whole()] * (4 + SLOTS),
        compiler_params=pltpu.CompilerParams(vmem_limit_bytes=VMEM),
        cost_estimate=pl.CostEstimate(flops=10**6, bytes_accessed=10**6, transcendentals=0),
        name="prepare_tables",
    )(small)
    return outs[:4], outs[4:]


def prepare_templates(templates, small):
    return pl.pallas_call(
        templates_kernel,
        out_shape=[
            jax.ShapeDtypeStruct((SLOTS, 3, NBLK, FB), jnp.float32),
            jax.ShapeDtypeStruct((SLOTS, SPREAD, LANES), jnp.float32),
        ],
        in_specs=[whole()] * 2,
        out_specs=[whole()] * 2,
        scratch_shapes=[pltpu.VMEM((LANES, LANES), jnp.float32)],
        compiler_params=pltpu.CompilerParams(vmem_limit_bytes=VMEM),
        cost_estimate=pl.CostEstimate(flops=10**6, bytes_accessed=10**6, transcendentals=0),
        name="prepare_templates",
    )(templates, small)


def bins_kernel(parts, last, *refs):
    count = len(parts)
    pieces, refs = refs[:count], refs[count:]
    bin_ref, table_ref, turn_ref, wide_ref, phase_ref = refs[:5]
    refs = refs[5:]
    if last:
        stat_ref, refs = refs[0], refs[1:]
    refs = refs[SLOTS:]
    binned, refs = refs[:SLOTS], refs[SLOTS:]
    if last:
        out_ref, refs = refs[0], refs[1:]
    prod_ref, rot_ref, step_ref = refs[:3]
    if last:
        best_ref = refs[3]

    lane = lax.broadcasted_iota(jnp.int32, (ROWS, LANES), 1)

    def at_lane(part, place):
        return jnp.sum(jnp.where(lane == place, phase_ref[part, :, FB:], 0.0), axis=1, keepdims=True)

    for part in range(2):
        step_ref[part] = jnp.broadcast_to(at_lane(part, NSL), (ROWS, TW))

    def product(piece_ref, which, c, jj):
        j = c * JS + jj
        both = piece_ref[which, jj].astype(jnp.float32)
        raw_r, raw_i = both[:ROWS], both[ROWS:]
        rc, rs = rot_ref[0], rot_ref[1]
        sr = raw_r * rc - raw_i * rs
        si = raw_r * rs + raw_i * rc
        su = sr + si
        if jj < JS - 1:
            pc = jnp.concatenate([step_ref[0], step_ref[0]], axis=1)
            ps = jnp.concatenate([step_ref[1], step_ref[1]], axis=1)
            rot_ref[0] = rc * pc - rs * ps
            rot_ref[1] = rc * ps + rs * pc
        for pair in range(SLOTS // 2):
            real, imag = [], []
            for k in (2 * pair, 2 * pair + 1):
                h = wide_ref[k, 0, pl.ds(j, 1), :]
                v = wide_ref[k, 1, pl.ds(j, 1), :]
                w = wide_ref[k, 2, pl.ds(j, 1), :]
                k1 = h * su
                real.append(k1 - si * w)
                imag.append(k1 - sr * v)
            base = jj * SLOTS * ROWS + 2 * ROWS * pair
            rows = slice(base, base + 2 * ROWS)
            prod_ref[rows, :FB] = jnp.concatenate(real, axis=0).astype(jnp.bfloat16)
            prod_ref[rows, FB:] = jnp.concatenate(imag, axis=0).astype(jnp.bfloat16)

    def post(c, jj, digits, series):
        cos = turn_ref[0, c, jj:jj + 1, :]
        sin = turn_ref[1, c, jj:jj + 1, :]
        for k in range(SLOTS):
            b = (digits[k] >> (4 * jj)) & (NBIN - 1)
            re = series[k * ROWS:(k + 1) * ROWS, :TW]
            im = series[k * ROWS:(k + 1) * ROWS, TW:]
            binned[k][b, :, :TW] += cos * re - sin * im
            binned[k][b, :, TW:] += cos * im + sin * re

    for piece_ref, (first, amount, other) in zip(pieces, parts):
        for which in range(amount):
            c = slice_of(first + which, other)
            sc, ss = at_lane(0, c), at_lane(1, c)
            slot_lane = lax.broadcasted_iota(jnp.int32, (SLOTS, LANES), 1)
            packed = jnp.sum(jnp.where(slot_lane == c, bin_ref[...], 0.0), axis=1, keepdims=True).astype(jnp.int32)
            digits = [packed[k, 0] for k in range(SLOTS)]
            lc, ls = phase_ref[0, :, :FB], phase_ref[1, :, :FB]
            rot_ref[0] = sc * lc - ss * ls
            rot_ref[1] = sc * ls + ss * lc
            for jj in range(JS):
                product(piece_ref, which, c, jj)
            half = JS // 2
            size = half * SLOTS * ROWS
            for h in range(2):
                series = jnp.dot(
                    prod_ref[h * size:(h + 1) * size], table_ref[...], preferred_element_type=jnp.float32
                )
                for m in range(half):
                    post(c, h * half + m, digits, series[m * SLOTS * ROWS:(m + 1) * SLOTS * ROWS])

    if last:
        best = jnp.zeros((SEGS, TW), jnp.float32)
        for k in range(SLOTS):
            total = binned[k][0]
            for b in range(1, NBIN):
                total = total + binned[k][b]
            chi = jnp.zeros((ROWS, TW), jnp.float32)
            for b in range(NBIN):
                share = jnp.concatenate([stat_ref[k, b:b + 1, :]] * 2, axis=1)
                gap = binned[k][b] - share * total
                gap = gap * gap
                chi = chi + (gap[:, :TW] + gap[:, TW:]) * stat_ref[k, NBIN + b:NBIN + b + 1, :]
            power = total * total
            snr2 = (power[:, :TW] + power[:, TW:]) * stat_ref[k, 2 * NBIN:2 * NBIN + 1, :]
            reduced = chi / (2.0 * NBIN - 2.0)
            cube = (1.0 + reduced * reduced * reduced) * 0.5
            factor = jnp.where(reduced > 1.0, jnp.exp(jnp.log(cube) * (-1.0 / 3.0)), 1.0)
            new2 = snr2 * factor
            net2 = new2[:SEGS] + new2[SEGS:2 * SEGS] + new2[2 * SEGS:]
            best = jnp.where(stat_ref[k, 2 * NBIN + 1:2 * NBIN + 2, :] > 0.5, jnp.maximum(best, net2), best)
        best = jnp.sqrt(best)
        best_ref[...] = jnp.concatenate(
            [jnp.max(best[:, w * WIN:(w + 1) * WIN], axis=1, keepdims=True) for w in range(NWIN)], axis=1
        )
        for place in range(SEGS):
            out_ref[pl.ds(segment_at(place), 1), :] = best_ref[place:place + 1, :]


def add_bins(pieces, parts, shared, binned, stat=None):
    last = stat is not None
    operands = [*pieces, *shared] + ([stat] if last else []) + list(binned)
    first = len(operands) - SLOTS
    out_shape = list(BINNED)
    scratch = [
        pltpu.VMEM((JS * SLOTS * ROWS, 2 * FB), jnp.bfloat16),
        pltpu.VMEM((2, ROWS, FB), jnp.float32),
        pltpu.VMEM((2, ROWS, TW), jnp.float32),
    ]
    if last:
        out_shape.append(jax.ShapeDtypeStruct((SEGS, NWIN), jnp.float32))
        scratch.append(pltpu.VMEM((SEGS, NWIN), jnp.float32))
    flops = sum(part[1] for part in parts) * 2 * JS * SLOTS * ROWS * 2 * FB * 2 * TW
    return pl.pallas_call(
        functools.partial(bins_kernel, parts, last),
        out_shape=out_shape,
        in_specs=[whole()] * len(operands),
        out_specs=[whole()] * len(out_shape),
        scratch_shapes=scratch,
        input_output_aliases={first + k: k for k in range(SLOTS)},
        compiler_params=pltpu.CompilerParams(vmem_limit_bytes=VMEM),
        cost_estimate=pl.CostEstimate(flops=2 * flops, bytes_accessed=10**6, transcendentals=0),
        name="last_bins" if last else "add_bins",
    )(*operands)


def per_device(strain, templates, live_count, chi_edges, shifts):
    small = small_numbers(chi_edges, live_count, shifts)
    (bin_of, turned, table, turn), binned = prepare_tables(small)
    wide, stat = prepare_templates(templates, small)

    x = jnp.transpose(strain[0], (2, 1, 0, 3)).reshape(JS, 2 * NDET, 1, FB)
    got = {0: x}
    for dx in (2, 3, 1):
        got[dx] = swap_with(x, across(dx=dx))
    x = jnp.concatenate([got[dx] for dx in range(4)], axis=2)
    x, turned = lax.optimization_barrier((x, turned))
    got = swap_with(x, across(dy=1))
    even = lax.axis_index("dt") % 2 == 0
    x, got, wide = lax.optimization_barrier((x, got, wide))
    x = jnp.concatenate([jnp.where(even, x, got), jnp.where(even, got, x)], axis=2)
    shared = (bin_of, table, turn, wide, turned)

    def to_core(piece):
        return swap_with(piece, across(dcore=1))

    def after(value, binned):
        value, first = lax.optimization_barrier((value, binned[0]))
        return value, [first, *binned[1:]]

    p0 = x.reshape(1, JS, 2 * ROWS, FB)
    q0 = to_core(p0)
    p1 = swap_with(p0, step_move(0))
    binned = add_bins((p0, q0), ((0, 1, 0), (0, 1, 1)), shared, binned)
    p1, binned = after(p1, binned)
    q1 = to_core(p1)
    p01 = jnp.concatenate([p0, p1], axis=0)
    p23 = swap_with(p01, step_move(1))
    binned = add_bins((p1, q1), ((1, 1, 0), (1, 1, 1)), shared, binned)
    p23, binned = after(p23, binned)
    q23 = to_core(p23)
    p01, p23 = lax.optimization_barrier((p01, p23))
    p45 = swap_with(p01, step_move(2))
    p67 = swap_with(p23, step_move(2))
    binned = add_bins((p23, q23), ((2, 2, 0), (2, 2, 1)), shared, binned)
    p45, binned = after(p45, binned)
    q45 = to_core(p45)
    binned = add_bins((p45,), ((4, 2, 0),), shared, binned)
    p67, binned = after(p67, binned)
    q67 = to_core(p67)
    binned = add_bins((q45,), ((4, 2, 1),), shared, binned)
    binned = add_bins((p67,), ((6, 2, 0),), shared, binned)
    best = add_bins((q67,), ((6, 2, 1),), shared, binned, stat)[-1]
    for move in (across(dcore=1), across(dz=1), across(dz=3), across(dy=2)):
        best = jnp.maximum(best, swap_with(best, move))
    return best[:, None, :]


def solution(mesh):
    in_specs = (
        P("dt", None, None, "tmpl", None),
        P(("dt", "tmpl"), None, None, None),
        P("dt", "tmpl"),
        P(("dt", "tmpl"), None),
        P(),
    )
    out_specs = P(None, "dt", None)
    return jax.shard_map(
        per_device, mesh=mesh, in_specs=in_specs, out_specs=out_specs, check_vma=False
    )
```

```python
import functools
import math

import jax
import jax.numpy as jnp
from jax import lax
from jax.experimental import pallas as pl
from jax.experimental.pallas import tpu as pltpu
from jax.sharding import PartitionSpec as P

FB = 256
NBLK = 96
NFFT = 1048576
FLOW = 5120
STRIDE = 4097
NBIN = 16
TW = 128
MARGIN = 64
WIN = 16
LANES = 128
SPREAD = 40
NWIN = TW // WIN
NDET = 3
SEGS = 8
SLOTS = 12
NSL = 16
JS = NBLK // NSL
ROWS = NDET * SEGS
EPSILON = 1e-05
TWO_PI = 2.0 * math.pi
AXES = ("dt", "tmpl")
VMEM = 16 * 1024 * 1024


def place_of(index):
    dt, tm = divmod(index, 16)
    return (dt // 2, (tm // 8) * 2 + dt % 2, (tm // 2) % 4, tm % 2)


def index_of(x, y, z, core):
    return (x * 2 + y % 2) * 16 + (y // 2) * 8 + z * 2 + core


def across(dx=0, dy=0, dz=0, dcore=0):
    return lambda x, y, z, core: (x ^ dx, y ^ dy, z ^ dz, core ^ dcore)


def swap_with(value, move):
    pairs = [(index, index_of(*move(*place_of(index)))) for index in range(128)]
    return lax.ppermute(value, AXES, pairs)


STEPS = (
    ({"dy": 3}, {"dz": 1}),
    ({"dz": 1}, {"dz": 3}),
    ({"dz": 3}, {"dy": 3}),
)


def step_move(step):
    first, second = across(**STEPS[step][0]), across(**STEPS[step][1])
    return lambda x, y, z, core: (second if core else first)(x, y, z, core)


def slice_of(piece, other):
    tm = lax.axis_index("tmpl")
    y_hi, z, core = tm // 8, (tm // 2) % 4, (tm % 2) ^ other
    change = []
    for which in range(2):
        dy = dz = 0
        for step in range(3):
            if piece >> step & 1:
                dy ^= STEPS[step][which].get("dy", 0) // 2
                dz ^= STEPS[step][which].get("dz", 0)
        change.append((dy, dz))
    dy = jnp.where(core == 0, change[0][0], change[1][0])
    dz = jnp.where(core == 0, change[0][1], change[1][1])
    return (y_hi ^ dy) * 8 + (z ^ dz) * 2 + core


def segment_at(place):
    return ((lax.axis_index("dt") // 2) ^ (place & 3)) * 2 + (place >> 2)


def circle(turns):
    turns = turns + NFFT // 8
    quarter = (turns >> 18) & 3
    rest = (turns & (NFFT // 4 - 1)) - NFFT // 8
    angle = rest.astype(jnp.float32) * jnp.float32(TWO_PI / NFFT)
    square = angle * angle
    cosine = 1.0 + square * (-1 / 2 + square * (1 / 24 + square * (-1 / 720 + square * (1 / 40320))))
    sine = angle * (1.0 + square * (-1 / 6 + square * (1 / 120 + square * (-1 / 5040 + square * (1 / 362880)))))
    odd = (quarter & 1) == 1
    real, imag = jnp.where(odd, -sine, cosine), jnp.where(odd, cosine, sine)
    return jnp.where(quarter >= 2, -real, real), jnp.where(quarter >= 2, -imag, imag)


def counted(shape, axis):
    return lax.broadcasted_iota(jnp.int32, shape, axis)


def tables_kernel(small_ref, bin_ref, phase_ref, table_ref, turn_ref, *binned):
    for ref in binned:
        ref[...] = jnp.zeros_like(ref)

    cosine, sine = circle(counted((FB, TW), 0) * counted((FB, TW), 1) * STRIDE)
    table_ref[:FB, :TW] = cosine.astype(jnp.bfloat16)
    table_ref[:FB, TW:] = sine.astype(jnp.bfloat16)
    table_ref[FB:, :TW] = (-sine).astype(jnp.bfloat16)
    table_ref[FB:, TW:] = cosine.astype(jnp.bfloat16)
    shape = (NSL, 8, TW)
    number = FLOW // FB + counted(shape, 0) * JS + counted(shape, 1)
    turn_ref[0], turn_ref[1] = circle(number * counted(shape, 2) * FB)

    place = counted((ROWS, LANES), 0) & (SEGS - 1)
    here = segment_at(place) == counted((ROWS, LANES), 1)
    spread = [jnp.broadcast_to(small_ref[SLOTS + d:SLOTS + d + 1, :], (SEGS, LANES)) for d in range(NDET)]
    held = jnp.where(here, jnp.concatenate(spread, axis=0), 0).astype(jnp.float32)
    first = MARGIN + jnp.sum(held, axis=1, keepdims=True).astype(jnp.int32)
    lane = counted((1, FB + LANES), 1)
    starts = (FLOW // FB + (lane - FB) * JS) * FB
    rate = jnp.where(lane < FB, lane * STRIDE, jnp.where(lane < FB + NSL, starts, FB))
    phase_ref[0], phase_ref[1] = circle(first * rate)

    lane = counted((SLOTS, LANES), 1)
    bin_of = jnp.zeros((SLOTS, LANES), jnp.int32)
    for e in range(NBIN - 1):
        bin_of = bin_of + (small_ref[:SLOTS, e:e + 1] <= lane).astype(jnp.int32)
    digit = counted((LANES, LANES), 0) - JS * counted((LANES, LANES), 1)
    held = (digit >= 0) & (digit < JS)
    weight = jnp.where(held, 1 << (4 * jnp.where(held, digit, 0)), 0).astype(jnp.float32)
    digits = bin_of.astype(jnp.float32).astype(jnp.bfloat16)
    bin_ref[...] = jnp.dot(digits, weight.astype(jnp.bfloat16), preferred_element_type=jnp.float32)


def templates_kernel(templ_ref, small_ref, wide_ref, spread_ref, stat_ref):
    stat_ref[...] = jnp.zeros_like(stat_ref)
    block = counted((NBLK, LANES), 0)
    at_lane = counted((1, LANES), 1)
    live_count = small_ref[SLOTS + NDET:SLOTS + NDET + 1, :]
    for k in range(SLOTS):
        h = templ_ref[k, 0].astype(jnp.float32)
        i = templ_ref[k, 1].astype(jnp.float32)
        wide_ref[k, 0] = h
        wide_ref[k, 1] = h + i
        wide_ref[k, 2] = h - i
        power = jnp.sum(h * h + i * i, axis=1, keepdims=True)
        upper = small_ref[k:k + 1, :]
        lower = jnp.where(at_lane == 0, 0, pltpu.roll(upper, 1, 1))
        inside = jnp.where((block >= lower) & (block < upper), power, 0.0)
        in_bins = jnp.sum(inside, axis=0, keepdims=True)
        sigma2 = jnp.sum(power, axis=0, keepdims=True) + EPSILON
        frac = (in_bins + EPSILON) / sigma2
        inv = pltpu.roll(1.0 / (frac * sigma2), NBIN, 1)
        live = (k < live_count).astype(jnp.float32)
        row = jnp.where(at_lane == 2 * NBIN, 0.5 / sigma2, live)
        row = jnp.where(at_lane < 2 * NBIN, inv, row)
        stat_ref[k:k + 1, :] = jnp.where(at_lane < NBIN, frac, row)
    columns = stat_ref[...].T
    for k in range(SLOTS):
        spread_ref[k] = jnp.broadcast_to(columns[:SPREAD, k:k + 1], (SPREAD, LANES))


def whole():
    return pl.BlockSpec(memory_space=pltpu.VMEM)


BINNED = [jax.ShapeDtypeStruct((NBIN, ROWS, 2 * TW), jnp.float32)] * SLOTS


def small_numbers(edges, live_count, shifts):
    return jnp.concatenate([
        jnp.pad(edges, ((0, 0), (0, LANES - NBIN + 1)), constant_values=NBLK),
        jnp.pad(shifts.T, ((0, 0), (0, LANES - SEGS))),
        jnp.broadcast_to(live_count, (1, LANES)),
    ], axis=0)


def prepare_tables(small):
    outs = pl.pallas_call(
        tables_kernel,
        out_shape=[
            jax.ShapeDtypeStruct((SLOTS, LANES), jnp.float32),
            jax.ShapeDtypeStruct((2, ROWS, FB + LANES), jnp.float32),
            jax.ShapeDtypeStruct((2 * FB, 2 * TW), jnp.bfloat16),
            jax.ShapeDtypeStruct((2, NSL, 8, TW), jnp.float32),
        ] + BINNED,
        in_specs=[whole()],
        out_specs=[whole()] * (4 + SLOTS),
        compiler_params=pltpu.CompilerParams(vmem_limit_bytes=VMEM),
        cost_estimate=pl.CostEstimate(flops=10**6, bytes_accessed=10**6, transcendentals=0),
        name="prepare_tables",
    )(small)
    return outs[:4], outs[4:]


def prepare_templates(templates, small):
    return pl.pallas_call(
        templates_kernel,
        out_shape=[
            jax.ShapeDtypeStruct((SLOTS, 3, NBLK, FB), jnp.float32),
            jax.ShapeDtypeStruct((SLOTS, SPREAD, LANES), jnp.float32),
        ],
        in_specs=[whole()] * 2,
        out_specs=[whole()] * 2,
        scratch_shapes=[pltpu.VMEM((LANES, LANES), jnp.float32)],
        compiler_params=pltpu.CompilerParams(vmem_limit_bytes=VMEM),
        cost_estimate=pl.CostEstimate(flops=10**6, bytes_accessed=10**6, transcendentals=0),
        name="prepare_templates",
    )(templates, small)


def bins_kernel(parts, last, *refs):
    count = len(parts)
    pieces, refs = refs[:count], refs[count:]
    bin_ref, table_ref, turn_ref, wide_ref, phase_ref = refs[:5]
    refs = refs[5:]
    if last:
        stat_ref, refs = refs[0], refs[1:]
    refs = refs[SLOTS:]
    binned, refs = refs[:SLOTS], refs[SLOTS:]
    if last:
        out_ref, refs = refs[0], refs[1:]
    prod_ref, rot_ref, step_ref = refs[:3]
    if last:
        best_ref = refs[3]

    lane = lax.broadcasted_iota(jnp.int32, (ROWS, LANES), 1)

    def at_lane(part, place):
        return jnp.sum(jnp.where(lane == place, phase_ref[part, :, FB:], 0.0), axis=1, keepdims=True)

    for part in range(2):
        step_ref[part] = jnp.broadcast_to(at_lane(part, NSL), (ROWS, TW))

    def product(piece_ref, which, c, jj):
        j = c * JS + jj
        both = piece_ref[which, jj].astype(jnp.float32)
        raw_r, raw_i = both[:ROWS], both[ROWS:]
        rc, rs = rot_ref[0], rot_ref[1]
        sr = raw_r * rc - raw_i * rs
        si = raw_r * rs + raw_i * rc
        su = sr + si
        if jj < JS - 1:
            pc = jnp.concatenate([step_ref[0], step_ref[0]], axis=1)
            ps = jnp.concatenate([step_ref[1], step_ref[1]], axis=1)
            rot_ref[0] = rc * pc - rs * ps
            rot_ref[1] = rc * ps + rs * pc
        for pair in range(SLOTS // 2):
            real, imag = [], []
            for k in (2 * pair, 2 * pair + 1):
                h = wide_ref[k, 0, pl.ds(j, 1), :]
                v = wide_ref[k, 1, pl.ds(j, 1), :]
                w = wide_ref[k, 2, pl.ds(j, 1), :]
                k1 = h * su
                real.append(k1 - si * w)
                imag.append(k1 - sr * v)
            base = jj * SLOTS * ROWS + 2 * ROWS * pair
            rows = slice(base, base + 2 * ROWS)
            prod_ref[rows, :FB] = jnp.concatenate(real, axis=0).astype(jnp.bfloat16)
            prod_ref[rows, FB:] = jnp.concatenate(imag, axis=0).astype(jnp.bfloat16)

    def post(c, jj, digits, series):
        cos = turn_ref[0, c, jj:jj + 1, :]
        sin = turn_ref[1, c, jj:jj + 1, :]
        for k in range(SLOTS):
            b = (digits[k] >> (4 * jj)) & (NBIN - 1)
            re = series[k * ROWS:(k + 1) * ROWS, :TW]
            im = series[k * ROWS:(k + 1) * ROWS, TW:]
            binned[k][b, :, :TW] += cos * re - sin * im
            binned[k][b, :, TW:] += cos * im + sin * re

    for piece_ref, (first, amount, other) in zip(pieces, parts):
        for which in range(amount):
            c = slice_of(first + which, other)
            sc, ss = at_lane(0, c), at_lane(1, c)
            slot_lane = lax.broadcasted_iota(jnp.int32, (SLOTS, LANES), 1)
            packed = jnp.sum(jnp.where(slot_lane == c, bin_ref[...], 0.0), axis=1, keepdims=True).astype(jnp.int32)
            digits = [packed[k, 0] for k in range(SLOTS)]
            lc, ls = phase_ref[0, :, :FB], phase_ref[1, :, :FB]
            rot_ref[0] = sc * lc - ss * ls
            rot_ref[1] = sc * ls + ss * lc
            for jj in range(JS):
                product(piece_ref, which, c, jj)
            half = JS // 2
            size = half * SLOTS * ROWS
            for h in range(2):
                series = jnp.dot(
                    prod_ref[h * size:(h + 1) * size], table_ref[...], preferred_element_type=jnp.float32
                )
                for m in range(half):
                    post(c, h * half + m, digits, series[m * SLOTS * ROWS:(m + 1) * SLOTS * ROWS])

    if last:
        best = jnp.zeros((SEGS, TW), jnp.float32)
        for k in range(SLOTS):
            total = binned[k][0]
            for b in range(1, NBIN):
                total = total + binned[k][b]
            chi = jnp.zeros((ROWS, TW), jnp.float32)
            for b in range(NBIN):
                share = jnp.concatenate([stat_ref[k, b:b + 1, :]] * 2, axis=1)
                gap = binned[k][b] - share * total
                gap = gap * gap
                chi = chi + (gap[:, :TW] + gap[:, TW:]) * stat_ref[k, NBIN + b:NBIN + b + 1, :]
            power = total * total
            snr2 = (power[:, :TW] + power[:, TW:]) * stat_ref[k, 2 * NBIN:2 * NBIN + 1, :]
            reduced = chi / (2.0 * NBIN - 2.0)
            cube = (1.0 + reduced * reduced * reduced) * 0.5
            factor = jnp.where(reduced > 1.0, jnp.exp(jnp.log(cube) * (-1.0 / 3.0)), 1.0)
            new2 = snr2 * factor
            net2 = new2[:SEGS] + new2[SEGS:2 * SEGS] + new2[2 * SEGS:]
            best = jnp.where(stat_ref[k, 2 * NBIN + 1:2 * NBIN + 2, :] > 0.5, jnp.maximum(best, net2), best)
        best = jnp.sqrt(best)
        best_ref[...] = jnp.concatenate(
            [jnp.max(best[:, w * WIN:(w + 1) * WIN], axis=1, keepdims=True) for w in range(NWIN)], axis=1
        )
        for place in range(SEGS):
            out_ref[pl.ds(segment_at(place), 1), :] = best_ref[place:place + 1, :]


def add_bins(pieces, parts, shared, binned, stat=None):
    last = stat is not None
    operands = [*pieces, *shared] + ([stat] if last else []) + list(binned)
    first = len(operands) - SLOTS
    out_shape = list(BINNED)
    scratch = [
        pltpu.VMEM((JS * SLOTS * ROWS, 2 * FB), jnp.bfloat16),
        pltpu.VMEM((2, ROWS, FB), jnp.float32),
        pltpu.VMEM((2, ROWS, TW), jnp.float32),
    ]
    if last:
        out_shape.append(jax.ShapeDtypeStruct((SEGS, NWIN), jnp.float32))
        scratch.append(pltpu.VMEM((SEGS, NWIN), jnp.float32))
    flops = sum(part[1] for part in parts) * 2 * JS * SLOTS * ROWS * 2 * FB * 2 * TW
    return pl.pallas_call(
        functools.partial(bins_kernel, parts, last),
        out_shape=out_shape,
        in_specs=[whole()] * len(operands),
        out_specs=[whole()] * len(out_shape),
        scratch_shapes=scratch,
        input_output_aliases={first + k: k for k in range(SLOTS)},
        compiler_params=pltpu.CompilerParams(vmem_limit_bytes=VMEM),
        cost_estimate=pl.CostEstimate(flops=2 * flops, bytes_accessed=10**6, transcendentals=0),
        name="last_bins" if last else "add_bins",
    )(*operands)


def per_device(strain, templates, live_count, chi_edges, shifts):
    small = small_numbers(chi_edges, live_count, shifts)
    (bin_of, turned, table, turn), binned = prepare_tables(small)
    wide, stat = prepare_templates(templates, small)

    shard, even = lax.optimization_barrier((strain[0], lax.axis_index("dt") % 2 == 0))
    x = jnp.transpose(shard, (2, 1, 0, 3)).reshape(JS, 2 * NDET, 1, FB)
    got = {0: x}
    for dx in (2, 3, 1):
        got[dx] = swap_with(x, across(dx=dx))
    x = jnp.concatenate([got[dx] for dx in range(4)], axis=2)
    x, turned = lax.optimization_barrier((x, turned))
    got = swap_with(x, across(dy=1))
    x, got, wide = lax.optimization_barrier((x, got, wide))
    x = jnp.concatenate([jnp.where(even, x, got), jnp.where(even, got, x)], axis=2)
    shared = (bin_of, table, turn, wide, turned)

    def to_core(piece):
        return swap_with(piece, across(dcore=1))

    def after(value, binned):
        value, first = lax.optimization_barrier((value, binned[0]))
        return value, [first, *binned[1:]]

    p0 = x.reshape(1, JS, 2 * ROWS, FB)
    q0 = to_core(p0)
    p1 = swap_with(p0, step_move(0))
    binned = add_bins((p0, q0), ((0, 1, 0), (0, 1, 1)), shared, binned)
    p1, binned = after(p1, binned)
    q1 = to_core(p1)
    p01 = jnp.concatenate([p0, p1], axis=0)
    p23 = swap_with(p01, step_move(1))
    binned = add_bins((p1, q1), ((1, 1, 0), (1, 1, 1)), shared, binned)
    p23, binned = after(p23, binned)
    q23 = to_core(p23)
    p01, p23 = lax.optimization_barrier((p01, p23))
    p45 = swap_with(p01, step_move(2))
    p67 = swap_with(p23, step_move(2))
    binned = add_bins((p23, q23), ((2, 2, 0), (2, 2, 1)), shared, binned)
    p45, binned = after(p45, binned)
    q45 = to_core(p45)
    binned = add_bins((p45,), ((4, 2, 0),), shared, binned)
    p67, binned = after(p67, binned)
    q67 = to_core(p67)
    binned = add_bins((q45,), ((4, 2, 1),), shared, binned)
    binned = add_bins((p67,), ((6, 2, 0),), shared, binned)
    best = add_bins((q67,), ((6, 2, 1),), shared, binned, stat)[-1]
    for move in (across(dcore=1), across(dz=1), across(dz=3), across(dy=2)):
        best = jnp.maximum(best, swap_with(best, move))
    return best[:, None, :]


def solution(mesh):
    in_specs = (
        P("dt", None, None, "tmpl", None),
        P(("dt", "tmpl"), None, None, None),
        P("dt", "tmpl"),
        P(("dt", "tmpl"), None),
        P(),
    )
    out_specs = P(None, "dt", None)
    return jax.shard_map(
        per_device, mesh=mesh, in_specs=in_specs, out_specs=out_specs, check_vma=False
    )
```

```python
import functools
import math

import jax
import jax.numpy as jnp
from jax import lax
from jax.experimental import pallas as pl
from jax.experimental.pallas import tpu as pltpu
from jax.sharding import PartitionSpec as P

FB = 256
NBLK = 96
NFFT = 1048576
FLOW = 5120
STRIDE = 4097
NBIN = 16
TW = 128
MARGIN = 64
WIN = 16
LANES = 128
SPREAD = 40
NWIN = TW // WIN
NDET = 3
SEGS = 8
SLOTS = 12
NSL = 16
JS = NBLK // NSL
ROWS = NDET * SEGS
EPSILON = 1e-05
TWO_PI = 2.0 * math.pi
AXES = ("dt", "tmpl")
VMEM = 16 * 1024 * 1024


def place_of(index):
    dt, tm = divmod(index, 16)
    return (dt // 2, (tm // 8) * 2 + dt % 2, (tm // 2) % 4, tm % 2)


def index_of(x, y, z, core):
    return (x * 2 + y % 2) * 16 + (y // 2) * 8 + z * 2 + core


def across(dx=0, dy=0, dz=0, dcore=0):
    return lambda x, y, z, core: (x ^ dx, y ^ dy, z ^ dz, core ^ dcore)


def swap_with(value, move):
    pairs = [(index, index_of(*move(*place_of(index)))) for index in range(128)]
    return lax.ppermute(value, AXES, pairs)


STEPS = (
    ({"dy": 3}, {"dz": 1}),
    ({"dz": 1}, {"dz": 3}),
    ({"dz": 3}, {"dy": 3}),
)


def step_move(step):
    first, second = across(**STEPS[step][0]), across(**STEPS[step][1])
    return lambda x, y, z, core: (second if core else first)(x, y, z, core)


def slice_of(piece, other):
    tm = lax.axis_index("tmpl")
    y_hi, z, core = tm // 8, (tm // 2) % 4, (tm % 2) ^ other
    change = []
    for which in range(2):
        dy = dz = 0
        for step in range(3):
            if piece >> step & 1:
                dy ^= STEPS[step][which].get("dy", 0) // 2
                dz ^= STEPS[step][which].get("dz", 0)
        change.append((dy, dz))
    dy = jnp.where(core == 0, change[0][0], change[1][0])
    dz = jnp.where(core == 0, change[0][1], change[1][1])
    return (y_hi ^ dy) * 8 + (z ^ dz) * 2 + core


def segment_at(place):
    return ((lax.axis_index("dt") // 2) ^ (place & 3)) * 2 + (place >> 2)


def circle(turns):
    turns = turns + NFFT // 8
    quarter = (turns >> 18) & 3
    rest = (turns & (NFFT // 4 - 1)) - NFFT // 8
    angle = rest.astype(jnp.float32) * jnp.float32(TWO_PI / NFFT)
    square = angle * angle
    cosine = 1.0 + square * (-1 / 2 + square * (1 / 24 + square * (-1 / 720 + square * (1 / 40320))))
    sine = angle * (1.0 + square * (-1 / 6 + square * (1 / 120 + square * (-1 / 5040 + square * (1 / 362880)))))
    odd = (quarter & 1) == 1
    real, imag = jnp.where(odd, -sine, cosine), jnp.where(odd, cosine, sine)
    return jnp.where(quarter >= 2, -real, real), jnp.where(quarter >= 2, -imag, imag)


def counted(shape, axis):
    return lax.broadcasted_iota(jnp.int32, shape, axis)


def tables_kernel(small_ref, bin_ref, turned_ref, table_ref, turn_ref, *refs):
    binned, (now_ref,) = refs[:SLOTS], refs[SLOTS:]
    for ref in binned:
        ref[...] = jnp.zeros_like(ref)

    cosine, sine = circle(counted((FB, TW), 0) * counted((FB, TW), 1) * STRIDE)
    table_ref[:FB, :TW] = cosine.astype(jnp.bfloat16)
    table_ref[:FB, TW:] = sine.astype(jnp.bfloat16)
    table_ref[FB:, :TW] = (-sine).astype(jnp.bfloat16)
    table_ref[FB:, TW:] = cosine.astype(jnp.bfloat16)
    shape = (NSL, 8, TW)
    number = FLOW // FB + counted(shape, 0) * JS + counted(shape, 1)
    turn_ref[0], turn_ref[1] = circle(number * counted(shape, 2) * FB)

    place = counted((ROWS, LANES), 0) & (SEGS - 1)
    here = segment_at(place) == counted((ROWS, LANES), 1)
    spread = [jnp.broadcast_to(small_ref[SLOTS + d:SLOTS + d + 1, :], (SEGS, LANES)) for d in range(NDET)]
    held = jnp.where(here, jnp.concatenate(spread, axis=0), 0).astype(jnp.float32)
    first = MARGIN + jnp.sum(held, axis=1, keepdims=True).astype(jnp.int32)
    now_ref[0], now_ref[1] = circle(first * (FLOW + counted((1, FB), 1)) * STRIDE)
    pc, ps = circle(jnp.broadcast_to(first * FB, (ROWS, TW)))
    pc, ps = jnp.concatenate([pc, pc], axis=1), jnp.concatenate([ps, ps], axis=1)

    def one_block(j, carry):
        rc, rs = now_ref[0], now_ref[1]
        turned_ref[j, 0] = rc
        turned_ref[j, 1] = rs
        now_ref[0] = rc * pc - rs * ps
        now_ref[1] = rc * ps + rs * pc
        return carry

    lax.fori_loop(0, NBLK, one_block, 0)

    lane = counted((SLOTS, LANES), 1)
    bin_of = jnp.zeros((SLOTS, LANES), jnp.int32)
    for e in range(NBIN - 1):
        bin_of = bin_of + (small_ref[:SLOTS, e:e + 1] <= lane).astype(jnp.int32)
    digit = counted((LANES, LANES), 0) - JS * counted((LANES, LANES), 1)
    held = (digit >= 0) & (digit < JS)
    weight = jnp.where(held, 1 << (4 * jnp.where(held, digit, 0)), 0).astype(jnp.float32)
    digits = bin_of.astype(jnp.float32).astype(jnp.bfloat16)
    bin_ref[...] = jnp.dot(digits, weight.astype(jnp.bfloat16), preferred_element_type=jnp.float32)


def templates_kernel(templ_ref, small_ref, wide_ref, spread_ref, stat_ref):
    stat_ref[...] = jnp.zeros_like(stat_ref)
    block = counted((NBLK, LANES), 0)
    at_lane = counted((1, LANES), 1)
    live_count = small_ref[SLOTS + NDET:SLOTS + NDET + 1, :]
    for k in range(SLOTS):
        h = templ_ref[k, 0].astype(jnp.float32)
        i = templ_ref[k, 1].astype(jnp.float32)
        wide_ref[k, 0] = h
        wide_ref[k, 1] = h + i
        wide_ref[k, 2] = h - i
        power = jnp.sum(h * h + i * i, axis=1, keepdims=True)
        upper = small_ref[k:k + 1, :]
        lower = jnp.where(at_lane == 0, 0, pltpu.roll(upper, 1, 1))
        inside = jnp.where((block >= lower) & (block < upper), power, 0.0)
        in_bins = jnp.sum(inside, axis=0, keepdims=True)
        sigma2 = jnp.sum(power, axis=0, keepdims=True) + EPSILON
        frac = (in_bins + EPSILON) / sigma2
        inv = pltpu.roll(1.0 / (frac * sigma2), NBIN, 1)
        live = (k < live_count).astype(jnp.float32)
        row = jnp.where(at_lane == 2 * NBIN, 0.5 / sigma2, live)
        row = jnp.where(at_lane < 2 * NBIN, inv, row)
        stat_ref[k:k + 1, :] = jnp.where(at_lane < NBIN, frac, row)
    columns = stat_ref[...].T
    for k in range(SLOTS):
        spread_ref[k] = jnp.broadcast_to(columns[:SPREAD, k:k + 1], (SPREAD, LANES))


def whole():
    return pl.BlockSpec(memory_space=pltpu.VMEM)


BINNED = [jax.ShapeDtypeStruct((NBIN, ROWS, 2 * TW), jnp.float32)] * SLOTS


def small_numbers(edges, live_count, shifts):
    return jnp.concatenate([
        jnp.pad(edges, ((0, 0), (0, LANES - NBIN + 1)), constant_values=NBLK),
        jnp.pad(shifts.T, ((0, 0), (0, LANES - SEGS))),
        jnp.broadcast_to(live_count, (1, LANES)),
    ], axis=0)


def prepare_tables(small):
    outs = pl.pallas_call(
        tables_kernel,
        out_shape=[
            jax.ShapeDtypeStruct((SLOTS, LANES), jnp.float32),
            jax.ShapeDtypeStruct((NBLK, 2, ROWS, FB), jnp.float32),
            jax.ShapeDtypeStruct((2 * FB, 2 * TW), jnp.bfloat16),
            jax.ShapeDtypeStruct((2, NSL, 8, TW), jnp.float32),
        ] + BINNED,
        in_specs=[whole()],
        out_specs=[whole()] * (4 + SLOTS),
        scratch_shapes=[pltpu.VMEM((2, ROWS, FB), jnp.float32)],
        compiler_params=pltpu.CompilerParams(vmem_limit_bytes=VMEM),
        cost_estimate=pl.CostEstimate(flops=10**6, bytes_accessed=10**6, transcendentals=0),
        name="prepare_tables",
    )(small)
    return outs[:4], outs[4:]


def prepare_templates(templates, small):
    return pl.pallas_call(
        templates_kernel,
        out_shape=[
            jax.ShapeDtypeStruct((SLOTS, 3, NBLK, FB), jnp.float32),
            jax.ShapeDtypeStruct((SLOTS, SPREAD, LANES), jnp.float32),
        ],
        in_specs=[whole()] * 2,
        out_specs=[whole()] * 2,
        scratch_shapes=[pltpu.VMEM((LANES, LANES), jnp.float32)],
        compiler_params=pltpu.CompilerParams(vmem_limit_bytes=VMEM),
        cost_estimate=pl.CostEstimate(flops=10**6, bytes_accessed=10**6, transcendentals=0),
        name="prepare_templates",
    )(templates, small)


def bins_kernel(parts, last, *refs):
    count = len(parts)
    pieces, refs = refs[:count], refs[count:]
    bin_ref, table_ref, turn_ref, wide_ref, turned_ref = refs[:5]
    refs = refs[5:]
    if last:
        stat_ref, refs = refs[0], refs[1:]
    refs = refs[SLOTS:]
    binned, refs = refs[:SLOTS], refs[SLOTS:]
    if last:
        out_ref, refs = refs[0], refs[1:]
    prod_ref = refs[0]
    if last:
        best_ref = refs[1]

    def product(piece_ref, which, c, jj):
        j = c * JS + jj
        both = piece_ref[which, jj].astype(jnp.float32)
        raw_r, raw_i = both[:ROWS], both[ROWS:]
        rc, rs = turned_ref[j, 0], turned_ref[j, 1]
        sr = raw_r * rc - raw_i * rs
        si = raw_r * rs + raw_i * rc
        su = sr + si
        for pair in range(SLOTS // 2):
            real, imag = [], []
            for k in (2 * pair, 2 * pair + 1):
                h = wide_ref[k, 0, pl.ds(j, 1), :]
                v = wide_ref[k, 1, pl.ds(j, 1), :]
                w = wide_ref[k, 2, pl.ds(j, 1), :]
                k1 = h * su
                real.append(k1 - si * w)
                imag.append(k1 - sr * v)
            base = jj * SLOTS * ROWS + 2 * ROWS * pair
            rows = slice(base, base + 2 * ROWS)
            prod_ref[rows, :FB] = jnp.concatenate(real, axis=0).astype(jnp.bfloat16)
            prod_ref[rows, FB:] = jnp.concatenate(imag, axis=0).astype(jnp.bfloat16)

    def post(c, jj, digits, series):
        cos = turn_ref[0, c, jj:jj + 1, :]
        sin = turn_ref[1, c, jj:jj + 1, :]
        for k in range(SLOTS):
            b = (digits[k] >> (4 * jj)) & (NBIN - 1)
            re = series[k * ROWS:(k + 1) * ROWS, :TW]
            im = series[k * ROWS:(k + 1) * ROWS, TW:]
            binned[k][b, :, :TW] += cos * re - sin * im
            binned[k][b, :, TW:] += cos * im + sin * re

    for piece_ref, (first, amount, other) in zip(pieces, parts):
        for which in range(amount):
            c = slice_of(first + which, other)
            slot_lane = lax.broadcasted_iota(jnp.int32, (SLOTS, LANES), 1)
            packed = jnp.sum(jnp.where(slot_lane == c, bin_ref[...], 0.0), axis=1, keepdims=True).astype(jnp.int32)
            digits = [packed[k, 0] for k in range(SLOTS)]
            for jj in range(JS):
                product(piece_ref, which, c, jj)
            half = JS // 2
            size = half * SLOTS * ROWS
            for h in range(2):
                series = jnp.dot(
                    prod_ref[h * size:(h + 1) * size], table_ref[...], preferred_element_type=jnp.float32
                )
                for m in range(half):
                    post(c, h * half + m, digits, series[m * SLOTS * ROWS:(m + 1) * SLOTS * ROWS])

    if last:
        best = jnp.zeros((SEGS, TW), jnp.float32)
        for k in range(SLOTS):
            total = binned[k][0]
            for b in range(1, NBIN):
                total = total + binned[k][b]
            chi = jnp.zeros((ROWS, TW), jnp.float32)
            for b in range(NBIN):
                share = jnp.concatenate([stat_ref[k, b:b + 1, :]] * 2, axis=1)
                gap = binned[k][b] - share * total
                gap = gap * gap
                chi = chi + (gap[:, :TW] + gap[:, TW:]) * stat_ref[k, NBIN + b:NBIN + b + 1, :]
            power = total * total
            snr2 = (power[:, :TW] + power[:, TW:]) * stat_ref[k, 2 * NBIN:2 * NBIN + 1, :]
            reduced = chi / (2.0 * NBIN - 2.0)
            cube = (1.0 + reduced * reduced * reduced) * 0.5
            factor = jnp.where(reduced > 1.0, jnp.exp(jnp.log(cube) * (-1.0 / 3.0)), 1.0)
            new2 = snr2 * factor
            net2 = new2[:SEGS] + new2[SEGS:2 * SEGS] + new2[2 * SEGS:]
            best = jnp.where(stat_ref[k, 2 * NBIN + 1:2 * NBIN + 2, :] > 0.5, jnp.maximum(best, net2), best)
        best = jnp.sqrt(best)
        best_ref[...] = jnp.concatenate(
            [jnp.max(best[:, w * WIN:(w + 1) * WIN], axis=1, keepdims=True) for w in range(NWIN)], axis=1
        )
        for place in range(SEGS):
            out_ref[pl.ds(segment_at(place), 1), :] = best_ref[place:place + 1, :]


def add_bins(pieces, parts, shared, binned, stat=None):
    last = stat is not None
    operands = [*pieces, *shared] + ([stat] if last else []) + list(binned)
    first = len(operands) - SLOTS
    out_shape = list(BINNED)
    scratch = [
        pltpu.VMEM((JS * SLOTS * ROWS, 2 * FB), jnp.bfloat16),
    ]
    if last:
        out_shape.append(jax.ShapeDtypeStruct((SEGS, NWIN), jnp.float32))
        scratch.append(pltpu.VMEM((SEGS, NWIN), jnp.float32))
    flops = sum(part[1] for part in parts) * 2 * JS * SLOTS * ROWS * 2 * FB * 2 * TW
    return pl.pallas_call(
        functools.partial(bins_kernel, parts, last),
        out_shape=out_shape,
        in_specs=[whole()] * len(operands),
        out_specs=[whole()] * len(out_shape),
        scratch_shapes=scratch,
        input_output_aliases={first + k: k for k in range(SLOTS)},
        compiler_params=pltpu.CompilerParams(vmem_limit_bytes=VMEM),
        cost_estimate=pl.CostEstimate(flops=2 * flops, bytes_accessed=10**6, transcendentals=0),
        name="last_bins" if last else "add_bins",
    )(*operands)


def per_device(strain, templates, live_count, chi_edges, shifts):
    small = small_numbers(chi_edges, live_count, shifts)
    (bin_of, turned, table, turn), binned = prepare_tables(small)
    wide, stat = prepare_templates(templates, small)

    shard, even = lax.optimization_barrier((strain[0], lax.axis_index("dt") % 2 == 0))
    x = jnp.transpose(shard, (2, 1, 0, 3)).reshape(JS, 2 * NDET, 1, FB)
    got = {0: x}
    for dx in (2, 3, 1):
        got[dx] = swap_with(x, across(dx=dx))
    x = jnp.concatenate([got[dx] for dx in range(4)], axis=2)
    x, turned = lax.optimization_barrier((x, turned))
    got = swap_with(x, across(dy=1))
    x, got, wide = lax.optimization_barrier((x, got, wide))
    x = jnp.concatenate([jnp.where(even, x, got), jnp.where(even, got, x)], axis=2)
    shared = (bin_of, table, turn, wide, turned)

    def to_core(piece):
        return swap_with(piece, across(dcore=1))

    def after(value, binned):
        value, first = lax.optimization_barrier((value, binned[0]))
        return value, [first, *binned[1:]]

    p0 = x.reshape(1, JS, 2 * ROWS, FB)
    q0 = to_core(p0)
    p1 = swap_with(p0, step_move(0))
    binned = add_bins((p0, q0), ((0, 1, 0), (0, 1, 1)), shared, binned)
    p1, binned = after(p1, binned)
    q1 = to_core(p1)
    p01 = jnp.concatenate([p0, p1], axis=0)
    p23 = swap_with(p01, step_move(1))
    binned = add_bins((p1,), ((1, 1, 0),), shared, binned)
    p23, binned = after(p23, binned)
    p01, p23 = lax.optimization_barrier((p01, p23))
    p45 = swap_with(p01, step_move(2))
    p67 = swap_with(p23, step_move(2))
    binned = add_bins((p23,), ((2, 2, 0),), shared, binned)
    p23, binned = after(p23, binned)
    q23 = to_core(p23)
    binned = add_bins((q1,), ((1, 1, 1),), shared, binned)
    binned = add_bins((q23,), ((2, 2, 1),), shared, binned)
    p45, binned = after(p45, binned)
    q45 = to_core(p45)
    binned = add_bins((p45,), ((4, 2, 0),), shared, binned)
    p67, binned = after(p67, binned)
    q67 = to_core(p67)
    binned = add_bins((q45,), ((4, 2, 1),), shared, binned)
    binned = add_bins((p67,), ((6, 2, 0),), shared, binned)
    best = add_bins((q67,), ((6, 2, 1),), shared, binned, stat)[-1]
    for move in (across(dcore=1), across(dz=1), across(dz=3), across(dy=2)):
        best = jnp.maximum(best, swap_with(best, move))
    return best[:, None, :]


def solution(mesh):
    in_specs = (
        P("dt", None, None, "tmpl", None),
        P(("dt", "tmpl"), None, None, None),
        P("dt", "tmpl"),
        P(("dt", "tmpl"), None),
        P(),
    )
    out_specs = P(None, "dt", None)
    return jax.shard_map(
        per_device, mesh=mesh, in_specs=in_specs, out_specs=out_specs, check_vma=False
    )
```

```python
import functools
import math

import jax
import jax.numpy as jnp
from jax import lax
from jax.experimental import pallas as pl
from jax.experimental.pallas import tpu as pltpu
from jax.sharding import PartitionSpec as P

FB = 256
NBLK = 96
NFFT = 1048576
FLOW = 5120
STRIDE = 4097
NBIN = 16
TW = 128
MARGIN = 64
WIN = 16
LANES = 128
SPREAD = 40
NWIN = TW // WIN
NDET = 3
SEGS = 8
SLOTS = 12
NSL = 16
JS = NBLK // NSL
ROWS = NDET * SEGS
EPSILON = 1e-05
TWO_PI = 2.0 * math.pi
AXES = ("dt", "tmpl")
VMEM = 16 * 1024 * 1024


def place_of(index):
    dt, tm = divmod(index, 16)
    return (dt // 2, (tm // 8) * 2 + dt % 2, (tm // 2) % 4, tm % 2)


def index_of(x, y, z, core):
    return (x * 2 + y % 2) * 16 + (y // 2) * 8 + z * 2 + core


def across(dx=0, dy=0, dz=0, dcore=0):
    return lambda x, y, z, core: (x ^ dx, y ^ dy, z ^ dz, core ^ dcore)


def swap_with(value, move):
    pairs = [(index, index_of(*move(*place_of(index)))) for index in range(128)]
    return lax.ppermute(value, AXES, pairs)


STEPS = (
    ({"dy": 3}, {"dz": 1}),
    ({"dz": 1}, {"dz": 3}),
    ({"dz": 3}, {"dy": 3}),
)


def step_move(step):
    first, second = across(**STEPS[step][0]), across(**STEPS[step][1])
    return lambda x, y, z, core: (second if core else first)(x, y, z, core)


def slice_of(piece, other):
    tm = lax.axis_index("tmpl")
    y_hi, z, core = tm // 8, (tm // 2) % 4, (tm % 2) ^ other
    change = []
    for which in range(2):
        dy = dz = 0
        for step in range(3):
            if piece >> step & 1:
                dy ^= STEPS[step][which].get("dy", 0) // 2
                dz ^= STEPS[step][which].get("dz", 0)
        change.append((dy, dz))
    dy = jnp.where(core == 0, change[0][0], change[1][0])
    dz = jnp.where(core == 0, change[0][1], change[1][1])
    return (y_hi ^ dy) * 8 + (z ^ dz) * 2 + core


def segment_at(place):
    return ((lax.axis_index("dt") // 2) ^ (place & 3)) * 2 + (place >> 2)


def circle(turns):
    turns = turns + NFFT // 8
    quarter = (turns >> 18) & 3
    rest = (turns & (NFFT // 4 - 1)) - NFFT // 8
    angle = rest.astype(jnp.float32) * jnp.float32(TWO_PI / NFFT)
    square = angle * angle
    cosine = 1.0 + square * (-1 / 2 + square * (1 / 24 + square * (-1 / 720 + square * (1 / 40320))))
    sine = angle * (1.0 + square * (-1 / 6 + square * (1 / 120 + square * (-1 / 5040 + square * (1 / 362880)))))
    odd = (quarter & 1) == 1
    real, imag = jnp.where(odd, -sine, cosine), jnp.where(odd, cosine, sine)
    return jnp.where(quarter >= 2, -real, real), jnp.where(quarter >= 2, -imag, imag)


def counted(shape, axis):
    return lax.broadcasted_iota(jnp.int32, shape, axis)


def tables_kernel(small_ref, bin_ref, turned_ref, table_ref, turn_ref, *refs):
    binned, (now_ref,) = refs[:SLOTS], refs[SLOTS:]
    for ref in binned:
        ref[...] = jnp.zeros_like(ref)

    cosine, sine = circle(counted((FB, TW), 0) * counted((FB, TW), 1) * STRIDE)
    table_ref[:FB, :TW] = cosine.astype(jnp.bfloat16)
    table_ref[:FB, TW:] = sine.astype(jnp.bfloat16)
    table_ref[FB:, :TW] = (-sine).astype(jnp.bfloat16)
    table_ref[FB:, TW:] = cosine.astype(jnp.bfloat16)
    shape = (NSL, 8, TW)
    number = FLOW // FB + counted(shape, 0) * JS + counted(shape, 1)
    turn_ref[0], turn_ref[1] = circle(number * counted(shape, 2) * FB)

    place = counted((ROWS, LANES), 0) & (SEGS - 1)
    here = segment_at(place) == counted((ROWS, LANES), 1)
    spread = [jnp.broadcast_to(small_ref[SLOTS + d:SLOTS + d + 1, :], (SEGS, LANES)) for d in range(NDET)]
    held = jnp.where(here, jnp.concatenate(spread, axis=0), 0).astype(jnp.float32)
    first = MARGIN + jnp.sum(held, axis=1, keepdims=True).astype(jnp.int32)
    now_ref[0], now_ref[1] = circle(first * (FLOW + counted((1, FB), 1)) * STRIDE)
    pc, ps = circle(jnp.broadcast_to(first * FB, (ROWS, TW)))
    pc, ps = jnp.concatenate([pc, pc], axis=1), jnp.concatenate([ps, ps], axis=1)

    def one_block(j, carry):
        rc, rs = now_ref[0], now_ref[1]
        turned_ref[j, 0] = rc
        turned_ref[j, 1] = rs
        now_ref[0] = rc * pc - rs * ps
        now_ref[1] = rc * ps + rs * pc
        return carry

    lax.fori_loop(0, NBLK, one_block, 0)

    lane = counted((SLOTS, LANES), 1)
    bin_of = jnp.zeros((SLOTS, LANES), jnp.int32)
    for e in range(NBIN - 1):
        bin_of = bin_of + (small_ref[:SLOTS, e:e + 1] <= lane).astype(jnp.int32)
    digit = counted((LANES, LANES), 0) - JS * counted((LANES, LANES), 1)
    held = (digit >= 0) & (digit < JS)
    weight = jnp.where(held, 1 << (4 * jnp.where(held, digit, 0)), 0).astype(jnp.float32)
    digits = bin_of.astype(jnp.float32).astype(jnp.bfloat16)
    bin_ref[...] = jnp.dot(digits, weight.astype(jnp.bfloat16), preferred_element_type=jnp.float32)


def templates_kernel(templ_ref, small_ref, wide_ref, spread_ref, stat_ref):
    stat_ref[...] = jnp.zeros_like(stat_ref)
    block = counted((NBLK, LANES), 0)
    at_lane = counted((1, LANES), 1)
    live_count = small_ref[SLOTS + NDET:SLOTS + NDET + 1, :]
    for k in range(SLOTS):
        h = templ_ref[k, 0].astype(jnp.float32)
        i = templ_ref[k, 1].astype(jnp.float32)
        wide_ref[k, 0] = h
        wide_ref[k, 1] = h + i
        wide_ref[k, 2] = h - i
        power = jnp.sum(h * h + i * i, axis=1, keepdims=True)
        upper = small_ref[k:k + 1, :]
        lower = jnp.where(at_lane == 0, 0, pltpu.roll(upper, 1, 1))
        inside = jnp.where((block >= lower) & (block < upper), power, 0.0)
        in_bins = jnp.sum(inside, axis=0, keepdims=True)
        sigma2 = jnp.sum(power, axis=0, keepdims=True) + EPSILON
        frac = (in_bins + EPSILON) / sigma2
        inv = pltpu.roll(1.0 / (frac * sigma2), NBIN, 1)
        live = (k < live_count).astype(jnp.float32)
        row = jnp.where(at_lane == 2 * NBIN, 0.5 / sigma2, live)
        row = jnp.where(at_lane < 2 * NBIN, inv, row)
        stat_ref[k:k + 1, :] = jnp.where(at_lane < NBIN, frac, row)
    columns = stat_ref[...].T
    for k in range(SLOTS):
        spread_ref[k] = jnp.broadcast_to(columns[:SPREAD, k:k + 1], (SPREAD, LANES))


def whole():
    return pl.BlockSpec(memory_space=pltpu.VMEM)


BINNED = [jax.ShapeDtypeStruct((NBIN, ROWS, 2 * TW), jnp.float32)] * SLOTS


def small_numbers(edges, live_count, shifts):
    return jnp.concatenate([
        jnp.pad(edges, ((0, 0), (0, LANES - NBIN + 1)), constant_values=NBLK),
        jnp.pad(shifts.T, ((0, 0), (0, LANES - SEGS))),
        jnp.broadcast_to(live_count, (1, LANES)),
    ], axis=0)


def prepare_tables(small):
    outs = pl.pallas_call(
        tables_kernel,
        out_shape=[
            jax.ShapeDtypeStruct((SLOTS, LANES), jnp.float32),
            jax.ShapeDtypeStruct((NBLK, 2, ROWS, FB), jnp.float32),
            jax.ShapeDtypeStruct((2 * FB, 2 * TW), jnp.bfloat16),
            jax.ShapeDtypeStruct((2, NSL, 8, TW), jnp.float32),
        ] + BINNED,
        in_specs=[whole()],
        out_specs=[whole()] * (4 + SLOTS),
        scratch_shapes=[pltpu.VMEM((2, ROWS, FB), jnp.float32)],
        compiler_params=pltpu.CompilerParams(vmem_limit_bytes=VMEM),
        cost_estimate=pl.CostEstimate(flops=10**6, bytes_accessed=10**6, transcendentals=0),
        name="prepare_tables",
    )(small)
    return outs[:4], outs[4:]


def prepare_templates(templates, small):
    return pl.pallas_call(
        templates_kernel,
        out_shape=[
            jax.ShapeDtypeStruct((SLOTS, 3, NBLK, FB), jnp.float32),
            jax.ShapeDtypeStruct((SLOTS, SPREAD, LANES), jnp.float32),
        ],
        in_specs=[whole()] * 2,
        out_specs=[whole()] * 2,
        scratch_shapes=[pltpu.VMEM((LANES, LANES), jnp.float32)],
        compiler_params=pltpu.CompilerParams(vmem_limit_bytes=VMEM),
        cost_estimate=pl.CostEstimate(flops=10**6, bytes_accessed=10**6, transcendentals=0),
        name="prepare_templates",
    )(templates, small)


def bins_kernel(parts, last, *refs):
    count = len(parts)
    pieces, refs = refs[:count], refs[count:]
    bin_ref, table_ref, turn_ref, wide_ref, turned_ref = refs[:5]
    refs = refs[5:]
    if last:
        stat_ref, refs = refs[0], refs[1:]
    refs = refs[SLOTS:]
    binned, refs = refs[:SLOTS], refs[SLOTS:]
    if last:
        out_ref, refs = refs[0], refs[1:]
    prod_ref = refs[0]
    if last:
        best_ref = refs[1]

    def product(piece_ref, which, c, jj):
        j = c * JS + jj
        both = piece_ref[which, jj].astype(jnp.float32)
        raw_r, raw_i = both[:ROWS], both[ROWS:]
        rc, rs = turned_ref[j, 0], turned_ref[j, 1]
        sr = raw_r * rc - raw_i * rs
        si = raw_r * rs + raw_i * rc
        su = sr + si
        for pair in range(SLOTS // 2):
            real, imag = [], []
            for k in (2 * pair, 2 * pair + 1):
                h = wide_ref[k, 0, pl.ds(j, 1), :]
                v = wide_ref[k, 1, pl.ds(j, 1), :]
                w = wide_ref[k, 2, pl.ds(j, 1), :]
                k1 = h * su
                real.append(k1 - si * w)
                imag.append(k1 - sr * v)
            base = jj * SLOTS * ROWS + 2 * ROWS * pair
            rows = slice(base, base + 2 * ROWS)
            prod_ref[rows, :FB] = jnp.concatenate(real, axis=0).astype(jnp.bfloat16)
            prod_ref[rows, FB:] = jnp.concatenate(imag, axis=0).astype(jnp.bfloat16)

    def post(c, jj, digits, series):
        cos = turn_ref[0, c, jj:jj + 1, :]
        sin = turn_ref[1, c, jj:jj + 1, :]
        for k in range(SLOTS):
            b = (digits[k] >> (4 * jj)) & (NBIN - 1)
            re = series[k * ROWS:(k + 1) * ROWS, :TW]
            im = series[k * ROWS:(k + 1) * ROWS, TW:]
            binned[k][b, :, :TW] += cos * re - sin * im
            binned[k][b, :, TW:] += cos * im + sin * re

    for piece_ref, (first, amount, other) in zip(pieces, parts):
        for which in range(amount):
            c = slice_of(first + which, other)
            slot_lane = lax.broadcasted_iota(jnp.int32, (SLOTS, LANES), 1)
            packed = jnp.sum(jnp.where(slot_lane == c, bin_ref[...], 0.0), axis=1, keepdims=True).astype(jnp.int32)
            digits = [packed[k, 0] for k in range(SLOTS)]
            for jj in range(JS):
                product(piece_ref, which, c, jj)
            half = JS // 2
            size = half * SLOTS * ROWS
            for h in range(2):
                series = jnp.dot(
                    prod_ref[h * size:(h + 1) * size], table_ref[...], preferred_element_type=jnp.float32
                )
                for m in range(half):
                    post(c, h * half + m, digits, series[m * SLOTS * ROWS:(m + 1) * SLOTS * ROWS])

    if last:
        best = jnp.zeros((SEGS, TW), jnp.float32)
        for k in range(SLOTS):
            total = binned[k][0]
            for b in range(1, NBIN):
                total = total + binned[k][b]
            chi = jnp.zeros((ROWS, TW), jnp.float32)
            for b in range(NBIN):
                share = jnp.concatenate([stat_ref[k, b:b + 1, :]] * 2, axis=1)
                gap = binned[k][b] - share * total
                gap = gap * gap
                chi = chi + (gap[:, :TW] + gap[:, TW:]) * stat_ref[k, NBIN + b:NBIN + b + 1, :]
            power = total * total
            snr2 = (power[:, :TW] + power[:, TW:]) * stat_ref[k, 2 * NBIN:2 * NBIN + 1, :]
            reduced = chi / (2.0 * NBIN - 2.0)
            cube = (1.0 + reduced * reduced * reduced) * 0.5
            factor = jnp.where(reduced > 1.0, jnp.exp(jnp.log(cube) * (-1.0 / 3.0)), 1.0)
            new2 = snr2 * factor
            net2 = new2[:SEGS] + new2[SEGS:2 * SEGS] + new2[2 * SEGS:]
            best = jnp.where(stat_ref[k, 2 * NBIN + 1:2 * NBIN + 2, :] > 0.5, jnp.maximum(best, net2), best)
        best = jnp.sqrt(best)
        best_ref[...] = jnp.concatenate(
            [jnp.max(best[:, w * WIN:(w + 1) * WIN], axis=1, keepdims=True) for w in range(NWIN)], axis=1
        )
        for place in range(SEGS):
            out_ref[pl.ds(segment_at(place), 1), :] = best_ref[place:place + 1, :]


def add_bins(pieces, parts, shared, binned, stat=None):
    last = stat is not None
    operands = [*pieces, *shared] + ([stat] if last else []) + list(binned)
    first = len(operands) - SLOTS
    out_shape = list(BINNED)
    scratch = [
        pltpu.VMEM((JS * SLOTS * ROWS, 2 * FB), jnp.bfloat16),
    ]
    if last:
        out_shape.append(jax.ShapeDtypeStruct((SEGS, NWIN), jnp.float32))
        scratch.append(pltpu.VMEM((SEGS, NWIN), jnp.float32))
    flops = sum(part[1] for part in parts) * 2 * JS * SLOTS * ROWS * 2 * FB * 2 * TW
    return pl.pallas_call(
        functools.partial(bins_kernel, parts, last),
        out_shape=out_shape,
        in_specs=[whole()] * len(operands),
        out_specs=[whole()] * len(out_shape),
        scratch_shapes=scratch,
        input_output_aliases={first + k: k for k in range(SLOTS)},
        compiler_params=pltpu.CompilerParams(vmem_limit_bytes=VMEM),
        cost_estimate=pl.CostEstimate(flops=2 * flops, bytes_accessed=10**6, transcendentals=0),
        name="last_bins" if last else "add_bins",
    )(*operands)


def per_device(strain, templates, live_count, chi_edges, shifts):
    small = small_numbers(chi_edges, live_count, shifts)
    (bin_of, turned, table, turn), binned = prepare_tables(small)
    wide, stat = prepare_templates(templates, small)

    shard, even = lax.optimization_barrier((strain[0], lax.axis_index("dt") % 2 == 0))
    x = jnp.transpose(shard, (2, 1, 0, 3)).reshape(JS, 2 * NDET, 1, FB)
    got = {0: x}
    for dx in (2, 3, 1):
        got[dx] = swap_with(x, across(dx=dx))
    x = jnp.concatenate([got[dx] for dx in range(4)], axis=2)
    x, turned = lax.optimization_barrier((x, turned))
    got = swap_with(x, across(dy=1))
    x, got, wide = lax.optimization_barrier((x, got, wide))
    x = jnp.concatenate([jnp.where(even, x, got), jnp.where(even, got, x)], axis=2)
    shared = (bin_of, table, turn, wide, turned)

    def to_core(piece):
        return swap_with(piece, across(dcore=1))

    def after(value, binned):
        value, first = lax.optimization_barrier((value, binned[0]))
        return value, [first, *binned[1:]]

    p0 = x.reshape(1, JS, 2 * ROWS, FB)
    q0 = to_core(p0)
    p1 = swap_with(p0, step_move(0))
    p2 = swap_with(p0, step_move(1))
    binned = add_bins((p0, q0), ((0, 1, 0), (0, 1, 1)), shared, binned)
    (p1, p2), binned = after((p1, p2), binned)
    q1, q2 = to_core(p1), to_core(p2)
    p3 = swap_with(p1, step_move(1))
    p45 = swap_with(jnp.concatenate([p0, p1], axis=0), step_move(2))
    binned = add_bins((p1, q1), ((1, 1, 0), (1, 1, 1)), shared, binned)
    binned = add_bins((p2, q2), ((2, 1, 0), (2, 1, 1)), shared, binned)
    (p3, p45), binned = after((p3, p45), binned)
    p67 = swap_with(jnp.concatenate([p2, p3], axis=0), step_move(2))
    q3, q45 = to_core(p3), to_core(p45)
    binned = add_bins((p3, q3), ((3, 1, 0), (3, 1, 1)), shared, binned)
    binned = add_bins((p45, q45), ((4, 2, 0), (4, 2, 1)), shared, binned)
    p67, binned = after(p67, binned)
    q67 = to_core(p67)
    binned = add_bins((p67,), ((6, 2, 0),), shared, binned)
    best = add_bins((q67,), ((6, 2, 1),), shared, binned, stat)[-1]
    for move in (across(dcore=1), across(dz=1), across(dz=3), across(dy=2)):
        best = jnp.maximum(best, swap_with(best, move))
    return best[:, None, :]


def solution(mesh):
    in_specs = (
        P("dt", None, None, "tmpl", None),
        P(("dt", "tmpl"), None, None, None),
        P("dt", "tmpl"),
        P(("dt", "tmpl"), None),
        P(),
    )
    out_specs = P(None, "dt", None)
    return jax.shard_map(
        per_device, mesh=mesh, in_specs=in_specs, out_specs=out_specs, check_vma=False
    )
```

```python
import functools
import math

import jax
import jax.numpy as jnp
from jax import lax
from jax.experimental import pallas as pl
from jax.experimental.pallas import tpu as pltpu
from jax.sharding import PartitionSpec as P

FB = 256
NBLK = 96
NFFT = 1048576
FLOW = 5120
STRIDE = 4097
NBIN = 16
TW = 128
MARGIN = 64
WIN = 16
LANES = 128
SPREAD = 40
NWIN = TW // WIN
NDET = 3
SEGS = 8
SLOTS = 12
NSL = 16
JS = NBLK // NSL
ROWS = NDET * SEGS
EPSILON = 1e-05
TWO_PI = 2.0 * math.pi
AXES = ("dt", "tmpl")
VMEM = 16 * 1024 * 1024


def place_of(index):
    dt, tm = divmod(index, 16)
    return (dt // 2, (tm // 8) * 2 + dt % 2, (tm // 2) % 4, tm % 2)


def index_of(x, y, z, core):
    return (x * 2 + y % 2) * 16 + (y // 2) * 8 + z * 2 + core


def across(dx=0, dy=0, dz=0, dcore=0):
    return lambda x, y, z, core: (x ^ dx, y ^ dy, z ^ dz, core ^ dcore)


def swap_with(value, move):
    pairs = [(index, index_of(*move(*place_of(index)))) for index in range(128)]
    return lax.ppermute(value, AXES, pairs)


STEPS = (
    ({"dy": 3}, {"dz": 1}),
    ({"dz": 1}, {"dz": 3}),
    ({"dz": 3}, {"dy": 3}),
)


def step_move(step):
    first, second = across(**STEPS[step][0]), across(**STEPS[step][1])
    return lambda x, y, z, core: (second if core else first)(x, y, z, core)


def slice_of(piece, other):
    tm = lax.axis_index("tmpl")
    y_hi, z, core = tm // 8, (tm // 2) % 4, (tm % 2) ^ other
    change = []
    for which in range(2):
        dy = dz = 0
        for step in range(3):
            if piece >> step & 1:
                dy ^= STEPS[step][which].get("dy", 0) // 2
                dz ^= STEPS[step][which].get("dz", 0)
        change.append((dy, dz))
    dy = jnp.where(core == 0, change[0][0], change[1][0])
    dz = jnp.where(core == 0, change[0][1], change[1][1])
    return (y_hi ^ dy) * 8 + (z ^ dz) * 2 + core


def segment_at(place):
    return ((lax.axis_index("dt") // 2) ^ (place & 3)) * 2 + (place >> 2)


def circle(turns):
    turns = turns + NFFT // 8
    quarter = (turns >> 18) & 3
    rest = (turns & (NFFT // 4 - 1)) - NFFT // 8
    angle = rest.astype(jnp.float32) * jnp.float32(TWO_PI / NFFT)
    square = angle * angle
    cosine = 1.0 + square * (-1 / 2 + square * (1 / 24 + square * (-1 / 720 + square * (1 / 40320))))
    sine = angle * (1.0 + square * (-1 / 6 + square * (1 / 120 + square * (-1 / 5040 + square * (1 / 362880)))))
    odd = (quarter & 1) == 1
    real, imag = jnp.where(odd, -sine, cosine), jnp.where(odd, cosine, sine)
    return jnp.where(quarter >= 2, -real, real), jnp.where(quarter >= 2, -imag, imag)


def counted(shape, axis):
    return lax.broadcasted_iota(jnp.int32, shape, axis)


def tables_kernel(small_ref, bin_ref, turned_ref, table_ref, turn_ref, *refs):
    binned, (now_ref,) = refs[:SLOTS], refs[SLOTS:]
    for ref in binned:
        ref[...] = jnp.zeros_like(ref)

    cosine, sine = circle(counted((FB, TW), 0) * counted((FB, TW), 1) * STRIDE)
    table_ref[:FB, :TW] = cosine.astype(jnp.bfloat16)
    table_ref[:FB, TW:] = sine.astype(jnp.bfloat16)
    table_ref[FB:, :TW] = (-sine).astype(jnp.bfloat16)
    table_ref[FB:, TW:] = cosine.astype(jnp.bfloat16)
    shape = (NSL, 8, TW)
    number = FLOW // FB + counted(shape, 0) * JS + counted(shape, 1)
    turn_ref[0], turn_ref[1] = circle(number * counted(shape, 2) * FB)

    place = counted((ROWS, LANES), 0) & (SEGS - 1)
    here = segment_at(place) == counted((ROWS, LANES), 1)
    spread = [jnp.broadcast_to(small_ref[SLOTS + d:SLOTS + d + 1, :], (SEGS, LANES)) for d in range(NDET)]
    held = jnp.where(here, jnp.concatenate(spread, axis=0), 0).astype(jnp.float32)
    first = MARGIN + jnp.sum(held, axis=1, keepdims=True).astype(jnp.int32)
    now_ref[0], now_ref[1] = circle(first * (FLOW + counted((1, FB), 1)) * STRIDE)
    pc, ps = circle(jnp.broadcast_to(first * FB, (ROWS, TW)))
    pc, ps = jnp.concatenate([pc, pc], axis=1), jnp.concatenate([ps, ps], axis=1)

    def one_block(j, carry):
        rc, rs = now_ref[0], now_ref[1]
        turned_ref[j, 0] = rc
        turned_ref[j, 1] = rs
        now_ref[0] = rc * pc - rs * ps
        now_ref[1] = rc * ps + rs * pc
        return carry

    lax.fori_loop(0, NBLK, one_block, 0)

    lane = counted((SLOTS, LANES), 1)
    bin_of = jnp.zeros((SLOTS, LANES), jnp.int32)
    for e in range(NBIN - 1):
        bin_of = bin_of + (small_ref[:SLOTS, e:e + 1] <= lane).astype(jnp.int32)
    digit = counted((LANES, LANES), 0) - JS * counted((LANES, LANES), 1)
    held = (digit >= 0) & (digit < JS)
    weight = jnp.where(held, 1 << (4 * jnp.where(held, digit, 0)), 0).astype(jnp.float32)
    digits = bin_of.astype(jnp.float32).astype(jnp.bfloat16)
    bin_ref[...] = jnp.dot(digits, weight.astype(jnp.bfloat16), preferred_element_type=jnp.float32)


def templates_kernel(templ_ref, small_ref, wide_ref, spread_ref, stat_ref):
    stat_ref[...] = jnp.zeros_like(stat_ref)
    block = counted((NBLK, LANES), 0)
    at_lane = counted((1, LANES), 1)
    live_count = small_ref[SLOTS + NDET:SLOTS + NDET + 1, :]
    for k in range(SLOTS):
        h = templ_ref[k, 0].astype(jnp.float32)
        i = templ_ref[k, 1].astype(jnp.float32)
        wide_ref[k, 0] = h
        wide_ref[k, 1] = h + i
        wide_ref[k, 2] = h - i
        power = jnp.sum(h * h + i * i, axis=1, keepdims=True)
        upper = small_ref[k:k + 1, :]
        lower = jnp.where(at_lane == 0, 0, pltpu.roll(upper, 1, 1))
        inside = jnp.where((block >= lower) & (block < upper), power, 0.0)
        in_bins = jnp.sum(inside, axis=0, keepdims=True)
        sigma2 = jnp.sum(power, axis=0, keepdims=True) + EPSILON
        frac = (in_bins + EPSILON) / sigma2
        inv = pltpu.roll(1.0 / (frac * sigma2), NBIN, 1)
        live = (k < live_count).astype(jnp.float32)
        row = jnp.where(at_lane == 2 * NBIN, 0.5 / sigma2, live)
        row = jnp.where(at_lane < 2 * NBIN, inv, row)
        stat_ref[k:k + 1, :] = jnp.where(at_lane < NBIN, frac, row)
    columns = stat_ref[...].T
    for k in range(SLOTS):
        spread_ref[k] = jnp.broadcast_to(columns[:SPREAD, k:k + 1], (SPREAD, LANES))


def whole():
    return pl.BlockSpec(memory_space=pltpu.VMEM)


BINNED = [jax.ShapeDtypeStruct((NBIN, ROWS, 2 * TW), jnp.float32)] * SLOTS


def small_numbers(edges, live_count, shifts):
    return jnp.concatenate([
        jnp.pad(edges, ((0, 0), (0, LANES - NBIN + 1)), constant_values=NBLK),
        jnp.pad(shifts.T, ((0, 0), (0, LANES - SEGS))),
        jnp.broadcast_to(live_count, (1, LANES)),
    ], axis=0)


def prepare_tables(small):
    outs = pl.pallas_call(
        tables_kernel,
        out_shape=[
            jax.ShapeDtypeStruct((SLOTS, LANES), jnp.float32),
            jax.ShapeDtypeStruct((NBLK, 2, ROWS, FB), jnp.float32),
            jax.ShapeDtypeStruct((2 * FB, 2 * TW), jnp.bfloat16),
            jax.ShapeDtypeStruct((2, NSL, 8, TW), jnp.float32),
        ] + BINNED,
        in_specs=[whole()],
        out_specs=[whole()] * (4 + SLOTS),
        scratch_shapes=[pltpu.VMEM((2, ROWS, FB), jnp.float32)],
        compiler_params=pltpu.CompilerParams(vmem_limit_bytes=VMEM),
        cost_estimate=pl.CostEstimate(flops=10**6, bytes_accessed=10**6, transcendentals=0),
        name="prepare_tables",
    )(small)
    return outs[:4], outs[4:]


def prepare_templates(templates, small):
    return pl.pallas_call(
        templates_kernel,
        out_shape=[
            jax.ShapeDtypeStruct((SLOTS, 3, NBLK, FB), jnp.float32),
            jax.ShapeDtypeStruct((SLOTS, SPREAD, LANES), jnp.float32),
        ],
        in_specs=[whole()] * 2,
        out_specs=[whole()] * 2,
        scratch_shapes=[pltpu.VMEM((LANES, LANES), jnp.float32)],
        compiler_params=pltpu.CompilerParams(vmem_limit_bytes=VMEM),
        cost_estimate=pl.CostEstimate(flops=10**6, bytes_accessed=10**6, transcendentals=0),
        name="prepare_templates",
    )(templates, small)


def bins_kernel(parts, last, *refs):
    count = len(parts)
    pieces, refs = refs[:count], refs[count:]
    bin_ref, table_ref, turn_ref, wide_ref, turned_ref = refs[:5]
    refs = refs[5:]
    if last:
        stat_ref, refs = refs[0], refs[1:]
    refs = refs[SLOTS:]
    binned, refs = refs[:SLOTS], refs[SLOTS:]
    if last:
        out_ref, refs = refs[0], refs[1:]
    prod_ref = refs[0]
    if last:
        best_ref = refs[1]

    def product(piece_ref, which, c, jj):
        j = c * JS + jj
        both = piece_ref[which, jj].astype(jnp.float32)
        raw_r, raw_i = both[:ROWS], both[ROWS:]
        rc, rs = turned_ref[j, 0], turned_ref[j, 1]
        sr = raw_r * rc - raw_i * rs
        si = raw_r * rs + raw_i * rc
        su = sr + si
        for pair in range(SLOTS // 2):
            real, imag = [], []
            for k in (2 * pair, 2 * pair + 1):
                h = wide_ref[k, 0, pl.ds(j, 1), :]
                v = wide_ref[k, 1, pl.ds(j, 1), :]
                w = wide_ref[k, 2, pl.ds(j, 1), :]
                k1 = h * su
                real.append(k1 - si * w)
                imag.append(k1 - sr * v)
            base = jj * SLOTS * ROWS + 2 * ROWS * pair
            rows = slice(base, base + 2 * ROWS)
            prod_ref[rows, :FB] = jnp.concatenate(real, axis=0).astype(jnp.bfloat16)
            prod_ref[rows, FB:] = jnp.concatenate(imag, axis=0).astype(jnp.bfloat16)

    def post(c, jj, digits, series):
        cos = turn_ref[0, c, jj:jj + 1, :]
        sin = turn_ref[1, c, jj:jj + 1, :]
        for k in range(SLOTS):
            b = (digits[k] >> (4 * jj)) & (NBIN - 1)
            re = series[k * ROWS:(k + 1) * ROWS, :TW]
            im = series[k * ROWS:(k + 1) * ROWS, TW:]
            binned[k][b, :, :TW] += cos * re - sin * im
            binned[k][b, :, TW:] += cos * im + sin * re

    for piece_ref, (first, amount, other, held) in zip(pieces, parts):
        for which in range(amount):
            c = slice_of(first + which, other)
            slot_lane = lax.broadcasted_iota(jnp.int32, (SLOTS, LANES), 1)
            packed = jnp.sum(jnp.where(slot_lane == c, bin_ref[...], 0.0), axis=1, keepdims=True).astype(jnp.int32)
            digits = [packed[k, 0] for k in range(SLOTS)]
            for jj in range(JS):
                product(piece_ref, held + which, c, jj)
            half = JS // 2
            size = half * SLOTS * ROWS
            for h in range(2):
                series = jnp.dot(
                    prod_ref[h * size:(h + 1) * size], table_ref[...], preferred_element_type=jnp.float32
                )
                for m in range(half):
                    post(c, h * half + m, digits, series[m * SLOTS * ROWS:(m + 1) * SLOTS * ROWS])

    if last:
        best = jnp.zeros((SEGS, TW), jnp.float32)
        for k in range(SLOTS):
            total = binned[k][0]
            for b in range(1, NBIN):
                total = total + binned[k][b]
            chi = jnp.zeros((ROWS, TW), jnp.float32)
            for b in range(NBIN):
                share = jnp.concatenate([stat_ref[k, b:b + 1, :]] * 2, axis=1)
                gap = binned[k][b] - share * total
                gap = gap * gap
                chi = chi + (gap[:, :TW] + gap[:, TW:]) * stat_ref[k, NBIN + b:NBIN + b + 1, :]
            power = total * total
            snr2 = (power[:, :TW] + power[:, TW:]) * stat_ref[k, 2 * NBIN:2 * NBIN + 1, :]
            reduced = chi / (2.0 * NBIN - 2.0)
            cube = (1.0 + reduced * reduced * reduced) * 0.5
            factor = jnp.where(reduced > 1.0, jnp.exp(jnp.log(cube) * (-1.0 / 3.0)), 1.0)
            new2 = snr2 * factor
            net2 = new2[:SEGS] + new2[SEGS:2 * SEGS] + new2[2 * SEGS:]
            best = jnp.where(stat_ref[k, 2 * NBIN + 1:2 * NBIN + 2, :] > 0.5, jnp.maximum(best, net2), best)
        best = jnp.sqrt(best)
        best_ref[...] = jnp.concatenate(
            [jnp.max(best[:, w * WIN:(w + 1) * WIN], axis=1, keepdims=True) for w in range(NWIN)], axis=1
        )
        for place in range(SEGS):
            out_ref[pl.ds(segment_at(place), 1), :] = best_ref[place:place + 1, :]


def add_bins(pieces, parts, shared, binned, stat=None):
    last = stat is not None
    operands = [*pieces, *shared] + ([stat] if last else []) + list(binned)
    first = len(operands) - SLOTS
    out_shape = list(BINNED)
    scratch = [
        pltpu.VMEM((JS * SLOTS * ROWS, 2 * FB), jnp.bfloat16),
    ]
    if last:
        out_shape.append(jax.ShapeDtypeStruct((SEGS, NWIN), jnp.float32))
        scratch.append(pltpu.VMEM((SEGS, NWIN), jnp.float32))
    flops = sum(part[1] for part in parts) * 2 * JS * SLOTS * ROWS * 2 * FB * 2 * TW
    return pl.pallas_call(
        functools.partial(bins_kernel, parts, last),
        out_shape=out_shape,
        in_specs=[whole()] * len(operands),
        out_specs=[whole()] * len(out_shape),
        scratch_shapes=scratch,
        input_output_aliases={first + k: k for k in range(SLOTS)},
        compiler_params=pltpu.CompilerParams(vmem_limit_bytes=VMEM),
        cost_estimate=pl.CostEstimate(flops=2 * flops, bytes_accessed=10**6, transcendentals=0),
        name="last_bins" if last else "add_bins",
    )(*operands)


def per_device(strain, templates, live_count, chi_edges, shifts):
    small = small_numbers(chi_edges, live_count, shifts)
    (bin_of, turned, table, turn), binned = prepare_tables(small)
    wide, stat = prepare_templates(templates, small)

    shard, even = lax.optimization_barrier((strain[0], lax.axis_index("dt") % 2 == 0))
    x = jnp.transpose(shard, (2, 1, 0, 3)).reshape(JS, 2 * NDET, 1, FB)
    got = {0: x}
    for dx in (2, 3, 1):
        got[dx] = swap_with(x, across(dx=dx))
    x = jnp.concatenate([got[dx] for dx in range(4)], axis=2)
    x, turned = lax.optimization_barrier((x, turned))
    got = swap_with(x, across(dy=1))
    x, got, wide = lax.optimization_barrier((x, got, wide))
    x = jnp.concatenate([jnp.where(even, x, got), jnp.where(even, got, x)], axis=2)
    shared = (bin_of, table, turn, wide, turned)

    def to_core(piece):
        return swap_with(piece, across(dcore=1))

    def after(value, binned):
        value, first = lax.optimization_barrier((value, binned[0]))
        return value, [first, *binned[1:]]

    p0 = x.reshape(1, JS, 2 * ROWS, FB)
    q0 = to_core(p0)
    p1 = swap_with(p0, step_move(0))
    p2 = swap_with(p0, step_move(1))
    binned = add_bins((p0, q0), ((0, 1, 0, 0), (0, 1, 1, 0)), shared, binned)
    (p1, p2), binned = after((p1, p2), binned)
    p12 = jnp.concatenate([p1, p2], axis=0)
    q12 = to_core(p12)
    p3 = swap_with(p1, step_move(1))
    p456 = swap_with(jnp.concatenate([p0, p12], axis=0), step_move(2))
    binned = add_bins((p12, q12), ((1, 1, 0, 0), (1, 1, 1, 0)), shared, binned)
    p3, binned = after(p3, binned)
    q3 = to_core(p3)
    p7 = swap_with(p3, step_move(2))
    binned = add_bins((p12, q12, p3), ((2, 1, 0, 1), (2, 1, 1, 1), (3, 1, 0, 0)), shared, binned)
    (p456, p7), binned = after((p456, p7), binned)
    p4567 = jnp.concatenate([p456, p7], axis=0)
    q4567 = to_core(p4567)
    binned = add_bins((p4567,), ((4, 4, 0, 0),), shared, binned)
    best = add_bins((q3, q4567), ((3, 1, 1, 0), (4, 4, 1, 0)), shared, binned, stat)[-1]
    for move in (across(dcore=1), across(dz=1), across(dz=3), across(dy=2)):
        best = jnp.maximum(best, swap_with(best, move))
    return best[:, None, :]


def solution(mesh):
    in_specs = (
        P("dt", None, None, "tmpl", None),
        P(("dt", "tmpl"), None, None, None),
        P("dt", "tmpl"),
        P(("dt", "tmpl"), None),
        P(),
    )
    out_specs = P(None, "dt", None)
    return jax.shard_map(
        per_device, mesh=mesh, in_specs=in_specs, out_specs=out_specs, check_vma=False
    )
```

```python
import functools
import math

import jax
import jax.numpy as jnp
from jax import lax
from jax.experimental import pallas as pl
from jax.experimental.pallas import tpu as pltpu
from jax.sharding import PartitionSpec as P

FB = 256
NBLK = 96
NFFT = 1048576
FLOW = 5120
STRIDE = 4097
NBIN = 16
TW = 128
MARGIN = 64
WIN = 16
LANES = 128
SPREAD = 40
NWIN = TW // WIN
NDET = 3
SEGS = 8
SLOTS = 12
NSL = 16
JS = NBLK // NSL
ROWS = NDET * SEGS
EPSILON = 1e-05
TWO_PI = 2.0 * math.pi
AXES = ("dt", "tmpl")
VMEM = 16 * 1024 * 1024


def place_of(index):
    dt, tm = divmod(index, 16)
    return (dt // 2, (tm // 8) * 2 + dt % 2, (tm // 2) % 4, tm % 2)


def index_of(x, y, z, core):
    return (x * 2 + y % 2) * 16 + (y // 2) * 8 + z * 2 + core


def across(dx=0, dy=0, dz=0, dcore=0):
    return lambda x, y, z, core: (x ^ dx, y ^ dy, z ^ dz, core ^ dcore)


def swap_with(value, move):
    pairs = [(index, index_of(*move(*place_of(index)))) for index in range(128)]
    return lax.ppermute(value, AXES, pairs)


STEPS = (
    ({"dy": 3}, {"dz": 1}),
    ({"dz": 1}, {"dz": 3}),
    ({"dz": 3}, {"dy": 3}),
)


def step_move(step):
    first, second = across(**STEPS[step][0]), across(**STEPS[step][1])
    return lambda x, y, z, core: (second if core else first)(x, y, z, core)


def slice_of(piece, other):
    tm = lax.axis_index("tmpl")
    y_hi, z, core = tm // 8, (tm // 2) % 4, (tm % 2) ^ other
    change = []
    for which in range(2):
        dy = dz = 0
        for step in range(3):
            if piece >> step & 1:
                dy ^= STEPS[step][which].get("dy", 0) // 2
                dz ^= STEPS[step][which].get("dz", 0)
        change.append((dy, dz))
    dy = jnp.where(core == 0, change[0][0], change[1][0])
    dz = jnp.where(core == 0, change[0][1], change[1][1])
    return (y_hi ^ dy) * 8 + (z ^ dz) * 2 + core


def segment_at(place):
    return ((lax.axis_index("dt") // 2) ^ (place & 3)) * 2 + (place >> 2)


def circle(turns):
    turns = turns + NFFT // 8
    quarter = (turns >> 18) & 3
    rest = (turns & (NFFT // 4 - 1)) - NFFT // 8
    angle = rest.astype(jnp.float32) * jnp.float32(TWO_PI / NFFT)
    square = angle * angle
    cosine = 1.0 + square * (-1 / 2 + square * (1 / 24 + square * (-1 / 720 + square * (1 / 40320))))
    sine = angle * (1.0 + square * (-1 / 6 + square * (1 / 120 + square * (-1 / 5040 + square * (1 / 362880)))))
    odd = (quarter & 1) == 1
    real, imag = jnp.where(odd, -sine, cosine), jnp.where(odd, cosine, sine)
    return jnp.where(quarter >= 2, -real, real), jnp.where(quarter >= 2, -imag, imag)


def counted(shape, axis):
    return lax.broadcasted_iota(jnp.int32, shape, axis)


def tables_kernel(small_ref, bin_ref, turned_ref, table_ref, turn_ref, *refs):
    binned, (now_ref,) = refs[:SLOTS], refs[SLOTS:]
    for ref in binned:
        ref[...] = jnp.zeros_like(ref)

    cosine, sine = circle(counted((FB, TW), 0) * counted((FB, TW), 1) * STRIDE)
    table_ref[:FB, :TW] = cosine.astype(jnp.bfloat16)
    table_ref[:FB, TW:] = sine.astype(jnp.bfloat16)
    table_ref[FB:, :TW] = (-sine).astype(jnp.bfloat16)
    table_ref[FB:, TW:] = cosine.astype(jnp.bfloat16)
    shape = (NSL, 8, TW)
    number = FLOW // FB + counted(shape, 0) * JS + counted(shape, 1)
    turn_ref[0], turn_ref[1] = circle(number * counted(shape, 2) * FB)

    place = counted((ROWS, LANES), 0) & (SEGS - 1)
    here = segment_at(place) == counted((ROWS, LANES), 1)
    spread = [jnp.broadcast_to(small_ref[SLOTS + d:SLOTS + d + 1, :], (SEGS, LANES)) for d in range(NDET)]
    held = jnp.where(here, jnp.concatenate(spread, axis=0), 0).astype(jnp.float32)
    first = MARGIN + jnp.sum(held, axis=1, keepdims=True).astype(jnp.int32)
    now_ref[0], now_ref[1] = circle(first * (FLOW + counted((1, FB), 1)) * STRIDE)
    pc, ps = circle(jnp.broadcast_to(first * FB, (ROWS, TW)))
    pc, ps = jnp.concatenate([pc, pc], axis=1), jnp.concatenate([ps, ps], axis=1)

    def one_block(j, carry):
        rc, rs = now_ref[0], now_ref[1]
        turned_ref[j, 0] = rc
        turned_ref[j, 1] = rs
        now_ref[0] = rc * pc - rs * ps
        now_ref[1] = rc * ps + rs * pc
        return carry

    lax.fori_loop(0, NBLK, one_block, 0)

    lane = counted((SLOTS, LANES), 1)
    bin_of = jnp.zeros((SLOTS, LANES), jnp.int32)
    for e in range(NBIN - 1):
        bin_of = bin_of + (small_ref[:SLOTS, e:e + 1] <= lane).astype(jnp.int32)
    digit = counted((LANES, LANES), 0) - JS * counted((LANES, LANES), 1)
    held = (digit >= 0) & (digit < JS)
    weight = jnp.where(held, 1 << (4 * jnp.where(held, digit, 0)), 0).astype(jnp.float32)
    digits = bin_of.astype(jnp.float32).astype(jnp.bfloat16)
    bin_ref[...] = jnp.dot(digits, weight.astype(jnp.bfloat16), preferred_element_type=jnp.float32)


def templates_kernel(templ_ref, small_ref, wide_ref, spread_ref, stat_ref):
    stat_ref[...] = jnp.zeros_like(stat_ref)
    block = counted((NBLK, LANES), 0)
    at_lane = counted((1, LANES), 1)
    live_count = small_ref[SLOTS + NDET:SLOTS + NDET + 1, :]
    for k in range(SLOTS):
        h = templ_ref[k, 0].astype(jnp.float32)
        i = templ_ref[k, 1].astype(jnp.float32)
        wide_ref[k, 0] = h
        wide_ref[k, 1] = h + i
        wide_ref[k, 2] = h - i
        power = jnp.sum(h * h + i * i, axis=1, keepdims=True)
        upper = small_ref[k:k + 1, :]
        lower = jnp.where(at_lane == 0, 0, pltpu.roll(upper, 1, 1))
        inside = jnp.where((block >= lower) & (block < upper), power, 0.0)
        in_bins = jnp.sum(inside, axis=0, keepdims=True)
        sigma2 = jnp.sum(power, axis=0, keepdims=True) + EPSILON
        frac = (in_bins + EPSILON) / sigma2
        inv = pltpu.roll(1.0 / (frac * sigma2), NBIN, 1)
        live = (k < live_count).astype(jnp.float32)
        row = jnp.where(at_lane == 2 * NBIN, 0.5 / sigma2, live)
        row = jnp.where(at_lane < 2 * NBIN, inv, row)
        stat_ref[k:k + 1, :] = jnp.where(at_lane < NBIN, frac, row)
    columns = stat_ref[...].T
    for k in range(SLOTS):
        spread_ref[k] = jnp.broadcast_to(columns[:SPREAD, k:k + 1], (SPREAD, LANES))


def whole():
    return pl.BlockSpec(memory_space=pltpu.VMEM)


BINNED = [jax.ShapeDtypeStruct((NBIN, ROWS, 2 * TW), jnp.float32)] * SLOTS


def small_numbers(edges, live_count, shifts):
    return jnp.concatenate([
        jnp.pad(edges, ((0, 0), (0, LANES - NBIN + 1)), constant_values=NBLK),
        jnp.pad(shifts.T, ((0, 0), (0, LANES - SEGS))),
        jnp.broadcast_to(live_count, (1, LANES)),
    ], axis=0)


def prepare_tables(small):
    outs = pl.pallas_call(
        tables_kernel,
        out_shape=[
            jax.ShapeDtypeStruct((SLOTS, LANES), jnp.float32),
            jax.ShapeDtypeStruct((NBLK, 2, ROWS, FB), jnp.float32),
            jax.ShapeDtypeStruct((2 * FB, 2 * TW), jnp.bfloat16),
            jax.ShapeDtypeStruct((2, NSL, 8, TW), jnp.float32),
        ] + BINNED,
        in_specs=[whole()],
        out_specs=[whole()] * (4 + SLOTS),
        scratch_shapes=[pltpu.VMEM((2, ROWS, FB), jnp.float32)],
        compiler_params=pltpu.CompilerParams(vmem_limit_bytes=VMEM),
        cost_estimate=pl.CostEstimate(flops=10**6, bytes_accessed=10**6, transcendentals=0),
        name="prepare_tables",
    )(small)
    return outs[:4], outs[4:]


def prepare_templates(templates, small):
    return pl.pallas_call(
        templates_kernel,
        out_shape=[
            jax.ShapeDtypeStruct((SLOTS, 3, NBLK, FB), jnp.float32),
            jax.ShapeDtypeStruct((SLOTS, SPREAD, LANES), jnp.float32),
        ],
        in_specs=[whole()] * 2,
        out_specs=[whole()] * 2,
        scratch_shapes=[pltpu.VMEM((LANES, LANES), jnp.float32)],
        compiler_params=pltpu.CompilerParams(vmem_limit_bytes=VMEM),
        cost_estimate=pl.CostEstimate(flops=10**6, bytes_accessed=10**6, transcendentals=0),
        name="prepare_templates",
    )(templates, small)


def bins_kernel(parts, last, *refs):
    count = len(parts)
    pieces, refs = refs[:count], refs[count:]
    bin_ref, table_ref, turn_ref, wide_ref, turned_ref = refs[:5]
    refs = refs[5:]
    if last:
        stat_ref, refs = refs[0], refs[1:]
    refs = refs[SLOTS:]
    binned, refs = refs[:SLOTS], refs[SLOTS:]
    if last:
        out_ref, refs = refs[0], refs[1:]
    prod_ref = refs[0]
    if last:
        best_ref = refs[1]

    def product(piece_ref, which, c, jj):
        j = c * JS + jj
        both = piece_ref[which, jj].astype(jnp.float32)
        raw_r, raw_i = both[:ROWS], both[ROWS:]
        rc, rs = turned_ref[j, 0], turned_ref[j, 1]
        sr = raw_r * rc - raw_i * rs
        si = raw_r * rs + raw_i * rc
        su = sr + si
        for pair in range(SLOTS // 2):
            real, imag = [], []
            for k in (2 * pair, 2 * pair + 1):
                h = wide_ref[k, 0, pl.ds(j, 1), :]
                v = wide_ref[k, 1, pl.ds(j, 1), :]
                w = wide_ref[k, 2, pl.ds(j, 1), :]
                k1 = h * su
                real.append(k1 - si * w)
                imag.append(k1 - sr * v)
            base = jj * SLOTS * ROWS + 2 * ROWS * pair
            rows = slice(base, base + 2 * ROWS)
            prod_ref[rows, :FB] = jnp.concatenate(real, axis=0).astype(jnp.bfloat16)
            prod_ref[rows, FB:] = jnp.concatenate(imag, axis=0).astype(jnp.bfloat16)

    def post(c, jj, digits, series):
        cos = turn_ref[0, c, jj:jj + 1, :]
        sin = turn_ref[1, c, jj:jj + 1, :]
        for k in range(SLOTS):
            b = (digits[k] >> (4 * jj)) & (NBIN - 1)
            re = series[k * ROWS:(k + 1) * ROWS, :TW]
            im = series[k * ROWS:(k + 1) * ROWS, TW:]
            binned[k][b, :, :TW] += cos * re - sin * im
            binned[k][b, :, TW:] += cos * im + sin * re

    for piece_ref, (first, amount, other) in zip(pieces, parts):
        for which in range(amount):
            c = slice_of(first + which, other)
            slot_lane = lax.broadcasted_iota(jnp.int32, (SLOTS, LANES), 1)
            packed = jnp.sum(jnp.where(slot_lane == c, bin_ref[...], 0.0), axis=1, keepdims=True).astype(jnp.int32)
            digits = [packed[k, 0] for k in range(SLOTS)]
            for jj in range(JS):
                product(piece_ref, which, c, jj)
            half = JS // 2
            size = half * SLOTS * ROWS
            for h in range(2):
                series = jnp.dot(
                    prod_ref[h * size:(h + 1) * size], table_ref[...], preferred_element_type=jnp.float32
                )
                for m in range(half):
                    post(c, h * half + m, digits, series[m * SLOTS * ROWS:(m + 1) * SLOTS * ROWS])

    if last:
        best = jnp.zeros((SEGS, TW), jnp.float32)
        for k in range(SLOTS):
            total = binned[k][0]
            for b in range(1, NBIN):
                total = total + binned[k][b]
            chi = jnp.zeros((ROWS, TW), jnp.float32)
            for b in range(NBIN):
                share = jnp.concatenate([stat_ref[k, b:b + 1, :]] * 2, axis=1)
                gap = binned[k][b] - share * total
                gap = gap * gap
                chi = chi + (gap[:, :TW] + gap[:, TW:]) * stat_ref[k, NBIN + b:NBIN + b + 1, :]
            power = total * total
            snr2 = (power[:, :TW] + power[:, TW:]) * stat_ref[k, 2 * NBIN:2 * NBIN + 1, :]
            reduced = chi / (2.0 * NBIN - 2.0)
            cube = (1.0 + reduced * reduced * reduced) * 0.5
            factor = jnp.where(reduced > 1.0, jnp.exp(jnp.log(cube) * (-1.0 / 3.0)), 1.0)
            new2 = snr2 * factor
            net2 = new2[:SEGS] + new2[SEGS:2 * SEGS] + new2[2 * SEGS:]
            best = jnp.where(stat_ref[k, 2 * NBIN + 1:2 * NBIN + 2, :] > 0.5, jnp.maximum(best, net2), best)
        best = jnp.sqrt(best)
        best_ref[...] = jnp.concatenate(
            [jnp.max(best[:, w * WIN:(w + 1) * WIN], axis=1, keepdims=True) for w in range(NWIN)], axis=1
        )
        for place in range(SEGS):
            out_ref[pl.ds(segment_at(place), 1), :] = best_ref[place:place + 1, :]


def add_bins(pieces, parts, shared, binned, stat=None):
    last = stat is not None
    operands = [*pieces, *shared] + ([stat] if last else []) + list(binned)
    first = len(operands) - SLOTS
    out_shape = list(BINNED)
    scratch = [
        pltpu.VMEM((JS * SLOTS * ROWS, 2 * FB), jnp.bfloat16),
    ]
    if last:
        out_shape.append(jax.ShapeDtypeStruct((SEGS, NWIN), jnp.float32))
        scratch.append(pltpu.VMEM((SEGS, NWIN), jnp.float32))
    flops = sum(part[1] for part in parts) * 2 * JS * SLOTS * ROWS * 2 * FB * 2 * TW
    return pl.pallas_call(
        functools.partial(bins_kernel, parts, last),
        out_shape=out_shape,
        in_specs=[whole()] * len(operands),
        out_specs=[whole()] * len(out_shape),
        scratch_shapes=scratch,
        input_output_aliases={first + k: k for k in range(SLOTS)},
        compiler_params=pltpu.CompilerParams(vmem_limit_bytes=VMEM),
        cost_estimate=pl.CostEstimate(flops=2 * flops, bytes_accessed=10**6, transcendentals=0),
        name="last_bins" if last else "add_bins",
    )(*operands)


def per_device(strain, templates, live_count, chi_edges, shifts):
    small = small_numbers(chi_edges, live_count, shifts)
    (bin_of, turned, table, turn), binned = prepare_tables(small)
    wide, stat = prepare_templates(templates, small)

    shard, even = lax.optimization_barrier((strain[0], lax.axis_index("dt") % 2 == 0))
    x = jnp.transpose(shard, (2, 1, 0, 3)).reshape(JS, 2 * NDET, 1, FB)
    got = {0: x}
    for dx in (2, 3, 1):
        got[dx] = swap_with(x, across(dx=dx))
    x = jnp.concatenate([got[dx] for dx in range(4)], axis=2)
    x, turned = lax.optimization_barrier((x, turned))
    got = swap_with(x, across(dy=1))
    x, got, wide = lax.optimization_barrier((x, got, wide))
    x = jnp.concatenate([jnp.where(even, x, got), jnp.where(even, got, x)], axis=2)
    shared = (bin_of, table, turn, wide, turned)

    def to_core(piece):
        return swap_with(piece, across(dcore=1))

    def after(value, binned):
        value, first = lax.optimization_barrier((value, binned[0]))
        return value, [first, *binned[1:]]

    p0 = x.reshape(1, JS, 2 * ROWS, FB)
    q0 = to_core(p0)
    p1 = swap_with(p0, step_move(0))
    p2 = swap_with(p0, step_move(1))
    binned = add_bins((p0, q0), ((0, 1, 0), (0, 1, 1)), shared, binned)
    (p1, p2), binned = after((p1, p2), binned)
    p12 = jnp.concatenate([p1, p2], axis=0)
    q12 = to_core(p12)
    p3 = swap_with(p1, step_move(1))
    p45 = swap_with(jnp.concatenate([p0, p1], axis=0), step_move(2))
    binned = add_bins((p12, q12), ((1, 2, 0), (1, 2, 1)), shared, binned)
    (p3, p45), binned = after((p3, p45), binned)
    p67 = swap_with(jnp.concatenate([p2, p3], axis=0), step_move(2))
    q3, q45 = to_core(p3), to_core(p45)
    binned = add_bins((p3, q3), ((3, 1, 0), (3, 1, 1)), shared, binned)
    binned = add_bins((p45, q45), ((4, 2, 0), (4, 2, 1)), shared, binned)
    p67, binned = after(p67, binned)
    q67 = to_core(p67)
    binned = add_bins((p67,), ((6, 2, 0),), shared, binned)
    best = add_bins((q67,), ((6, 2, 1),), shared, binned, stat)[-1]
    for move in (across(dcore=1), across(dz=1), across(dz=3), across(dy=2)):
        best = jnp.maximum(best, swap_with(best, move))
    return best[:, None, :]


def solution(mesh):
    in_specs = (
        P("dt", None, None, "tmpl", None),
        P(("dt", "tmpl"), None, None, None),
        P("dt", "tmpl"),
        P(("dt", "tmpl"), None),
        P(),
    )
    out_specs = P(None, "dt", None)
    return jax.shard_map(
        per_device, mesh=mesh, in_specs=in_specs, out_specs=out_specs, check_vma=False
    )
```

```python
import functools
import math

import jax
import jax.numpy as jnp
from jax import lax
from jax.experimental import pallas as pl
from jax.experimental.pallas import tpu as pltpu
from jax.sharding import PartitionSpec as P

FB = 256
NBLK = 96
NFFT = 1048576
FLOW = 5120
STRIDE = 4097
NBIN = 16
TW = 128
MARGIN = 64
WIN = 16
LANES = 128
SPREAD = 40
NWIN = TW // WIN
NDET = 3
SEGS = 8
SLOTS = 12
NSL = 16
JS = NBLK // NSL
ROWS = NDET * SEGS
EPSILON = 1e-05
TWO_PI = 2.0 * math.pi
AXES = ("dt", "tmpl")
VMEM = 16 * 1024 * 1024


def place_of(index):
    dt, tm = divmod(index, 16)
    return (dt // 2, (tm // 8) * 2 + dt % 2, (tm // 2) % 4, tm % 2)


def index_of(x, y, z, core):
    return (x * 2 + y % 2) * 16 + (y // 2) * 8 + z * 2 + core


def across(dx=0, dy=0, dz=0, dcore=0):
    return lambda x, y, z, core: (x ^ dx, y ^ dy, z ^ dz, core ^ dcore)


def swap_with(value, move):
    pairs = [(index, index_of(*move(*place_of(index)))) for index in range(128)]
    return lax.ppermute(value, AXES, pairs)


STEPS = (
    ({"dy": 3}, {"dz": 3}),
    ({"dz": 1}, {"dz": 1}),
    ({"dz": 3}, {"dy": 3}),
)


def step_move(step):
    first, second = across(**STEPS[step][0]), across(**STEPS[step][1])
    return lambda x, y, z, core: (second if core else first)(x, y, z, core)


def slice_of(piece, other):
    tm = lax.axis_index("tmpl")
    y_hi, z, core = tm // 8, (tm // 2) % 4, (tm % 2) ^ other
    change = []
    for which in range(2):
        dy = dz = 0
        for step in range(3):
            if piece >> step & 1:
                dy ^= STEPS[step][which].get("dy", 0) // 2
                dz ^= STEPS[step][which].get("dz", 0)
        change.append((dy, dz))
    dy = jnp.where(core == 0, change[0][0], change[1][0])
    dz = jnp.where(core == 0, change[0][1], change[1][1])
    return (y_hi ^ dy) * 8 + (z ^ dz) * 2 + core


def segment_at(place):
    return ((lax.axis_index("dt") // 2) ^ (place & 3)) * 2 + (place >> 2)


def circle(turns):
    turns = turns + NFFT // 8
    quarter = (turns >> 18) & 3
    rest = (turns & (NFFT // 4 - 1)) - NFFT // 8
    angle = rest.astype(jnp.float32) * jnp.float32(TWO_PI / NFFT)
    square = angle * angle
    cosine = 1.0 + square * (-1 / 2 + square * (1 / 24 + square * (-1 / 720 + square * (1 / 40320))))
    sine = angle * (1.0 + square * (-1 / 6 + square * (1 / 120 + square * (-1 / 5040 + square * (1 / 362880)))))
    odd = (quarter & 1) == 1
    real, imag = jnp.where(odd, -sine, cosine), jnp.where(odd, cosine, sine)
    return jnp.where(quarter >= 2, -real, real), jnp.where(quarter >= 2, -imag, imag)


def counted(shape, axis):
    return lax.broadcasted_iota(jnp.int32, shape, axis)


def tables_kernel(small_ref, bin_ref, turned_ref, table_ref, turn_ref, *refs):
    binned, (now_ref,) = refs[:SLOTS], refs[SLOTS:]
    for ref in binned:
        ref[...] = jnp.zeros_like(ref)

    cosine, sine = circle(counted((FB, TW), 0) * counted((FB, TW), 1) * STRIDE)
    table_ref[:FB, :TW] = cosine.astype(jnp.bfloat16)
    table_ref[:FB, TW:] = sine.astype(jnp.bfloat16)
    table_ref[FB:, :TW] = (-sine).astype(jnp.bfloat16)
    table_ref[FB:, TW:] = cosine.astype(jnp.bfloat16)
    shape = (NSL, 8, TW)
    number = FLOW // FB + counted(shape, 0) * JS + counted(shape, 1)
    turn_ref[0], turn_ref[1] = circle(number * counted(shape, 2) * FB)

    place = counted((ROWS, LANES), 0) & (SEGS - 1)
    here = segment_at(place) == counted((ROWS, LANES), 1)
    spread = [jnp.broadcast_to(small_ref[SLOTS + d:SLOTS + d + 1, :], (SEGS, LANES)) for d in range(NDET)]
    held = jnp.where(here, jnp.concatenate(spread, axis=0), 0).astype(jnp.float32)
    first = MARGIN + jnp.sum(held, axis=1, keepdims=True).astype(jnp.int32)
    now_ref[0], now_ref[1] = circle(first * (FLOW + counted((1, FB), 1)) * STRIDE)
    pc, ps = circle(jnp.broadcast_to(first * FB, (ROWS, TW)))
    pc, ps = jnp.concatenate([pc, pc], axis=1), jnp.concatenate([ps, ps], axis=1)

    def one_block(j, carry):
        rc, rs = now_ref[0], now_ref[1]
        turned_ref[j, 0] = rc
        turned_ref[j, 1] = rs
        now_ref[0] = rc * pc - rs * ps
        now_ref[1] = rc * ps + rs * pc
        return carry

    lax.fori_loop(0, NBLK, one_block, 0)

    lane = counted((SLOTS, LANES), 1)
    bin_of = jnp.zeros((SLOTS, LANES), jnp.int32)
    for e in range(NBIN - 1):
        bin_of = bin_of + (small_ref[:SLOTS, e:e + 1] <= lane).astype(jnp.int32)
    digit = counted((LANES, LANES), 0) - JS * counted((LANES, LANES), 1)
    held = (digit >= 0) & (digit < JS)
    weight = jnp.where(held, 1 << (4 * jnp.where(held, digit, 0)), 0).astype(jnp.float32)
    digits = bin_of.astype(jnp.float32).astype(jnp.bfloat16)
    bin_ref[...] = jnp.dot(digits, weight.astype(jnp.bfloat16), preferred_element_type=jnp.float32)


def templates_kernel(templ_ref, small_ref, wide_ref, spread_ref, stat_ref):
    stat_ref[...] = jnp.zeros_like(stat_ref)
    block = counted((NBLK, LANES), 0)
    at_lane = counted((1, LANES), 1)
    live_count = small_ref[SLOTS + NDET:SLOTS + NDET + 1, :]
    for k in range(SLOTS):
        h = templ_ref[k, 0].astype(jnp.float32)
        i = templ_ref[k, 1].astype(jnp.float32)
        wide_ref[k, 0] = h
        wide_ref[k, 1] = h + i
        wide_ref[k, 2] = h - i
        power = jnp.sum(h * h + i * i, axis=1, keepdims=True)
        upper = small_ref[k:k + 1, :]
        lower = jnp.where(at_lane == 0, 0, pltpu.roll(upper, 1, 1))
        inside = jnp.where((block >= lower) & (block < upper), power, 0.0)
        in_bins = jnp.sum(inside, axis=0, keepdims=True)
        sigma2 = jnp.sum(power, axis=0, keepdims=True) + EPSILON
        frac = (in_bins + EPSILON) / sigma2
        inv = pltpu.roll(1.0 / (frac * sigma2), NBIN, 1)
        live = (k < live_count).astype(jnp.float32)
        row = jnp.where(at_lane == 2 * NBIN, 0.5 / sigma2, live)
        row = jnp.where(at_lane < 2 * NBIN, inv, row)
        stat_ref[k:k + 1, :] = jnp.where(at_lane < NBIN, frac, row)
    columns = stat_ref[...].T
    for k in range(SLOTS):
        spread_ref[k] = jnp.broadcast_to(columns[:SPREAD, k:k + 1], (SPREAD, LANES))


def whole():
    return pl.BlockSpec(memory_space=pltpu.VMEM)


BINNED = [jax.ShapeDtypeStruct((NBIN, ROWS, 2 * TW), jnp.float32)] * SLOTS


def small_numbers(edges, live_count, shifts):
    return jnp.concatenate([
        jnp.pad(edges, ((0, 0), (0, LANES - NBIN + 1)), constant_values=NBLK),
        jnp.pad(shifts.T, ((0, 0), (0, LANES - SEGS))),
        jnp.broadcast_to(live_count, (1, LANES)),
    ], axis=0)


def prepare_tables(small):
    outs = pl.pallas_call(
        tables_kernel,
        out_shape=[
            jax.ShapeDtypeStruct((SLOTS, LANES), jnp.float32),
            jax.ShapeDtypeStruct((NBLK, 2, ROWS, FB), jnp.float32),
            jax.ShapeDtypeStruct((2 * FB, 2 * TW), jnp.bfloat16),
            jax.ShapeDtypeStruct((2, NSL, 8, TW), jnp.float32),
        ] + BINNED,
        in_specs=[whole()],
        out_specs=[whole()] * (4 + SLOTS),
        scratch_shapes=[pltpu.VMEM((2, ROWS, FB), jnp.float32)],
        compiler_params=pltpu.CompilerParams(vmem_limit_bytes=VMEM),
        cost_estimate=pl.CostEstimate(flops=10**6, bytes_accessed=10**6, transcendentals=0),
        name="prepare_tables",
    )(small)
    return outs[:4], outs[4:]


def prepare_templates(templates, small):
    return pl.pallas_call(
        templates_kernel,
        out_shape=[
            jax.ShapeDtypeStruct((SLOTS, 3, NBLK, FB), jnp.float32),
            jax.ShapeDtypeStruct((SLOTS, SPREAD, LANES), jnp.float32),
        ],
        in_specs=[whole()] * 2,
        out_specs=[whole()] * 2,
        scratch_shapes=[pltpu.VMEM((LANES, LANES), jnp.float32)],
        compiler_params=pltpu.CompilerParams(vmem_limit_bytes=VMEM),
        cost_estimate=pl.CostEstimate(flops=10**6, bytes_accessed=10**6, transcendentals=0),
        name="prepare_templates",
    )(templates, small)


def bins_kernel(parts, last, *refs):
    count = len(parts)
    pieces, refs = refs[:count], refs[count:]
    bin_ref, table_ref, turn_ref, wide_ref, turned_ref = refs[:5]
    refs = refs[5:]
    if last:
        stat_ref, refs = refs[0], refs[1:]
    refs = refs[SLOTS:]
    binned, refs = refs[:SLOTS], refs[SLOTS:]
    if last:
        out_ref, refs = refs[0], refs[1:]
    prod_ref = refs[0]
    if last:
        best_ref = refs[1]

    def product(piece_ref, which, c, jj):
        j = c * JS + jj
        both = piece_ref[which, jj].astype(jnp.float32)
        raw_r, raw_i = both[:ROWS], both[ROWS:]
        rc, rs = turned_ref[j, 0], turned_ref[j, 1]
        sr = raw_r * rc - raw_i * rs
        si = raw_r * rs + raw_i * rc
        su = sr + si
        for pair in range(SLOTS // 2):
            real, imag = [], []
            for k in (2 * pair, 2 * pair + 1):
                h = wide_ref[k, 0, pl.ds(j, 1), :]
                v = wide_ref[k, 1, pl.ds(j, 1), :]
                w = wide_ref[k, 2, pl.ds(j, 1), :]
                k1 = h * su
                real.append(k1 - si * w)
                imag.append(k1 - sr * v)
            base = jj * SLOTS * ROWS + 2 * ROWS * pair
            rows = slice(base, base + 2 * ROWS)
            prod_ref[rows, :FB] = jnp.concatenate(real, axis=0).astype(jnp.bfloat16)
            prod_ref[rows, FB:] = jnp.concatenate(imag, axis=0).astype(jnp.bfloat16)

    def post(c, jj, digits, series):
        cos = turn_ref[0, c, jj:jj + 1, :]
        sin = turn_ref[1, c, jj:jj + 1, :]
        for k in range(SLOTS):
            b = (digits[k] >> (4 * jj)) & (NBIN - 1)
            re = series[k * ROWS:(k + 1) * ROWS, :TW]
            im = series[k * ROWS:(k + 1) * ROWS, TW:]
            binned[k][b, :, :TW] += cos * re - sin * im
            binned[k][b, :, TW:] += cos * im + sin * re

    for piece_ref, (first, amount, other) in zip(pieces, parts):
        for which in range(amount):
            c = slice_of(first + which, other)
            slot_lane = lax.broadcasted_iota(jnp.int32, (SLOTS, LANES), 1)
            packed = jnp.sum(jnp.where(slot_lane == c, bin_ref[...], 0.0), axis=1, keepdims=True).astype(jnp.int32)
            digits = [packed[k, 0] for k in range(SLOTS)]
            for jj in range(JS):
                product(piece_ref, which, c, jj)
            half = JS // 2
            size = half * SLOTS * ROWS
            for h in range(2):
                series = jnp.dot(
                    prod_ref[h * size:(h + 1) * size], table_ref[...], preferred_element_type=jnp.float32
                )
                for m in range(half):
                    post(c, h * half + m, digits, series[m * SLOTS * ROWS:(m + 1) * SLOTS * ROWS])

    if last:
        best = jnp.zeros((SEGS, TW), jnp.float32)
        for k in range(SLOTS):
            total = binned[k][0]
            for b in range(1, NBIN):
                total = total + binned[k][b]
            chi = jnp.zeros((ROWS, TW), jnp.float32)
            for b in range(NBIN):
                share = jnp.concatenate([stat_ref[k, b:b + 1, :]] * 2, axis=1)
                gap = binned[k][b] - share * total
                gap = gap * gap
                chi = chi + (gap[:, :TW] + gap[:, TW:]) * stat_ref[k, NBIN + b:NBIN + b + 1, :]
            power = total * total
            snr2 = (power[:, :TW] + power[:, TW:]) * stat_ref[k, 2 * NBIN:2 * NBIN + 1, :]
            reduced = chi / (2.0 * NBIN - 2.0)
            cube = (1.0 + reduced * reduced * reduced) * 0.5
            factor = jnp.where(reduced > 1.0, jnp.exp(jnp.log(cube) * (-1.0 / 3.0)), 1.0)
            new2 = snr2 * factor
            net2 = new2[:SEGS] + new2[SEGS:2 * SEGS] + new2[2 * SEGS:]
            best = jnp.where(stat_ref[k, 2 * NBIN + 1:2 * NBIN + 2, :] > 0.5, jnp.maximum(best, net2), best)
        best = jnp.sqrt(best)
        best_ref[...] = jnp.concatenate(
            [jnp.max(best[:, w * WIN:(w + 1) * WIN], axis=1, keepdims=True) for w in range(NWIN)], axis=1
        )
        for place in range(SEGS):
            out_ref[pl.ds(segment_at(place), 1), :] = best_ref[place:place + 1, :]


def add_bins(pieces, parts, shared, binned, stat=None):
    last = stat is not None
    operands = [*pieces, *shared] + ([stat] if last else []) + list(binned)
    first = len(operands) - SLOTS
    out_shape = list(BINNED)
    scratch = [
        pltpu.VMEM((JS * SLOTS * ROWS, 2 * FB), jnp.bfloat16),
    ]
    if last:
        out_shape.append(jax.ShapeDtypeStruct((SEGS, NWIN), jnp.float32))
        scratch.append(pltpu.VMEM((SEGS, NWIN), jnp.float32))
    flops = sum(part[1] for part in parts) * 2 * JS * SLOTS * ROWS * 2 * FB * 2 * TW
    return pl.pallas_call(
        functools.partial(bins_kernel, parts, last),
        out_shape=out_shape,
        in_specs=[whole()] * len(operands),
        out_specs=[whole()] * len(out_shape),
        scratch_shapes=scratch,
        input_output_aliases={first + k: k for k in range(SLOTS)},
        compiler_params=pltpu.CompilerParams(vmem_limit_bytes=VMEM),
        cost_estimate=pl.CostEstimate(flops=2 * flops, bytes_accessed=10**6, transcendentals=0),
        name="last_bins" if last else "add_bins",
    )(*operands)


def per_device(strain, templates, live_count, chi_edges, shifts):
    small = small_numbers(chi_edges, live_count, shifts)
    (bin_of, turned, table, turn), binned = prepare_tables(small)
    wide, stat = prepare_templates(templates, small)

    shard, even = lax.optimization_barrier((strain[0], lax.axis_index("dt") % 2 == 0))
    x = jnp.transpose(shard, (2, 1, 0, 3)).reshape(JS, 2 * NDET, 1, FB)
    got = {0: x}
    for dx in (2, 3, 1):
        got[dx] = swap_with(x, across(dx=dx))
    x = jnp.concatenate([got[dx] for dx in range(4)], axis=2)
    x, turned = lax.optimization_barrier((x, turned))
    got = swap_with(x, across(dy=1))
    x, got, wide = lax.optimization_barrier((x, got, wide))
    x = jnp.concatenate([jnp.where(even, x, got), jnp.where(even, got, x)], axis=2)
    shared = (bin_of, table, turn, wide, turned)

    def to_core(piece):
        return swap_with(piece, across(dcore=1))

    def after(value, binned):
        value, first = lax.optimization_barrier((value, binned[0]))
        return value, [first, *binned[1:]]

    p0 = x.reshape(1, JS, 2 * ROWS, FB)
    q0 = to_core(p0)
    p1 = swap_with(p0, step_move(0))
    p2 = swap_with(p0, step_move(1))
    binned = add_bins((p0, q0), ((0, 1, 0), (0, 1, 1)), shared, binned)
    (p1, p2), binned = after((p1, p2), binned)
    q1, q2 = to_core(p1), to_core(p2)
    p3 = swap_with(p1, step_move(1))
    p45 = swap_with(jnp.concatenate([p0, p1], axis=0), step_move(2))
    binned = add_bins((p1, q1), ((1, 1, 0), (1, 1, 1)), shared, binned)
    binned = add_bins((p2, q2), ((2, 1, 0), (2, 1, 1)), shared, binned)
    (p3, p45), binned = after((p3, p45), binned)
    p67 = swap_with(jnp.concatenate([p2, p3], axis=0), step_move(2))
    q3, q45 = to_core(p3), to_core(p45)
    binned = add_bins((p3, q3), ((3, 1, 0), (3, 1, 1)), shared, binned)
    binned = add_bins((p45, q45), ((4, 2, 0), (4, 2, 1)), shared, binned)
    p67, binned = after(p67, binned)
    q67 = to_core(p67)
    binned = add_bins((p67,), ((6, 2, 0),), shared, binned)
    best = add_bins((q67,), ((6, 2, 1),), shared, binned, stat)[-1]
    for move in (across(dcore=1), across(dz=1), across(dz=3), across(dy=2)):
        best = jnp.maximum(best, swap_with(best, move))
    return best[:, None, :]


def solution(mesh):
    in_specs = (
        P("dt", None, None, "tmpl", None),
        P(("dt", "tmpl"), None, None, None),
        P("dt", "tmpl"),
        P(("dt", "tmpl"), None),
        P(),
    )
    out_specs = P(None, "dt", None)
    return jax.shard_map(
        per_device, mesh=mesh, in_specs=in_specs, out_specs=out_specs, check_vma=False
    )
```

```python
import functools
import math

import jax
import jax.numpy as jnp
from jax import lax
from jax.experimental import pallas as pl
from jax.experimental.pallas import tpu as pltpu
from jax.sharding import PartitionSpec as P

FB = 256
NBLK = 96
NFFT = 1048576
FLOW = 5120
STRIDE = 4097
NBIN = 16
TW = 128
MARGIN = 64
WIN = 16
LANES = 128
SPREAD = 40
NWIN = TW // WIN
NDET = 3
SEGS = 8
SLOTS = 12
NSL = 16
JS = NBLK // NSL
ROWS = NDET * SEGS
EPSILON = 1e-05
TWO_PI = 2.0 * math.pi
AXES = ("dt", "tmpl")
VMEM = 16 * 1024 * 1024


def place_of(index):
    dt, tm = divmod(index, 16)
    return (dt // 2, (tm // 8) * 2 + dt % 2, (tm // 2) % 4, tm % 2)


def index_of(x, y, z, core):
    return (x * 2 + y % 2) * 16 + (y // 2) * 8 + z * 2 + core


def across(dx=0, dy=0, dz=0, dcore=0):
    return lambda x, y, z, core: (x ^ dx, y ^ dy, z ^ dz, core ^ dcore)


def swap_with(value, move):
    pairs = [(index, index_of(*move(*place_of(index)))) for index in range(128)]
    return lax.ppermute(value, AXES, pairs)


STEPS = (
    ({"dy": 3}, {"dz": 3}),
    ({"dz": 1}, {"dz": 1}),
    ({"dz": 3}, {"dy": 3}),
)


def step_move(step):
    first, second = across(**STEPS[step][0]), across(**STEPS[step][1])
    return lambda x, y, z, core: (second if core else first)(x, y, z, core)


def slice_of(piece, other):
    tm = lax.axis_index("tmpl")
    y_hi, z, core = tm // 8, (tm // 2) % 4, (tm % 2) ^ other
    change = []
    for which in range(2):
        dy = dz = 0
        for step in range(3):
            if piece >> step & 1:
                dy ^= STEPS[step][which].get("dy", 0) // 2
                dz ^= STEPS[step][which].get("dz", 0)
        change.append((dy, dz))
    dy = jnp.where(core == 0, change[0][0], change[1][0])
    dz = jnp.where(core == 0, change[0][1], change[1][1])
    return (y_hi ^ dy) * 8 + (z ^ dz) * 2 + core


def segment_at(place):
    return ((lax.axis_index("dt") // 2) ^ (place & 3)) * 2 + (place >> 2)


def circle(turns):
    turns = turns + NFFT // 8
    quarter = (turns >> 18) & 3
    rest = (turns & (NFFT // 4 - 1)) - NFFT // 8
    angle = rest.astype(jnp.float32) * jnp.float32(TWO_PI / NFFT)
    square = angle * angle
    cosine = 1.0 + square * (-1 / 2 + square * (1 / 24 + square * (-1 / 720 + square * (1 / 40320))))
    sine = angle * (1.0 + square * (-1 / 6 + square * (1 / 120 + square * (-1 / 5040 + square * (1 / 362880)))))
    odd = (quarter & 1) == 1
    real, imag = jnp.where(odd, -sine, cosine), jnp.where(odd, cosine, sine)
    return jnp.where(quarter >= 2, -real, real), jnp.where(quarter >= 2, -imag, imag)


def counted(shape, axis):
    return lax.broadcasted_iota(jnp.int32, shape, axis)


def tables_kernel(small_ref, bin_ref, turned_ref, table_ref, turn_ref, *refs):
    binned, (now_ref,) = refs[:SLOTS], refs[SLOTS:]
    for ref in binned:
        ref[...] = jnp.zeros_like(ref)

    cosine, sine = circle(counted((FB, TW), 0) * counted((FB, TW), 1) * STRIDE)
    table_ref[:FB, :TW] = cosine.astype(jnp.bfloat16)
    table_ref[:FB, TW:] = sine.astype(jnp.bfloat16)
    table_ref[FB:, :TW] = (-sine).astype(jnp.bfloat16)
    table_ref[FB:, TW:] = cosine.astype(jnp.bfloat16)
    shape = (NSL, 8, TW)
    number = FLOW // FB + counted(shape, 0) * JS + counted(shape, 1)
    turn_ref[0], turn_ref[1] = circle(number * counted(shape, 2) * FB)

    place = counted((ROWS, LANES), 0) & (SEGS - 1)
    here = segment_at(place) == counted((ROWS, LANES), 1)
    spread = [jnp.broadcast_to(small_ref[SLOTS + d:SLOTS + d + 1, :], (SEGS, LANES)) for d in range(NDET)]
    held = jnp.where(here, jnp.concatenate(spread, axis=0), 0).astype(jnp.float32)
    first = MARGIN + jnp.sum(held, axis=1, keepdims=True).astype(jnp.int32)
    now_ref[0], now_ref[1] = circle(first * (FLOW + counted((1, FB), 1)) * STRIDE)
    pc, ps = circle(jnp.broadcast_to(first * FB, (ROWS, TW)))
    pc, ps = jnp.concatenate([pc, pc], axis=1), jnp.concatenate([ps, ps], axis=1)

    def one_block(j, carry):
        rc, rs = now_ref[0], now_ref[1]
        turned_ref[j, 0] = rc
        turned_ref[j, 1] = rs
        now_ref[0] = rc * pc - rs * ps
        now_ref[1] = rc * ps + rs * pc
        return carry

    lax.fori_loop(0, NBLK, one_block, 0)

    lane = counted((SLOTS, LANES), 1)
    bin_of = jnp.zeros((SLOTS, LANES), jnp.int32)
    for e in range(NBIN - 1):
        bin_of = bin_of + (small_ref[:SLOTS, e:e + 1] <= lane).astype(jnp.int32)
    digit = counted((LANES, LANES), 0) - JS * counted((LANES, LANES), 1)
    held = (digit >= 0) & (digit < JS)
    weight = jnp.where(held, 1 << (4 * jnp.where(held, digit, 0)), 0).astype(jnp.float32)
    digits = bin_of.astype(jnp.float32).astype(jnp.bfloat16)
    bin_ref[...] = jnp.dot(digits, weight.astype(jnp.bfloat16), preferred_element_type=jnp.float32)


def templates_kernel(templ_ref, small_ref, wide_ref, spread_ref, stat_ref):
    stat_ref[...] = jnp.zeros_like(stat_ref)
    block = counted((NBLK, LANES), 0)
    at_lane = counted((1, LANES), 1)
    live_count = small_ref[SLOTS + NDET:SLOTS + NDET + 1, :]
    for k in range(SLOTS):
        h = templ_ref[k, 0].astype(jnp.float32)
        i = templ_ref[k, 1].astype(jnp.float32)
        wide_ref[k, 0] = h
        wide_ref[k, 1] = h + i
        wide_ref[k, 2] = h - i
        power = jnp.sum(h * h + i * i, axis=1, keepdims=True)
        upper = small_ref[k:k + 1, :]
        lower = jnp.where(at_lane == 0, 0, pltpu.roll(upper, 1, 1))
        inside = jnp.where((block >= lower) & (block < upper), power, 0.0)
        in_bins = jnp.sum(inside, axis=0, keepdims=True)
        sigma2 = jnp.sum(power, axis=0, keepdims=True) + EPSILON
        frac = (in_bins + EPSILON) / sigma2
        inv = pltpu.roll(1.0 / (frac * sigma2), NBIN, 1)
        live = (k < live_count).astype(jnp.float32)
        row = jnp.where(at_lane == 2 * NBIN, 0.5 / sigma2, live)
        row = jnp.where(at_lane < 2 * NBIN, inv, row)
        stat_ref[k:k + 1, :] = jnp.where(at_lane < NBIN, frac, row)
    columns = stat_ref[...].T
    for k in range(SLOTS):
        spread_ref[k] = jnp.broadcast_to(columns[:SPREAD, k:k + 1], (SPREAD, LANES))


def whole():
    return pl.BlockSpec(memory_space=pltpu.VMEM)


BINNED = [jax.ShapeDtypeStruct((NBIN, ROWS, 2 * TW), jnp.float32)] * SLOTS


def small_numbers(edges, live_count, shifts):
    return jnp.concatenate([
        jnp.pad(edges, ((0, 0), (0, LANES - NBIN + 1)), constant_values=NBLK),
        jnp.pad(shifts.T, ((0, 0), (0, LANES - SEGS))),
        jnp.broadcast_to(live_count, (1, LANES)),
    ], axis=0)


def prepare_tables(small):
    outs = pl.pallas_call(
        tables_kernel,
        out_shape=[
            jax.ShapeDtypeStruct((SLOTS, LANES), jnp.float32),
            jax.ShapeDtypeStruct((NBLK, 2, ROWS, FB), jnp.float32),
            jax.ShapeDtypeStruct((2 * FB, 2 * TW), jnp.bfloat16),
            jax.ShapeDtypeStruct((2, NSL, 8, TW), jnp.float32),
        ] + BINNED,
        in_specs=[whole()],
        out_specs=[whole()] * (4 + SLOTS),
        scratch_shapes=[pltpu.VMEM((2, ROWS, FB), jnp.float32)],
        compiler_params=pltpu.CompilerParams(vmem_limit_bytes=VMEM),
        cost_estimate=pl.CostEstimate(flops=10**6, bytes_accessed=10**6, transcendentals=0),
        name="prepare_tables",
    )(small)
    return outs[:4], outs[4:]


def prepare_templates(templates, small):
    return pl.pallas_call(
        templates_kernel,
        out_shape=[
            jax.ShapeDtypeStruct((SLOTS, 3, NBLK, FB), jnp.float32),
            jax.ShapeDtypeStruct((SLOTS, SPREAD, LANES), jnp.float32),
        ],
        in_specs=[whole()] * 2,
        out_specs=[whole()] * 2,
        scratch_shapes=[pltpu.VMEM((LANES, LANES), jnp.float32)],
        compiler_params=pltpu.CompilerParams(vmem_limit_bytes=VMEM),
        cost_estimate=pl.CostEstimate(flops=10**6, bytes_accessed=10**6, transcendentals=0),
        name="prepare_templates",
    )(templates, small)


def bins_kernel(parts, last, *refs):
    count = len(parts)
    pieces, refs = refs[:count], refs[count:]
    bin_ref, table_ref, turn_ref, wide_ref, turned_ref = refs[:5]
    refs = refs[5:]
    if last:
        stat_ref, refs = refs[0], refs[1:]
    refs = refs[SLOTS:]
    binned, refs = refs[:SLOTS], refs[SLOTS:]
    if last:
        out_ref, refs = refs[0], refs[1:]
    prod_ref = refs[0]
    if last:
        best_ref = refs[1]

    def product(piece_ref, which, c, jj):
        j = c * JS + jj
        both = piece_ref[which, jj].astype(jnp.float32)
        raw_r, raw_i = both[:ROWS], both[ROWS:]
        rc, rs = turned_ref[j, 0], turned_ref[j, 1]
        sr = raw_r * rc - raw_i * rs
        si = raw_r * rs + raw_i * rc
        su = sr + si
        for pair in range(SLOTS // 2):
            real, imag = [], []
            for k in (2 * pair, 2 * pair + 1):
                h = wide_ref[k, 0, pl.ds(j, 1), :]
                v = wide_ref[k, 1, pl.ds(j, 1), :]
                w = wide_ref[k, 2, pl.ds(j, 1), :]
                k1 = h * su
                real.append(k1 - si * w)
                imag.append(k1 - sr * v)
            base = jj * SLOTS * ROWS + 2 * ROWS * pair
            rows = slice(base, base + 2 * ROWS)
            prod_ref[rows, :FB] = jnp.concatenate(real, axis=0).astype(jnp.bfloat16)
            prod_ref[rows, FB:] = jnp.concatenate(imag, axis=0).astype(jnp.bfloat16)

    def post(c, jj, digits, series):
        cos = turn_ref[0, c, jj:jj + 1, :]
        sin = turn_ref[1, c, jj:jj + 1, :]
        for k in range(SLOTS):
            b = (digits[k] >> (4 * jj)) & (NBIN - 1)
            re = series[k * ROWS:(k + 1) * ROWS, :TW]
            im = series[k * ROWS:(k + 1) * ROWS, TW:]
            binned[k][b, :, :TW] += cos * re - sin * im
            binned[k][b, :, TW:] += cos * im + sin * re

    for piece_ref, (first, amount, other) in zip(pieces, parts):
        for which in range(amount):
            c = slice_of(first + which, other)
            slot_lane = lax.broadcasted_iota(jnp.int32, (SLOTS, LANES), 1)
            packed = jnp.sum(jnp.where(slot_lane == c, bin_ref[...], 0.0), axis=1, keepdims=True).astype(jnp.int32)
            digits = [packed[k, 0] for k in range(SLOTS)]
            for jj in range(JS):
                product(piece_ref, which, c, jj)
            half = JS // 2
            size = half * SLOTS * ROWS
            for h in range(2):
                series = jnp.dot(
                    prod_ref[h * size:(h + 1) * size], table_ref[...], preferred_element_type=jnp.float32
                )
                for m in range(half):
                    post(c, h * half + m, digits, series[m * SLOTS * ROWS:(m + 1) * SLOTS * ROWS])

    if last:
        best = jnp.zeros((SEGS, TW), jnp.float32)
        for k in range(SLOTS):
            total = binned[k][0]
            for b in range(1, NBIN):
                total = total + binned[k][b]
            chi = jnp.zeros((ROWS, TW), jnp.float32)
            for b in range(NBIN):
                share = jnp.concatenate([stat_ref[k, b:b + 1, :]] * 2, axis=1)
                gap = binned[k][b] - share * total
                gap = gap * gap
                chi = chi + (gap[:, :TW] + gap[:, TW:]) * stat_ref[k, NBIN + b:NBIN + b + 1, :]
            power = total * total
            snr2 = (power[:, :TW] + power[:, TW:]) * stat_ref[k, 2 * NBIN:2 * NBIN + 1, :]
            reduced = chi / (2.0 * NBIN - 2.0)
            cube = (1.0 + reduced * reduced * reduced) * 0.5
            factor = jnp.where(reduced > 1.0, jnp.exp(jnp.log(cube) * (-1.0 / 3.0)), 1.0)
            new2 = snr2 * factor
            net2 = new2[:SEGS] + new2[SEGS:2 * SEGS] + new2[2 * SEGS:]
            best = jnp.where(stat_ref[k, 2 * NBIN + 1:2 * NBIN + 2, :] > 0.5, jnp.maximum(best, net2), best)
        best = jnp.sqrt(best)
        best_ref[...] = jnp.concatenate(
            [jnp.max(best[:, w * WIN:(w + 1) * WIN], axis=1, keepdims=True) for w in range(NWIN)], axis=1
        )
        for place in range(SEGS):
            out_ref[pl.ds(segment_at(place), 1), :] = best_ref[place:place + 1, :]


def add_bins(pieces, parts, shared, binned, stat=None):
    last = stat is not None
    operands = [*pieces, *shared] + ([stat] if last else []) + list(binned)
    first = len(operands) - SLOTS
    out_shape = list(BINNED)
    scratch = [
        pltpu.VMEM((JS * SLOTS * ROWS, 2 * FB), jnp.bfloat16),
    ]
    if last:
        out_shape.append(jax.ShapeDtypeStruct((SEGS, NWIN), jnp.float32))
        scratch.append(pltpu.VMEM((SEGS, NWIN), jnp.float32))
    flops = sum(part[1] for part in parts) * 2 * JS * SLOTS * ROWS * 2 * FB * 2 * TW
    return pl.pallas_call(
        functools.partial(bins_kernel, parts, last),
        out_shape=out_shape,
        in_specs=[whole()] * len(operands),
        out_specs=[whole()] * len(out_shape),
        scratch_shapes=scratch,
        input_output_aliases={first + k: k for k in range(SLOTS)},
        compiler_params=pltpu.CompilerParams(vmem_limit_bytes=VMEM),
        cost_estimate=pl.CostEstimate(flops=2 * flops, bytes_accessed=10**6, transcendentals=0),
        name="last_bins" if last else "add_bins",
    )(*operands)


def per_device(strain, templates, live_count, chi_edges, shifts):
    small = small_numbers(chi_edges, live_count, shifts)
    (bin_of, turned, table, turn), binned = prepare_tables(small)
    wide, stat = prepare_templates(templates, small)

    shard, even = lax.optimization_barrier((strain[0], lax.axis_index("dt") % 2 == 0))
    got = {0: shard}
    for dx in (2, 3, 1):
        got[dx] = swap_with(shard, across(dx=dx))
    pieces = [jnp.transpose(got[dx], (2, 1, 0, 3)).reshape(JS, 2 * NDET, 1, FB) for dx in range(4)]
    x = jnp.concatenate(pieces, axis=2)
    x, turned = lax.optimization_barrier((x, turned))
    got = swap_with(x, across(dy=1))
    x, got, wide = lax.optimization_barrier((x, got, wide))
    x = jnp.concatenate([jnp.where(even, x, got), jnp.where(even, got, x)], axis=2)
    shared = (bin_of, table, turn, wide, turned)

    def to_core(piece):
        return swap_with(piece, across(dcore=1))

    def after(value, binned):
        value, first = lax.optimization_barrier((value, binned[0]))
        return value, [first, *binned[1:]]

    p0 = x.reshape(1, JS, 2 * ROWS, FB)
    q0 = to_core(p0)
    p1 = swap_with(p0, step_move(0))
    p2 = swap_with(p0, step_move(1))
    binned = add_bins((p0, q0), ((0, 1, 0), (0, 1, 1)), shared, binned)
    (p1, p2), binned = after((p1, p2), binned)
    q1, q2 = to_core(p1), to_core(p2)
    p3 = swap_with(p1, step_move(1))
    p45 = swap_with(jnp.concatenate([p0, p1], axis=0), step_move(2))
    binned = add_bins((p1, q1), ((1, 1, 0), (1, 1, 1)), shared, binned)
    binned = add_bins((p2, q2), ((2, 1, 0), (2, 1, 1)), shared, binned)
    (p3, p45), binned = after((p3, p45), binned)
    p67 = swap_with(jnp.concatenate([p2, p3], axis=0), step_move(2))
    q3, q45 = to_core(p3), to_core(p45)
    binned = add_bins((p3, q3), ((3, 1, 0), (3, 1, 1)), shared, binned)
    binned = add_bins((p45, q45), ((4, 2, 0), (4, 2, 1)), shared, binned)
    p67, binned = after(p67, binned)
    q67 = to_core(p67)
    binned = add_bins((p67,), ((6, 2, 0),), shared, binned)
    best = add_bins((q67,), ((6, 2, 1),), shared, binned, stat)[-1]
    for move in (across(dcore=1), across(dz=1), across(dz=3), across(dy=2)):
        best = jnp.maximum(best, swap_with(best, move))
    return best[:, None, :]


def solution(mesh):
    in_specs = (
        P("dt", None, None, "tmpl", None),
        P(("dt", "tmpl"), None, None, None),
        P("dt", "tmpl"),
        P(("dt", "tmpl"), None),
        P(),
    )
    out_specs = P(None, "dt", None)
    return jax.shard_map(
        per_device, mesh=mesh, in_specs=in_specs, out_specs=out_specs, check_vma=False
    )
```

```python
import functools
import math

import jax
import jax.numpy as jnp
from jax import lax
from jax.experimental import pallas as pl
from jax.experimental.pallas import tpu as pltpu
from jax.sharding import PartitionSpec as P

FB = 256
NBLK = 96
NFFT = 1048576
FLOW = 5120
STRIDE = 4097
NBIN = 16
TW = 128
MARGIN = 64
WIN = 16
LANES = 128
SPREAD = 40
NWIN = TW // WIN
NDET = 3
SEGS = 8
SLOTS = 12
NSL = 16
JS = NBLK // NSL
ROWS = NDET * SEGS
EPSILON = 1e-05
TWO_PI = 2.0 * math.pi
AXES = ("dt", "tmpl")
VMEM = 16 * 1024 * 1024


def place_of(index):
    dt, tm = divmod(index, 16)
    return (dt // 2, (tm // 8) * 2 + dt % 2, (tm // 2) % 4, tm % 2)


def index_of(x, y, z, core):
    return (x * 2 + y % 2) * 16 + (y // 2) * 8 + z * 2 + core


def across(dx=0, dy=0, dz=0, dcore=0):
    return lambda x, y, z, core: (x ^ dx, y ^ dy, z ^ dz, core ^ dcore)


def swap_with(value, move):
    pairs = [(index, index_of(*move(*place_of(index)))) for index in range(128)]
    return lax.ppermute(value, AXES, pairs)


STEPS = (
    ({"dy": 3}, {"dz": 3}),
    ({"dz": 1}, {"dz": 1}),
    ({"dz": 3}, {"dy": 3}),
)


def step_move(step):
    first, second = across(**STEPS[step][0]), across(**STEPS[step][1])
    return lambda x, y, z, core: (second if core else first)(x, y, z, core)


def slice_of(piece, other):
    tm = lax.axis_index("tmpl")
    y_hi, z, core = tm // 8, (tm // 2) % 4, (tm % 2) ^ other
    change = []
    for which in range(2):
        dy = dz = 0
        for step in range(3):
            if piece >> step & 1:
                dy ^= STEPS[step][which].get("dy", 0) // 2
                dz ^= STEPS[step][which].get("dz", 0)
        change.append((dy, dz))
    dy = jnp.where(core == 0, change[0][0], change[1][0])
    dz = jnp.where(core == 0, change[0][1], change[1][1])
    return (y_hi ^ dy) * 8 + (z ^ dz) * 2 + core


def segment_at(place):
    return ((lax.axis_index("dt") // 2) ^ (place & 3)) * 2 + (place >> 2)


def circle(turns):
    turns = turns + NFFT // 8
    quarter = (turns >> 18) & 3
    rest = (turns & (NFFT // 4 - 1)) - NFFT // 8
    angle = rest.astype(jnp.float32) * jnp.float32(TWO_PI / NFFT)
    square = angle * angle
    cosine = 1.0 + square * (-1 / 2 + square * (1 / 24 + square * (-1 / 720 + square * (1 / 40320))))
    sine = angle * (1.0 + square * (-1 / 6 + square * (1 / 120 + square * (-1 / 5040 + square * (1 / 362880)))))
    odd = (quarter & 1) == 1
    real, imag = jnp.where(odd, -sine, cosine), jnp.where(odd, cosine, sine)
    return jnp.where(quarter >= 2, -real, real), jnp.where(quarter >= 2, -imag, imag)


def counted(shape, axis):
    return lax.broadcasted_iota(jnp.int32, shape, axis)


def tables_kernel(small_ref, bin_ref, turned_ref, table_ref, turn_ref, *refs):
    binned, (now_ref,) = refs[:SLOTS], refs[SLOTS:]
    for ref in binned:
        ref[...] = jnp.zeros_like(ref)

    cosine, sine = circle(counted((FB, TW), 0) * counted((FB, TW), 1) * STRIDE)
    table_ref[:FB, :TW] = cosine.astype(jnp.bfloat16)
    table_ref[:FB, TW:] = sine.astype(jnp.bfloat16)
    table_ref[FB:, :TW] = (-sine).astype(jnp.bfloat16)
    table_ref[FB:, TW:] = cosine.astype(jnp.bfloat16)
    shape = (NSL, 8, TW)
    number = FLOW // FB + counted(shape, 0) * JS + counted(shape, 1)
    turn_ref[0], turn_ref[1] = circle(number * counted(shape, 2) * FB)

    place = counted((ROWS, LANES), 0) & (SEGS - 1)
    here = segment_at(place) == counted((ROWS, LANES), 1)
    spread = [jnp.broadcast_to(small_ref[SLOTS + d:SLOTS + d + 1, :], (SEGS, LANES)) for d in range(NDET)]
    held = jnp.where(here, jnp.concatenate(spread, axis=0), 0).astype(jnp.float32)
    first = MARGIN + jnp.sum(held, axis=1, keepdims=True).astype(jnp.int32)
    now_ref[0], now_ref[1] = circle(first * (FLOW + counted((1, FB), 1)) * STRIDE)
    pc, ps = circle(jnp.broadcast_to(first * FB, (ROWS, TW)))
    pc, ps = jnp.concatenate([pc, pc], axis=1), jnp.concatenate([ps, ps], axis=1)

    def one_block(j, carry):
        rc, rs = now_ref[0], now_ref[1]
        turned_ref[j, 0] = rc
        turned_ref[j, 1] = rs
        now_ref[0] = rc * pc - rs * ps
        now_ref[1] = rc * ps + rs * pc
        return carry

    lax.fori_loop(0, NBLK, one_block, 0)

    lane = counted((SLOTS, LANES), 1)
    bin_of = jnp.zeros((SLOTS, LANES), jnp.int32)
    for e in range(NBIN - 1):
        bin_of = bin_of + (small_ref[:SLOTS, e:e + 1] <= lane).astype(jnp.int32)
    digit = counted((LANES, LANES), 0) - JS * counted((LANES, LANES), 1)
    held = (digit >= 0) & (digit < JS)
    weight = jnp.where(held, 1 << (4 * jnp.where(held, digit, 0)), 0).astype(jnp.float32)
    digits = bin_of.astype(jnp.float32).astype(jnp.bfloat16)
    bin_ref[...] = jnp.dot(digits, weight.astype(jnp.bfloat16), preferred_element_type=jnp.float32)


def templates_kernel(templ_ref, small_ref, wide_ref, spread_ref, stat_ref):
    stat_ref[...] = jnp.zeros_like(stat_ref)
    block = counted((NBLK, LANES), 0)
    at_lane = counted((1, LANES), 1)
    live_count = small_ref[SLOTS + NDET:SLOTS + NDET + 1, :]
    for k in range(SLOTS):
        h = templ_ref[k, 0].astype(jnp.float32)
        i = templ_ref[k, 1].astype(jnp.float32)
        wide_ref[k, 0] = h
        wide_ref[k, 1] = h + i
        wide_ref[k, 2] = h - i
        power = jnp.sum(h * h + i * i, axis=1, keepdims=True)
        upper = small_ref[k:k + 1, :]
        lower = jnp.where(at_lane == 0, 0, pltpu.roll(upper, 1, 1))
        inside = jnp.where((block >= lower) & (block < upper), power, 0.0)
        in_bins = jnp.sum(inside, axis=0, keepdims=True)
        sigma2 = jnp.sum(power, axis=0, keepdims=True) + EPSILON
        frac = (in_bins + EPSILON) / sigma2
        inv = pltpu.roll(1.0 / (frac * sigma2), NBIN, 1)
        live = (k < live_count).astype(jnp.float32)
        row = jnp.where(at_lane == 2 * NBIN, 0.5 / sigma2, live)
        row = jnp.where(at_lane < 2 * NBIN, inv, row)
        stat_ref[k:k + 1, :] = jnp.where(at_lane < NBIN, frac, row)
    columns = stat_ref[...].T
    for k in range(SLOTS):
        spread_ref[k] = jnp.broadcast_to(columns[:SPREAD, k:k + 1], (SPREAD, LANES))


def whole():
    return pl.BlockSpec(memory_space=pltpu.VMEM)


BINNED = [jax.ShapeDtypeStruct((NBIN, ROWS, 2 * TW), jnp.float32)] * SLOTS


def small_numbers(edges, live_count, shifts):
    return jnp.concatenate([
        jnp.pad(edges, ((0, 0), (0, LANES - NBIN + 1)), constant_values=NBLK),
        jnp.pad(shifts.T, ((0, 0), (0, LANES - SEGS))),
        jnp.broadcast_to(live_count, (1, LANES)),
    ], axis=0)


def prepare_tables(small):
    outs = pl.pallas_call(
        tables_kernel,
        out_shape=[
            jax.ShapeDtypeStruct((SLOTS, LANES), jnp.float32),
            jax.ShapeDtypeStruct((NBLK, 2, ROWS, FB), jnp.float32),
            jax.ShapeDtypeStruct((2 * FB, 2 * TW), jnp.bfloat16),
            jax.ShapeDtypeStruct((2, NSL, 8, TW), jnp.float32),
        ] + BINNED,
        in_specs=[whole()],
        out_specs=[whole()] * (4 + SLOTS),
        scratch_shapes=[pltpu.VMEM((2, ROWS, FB), jnp.float32)],
        compiler_params=pltpu.CompilerParams(vmem_limit_bytes=VMEM),
        cost_estimate=pl.CostEstimate(flops=10**6, bytes_accessed=10**6, transcendentals=0),
        name="prepare_tables",
    )(small)
    return outs[:4], outs[4:]


def prepare_templates(templates, small):
    return pl.pallas_call(
        templates_kernel,
        out_shape=[
            jax.ShapeDtypeStruct((SLOTS, 3, NBLK, FB), jnp.float32),
            jax.ShapeDtypeStruct((SLOTS, SPREAD, LANES), jnp.float32),
        ],
        in_specs=[whole()] * 2,
        out_specs=[whole()] * 2,
        scratch_shapes=[pltpu.VMEM((LANES, LANES), jnp.float32)],
        compiler_params=pltpu.CompilerParams(vmem_limit_bytes=VMEM),
        cost_estimate=pl.CostEstimate(flops=10**6, bytes_accessed=10**6, transcendentals=0),
        name="prepare_templates",
    )(templates, small)


def bins_kernel(parts, last, *refs):
    count = len(parts)
    pieces, refs = refs[:count], refs[count:]
    bin_ref, table_ref, turn_ref, wide_ref, turned_ref = refs[:5]
    refs = refs[5:]
    if last:
        stat_ref, refs = refs[0], refs[1:]
    refs = refs[SLOTS:]
    binned, refs = refs[:SLOTS], refs[SLOTS:]
    if last:
        out_ref, refs = refs[0], refs[1:]
    prod_ref = refs[0]
    if last:
        best_ref = refs[1]

    def product(piece_ref, which, c, jj):
        j = c * JS + jj
        both = piece_ref[which, jj].astype(jnp.float32)
        raw_r, raw_i = both[:ROWS], both[ROWS:]
        rc, rs = turned_ref[j, 0], turned_ref[j, 1]
        sr = raw_r * rc - raw_i * rs
        si = raw_r * rs + raw_i * rc
        su = sr + si
        for pair in range(SLOTS // 2):
            real, imag = [], []
            for k in (2 * pair, 2 * pair + 1):
                h = wide_ref[k, 0, pl.ds(j, 1), :]
                v = wide_ref[k, 1, pl.ds(j, 1), :]
                w = wide_ref[k, 2, pl.ds(j, 1), :]
                k1 = h * su
                real.append(k1 - si * w)
                imag.append(k1 - sr * v)
            base = jj * SLOTS * ROWS + 2 * ROWS * pair
            rows = slice(base, base + 2 * ROWS)
            prod_ref[rows, :FB] = jnp.concatenate(real, axis=0).astype(jnp.bfloat16)
            prod_ref[rows, FB:] = jnp.concatenate(imag, axis=0).astype(jnp.bfloat16)

    def post(c, jj, digits, series):
        cos = turn_ref[0, c, jj:jj + 1, :]
        sin = turn_ref[1, c, jj:jj + 1, :]
        for k in range(SLOTS):
            b = (digits[k] >> (4 * jj)) & (NBIN - 1)
            re = series[k * ROWS:(k + 1) * ROWS, :TW]
            im = series[k * ROWS:(k + 1) * ROWS, TW:]
            binned[k][b, :, :TW] += cos * re - sin * im
            binned[k][b, :, TW:] += cos * im + sin * re

    for piece_ref, (first, amount, other) in zip(pieces, parts):
        for which in range(amount):
            c = slice_of(first + which, other)
            slot_lane = lax.broadcasted_iota(jnp.int32, (SLOTS, LANES), 1)
            packed = jnp.sum(jnp.where(slot_lane == c, bin_ref[...], 0.0), axis=1, keepdims=True).astype(jnp.int32)
            digits = [packed[k, 0] for k in range(SLOTS)]
            for jj in range(JS):
                product(piece_ref, which, c, jj)
            half = JS // 2
            size = half * SLOTS * ROWS
            for h in range(2):
                series = jnp.dot(
                    prod_ref[h * size:(h + 1) * size], table_ref[...], preferred_element_type=jnp.float32
                )
                for m in range(half):
                    post(c, h * half + m, digits, series[m * SLOTS * ROWS:(m + 1) * SLOTS * ROWS])

    if last:
        best = jnp.zeros((SEGS, TW), jnp.float32)
        for k in range(SLOTS):
            total = binned[k][0]
            for b in range(1, NBIN):
                total = total + binned[k][b]
            chi = jnp.zeros((ROWS, TW), jnp.float32)
            for b in range(NBIN):
                share = jnp.concatenate([stat_ref[k, b:b + 1, :]] * 2, axis=1)
                gap = binned[k][b] - share * total
                gap = gap * gap
                chi = chi + (gap[:, :TW] + gap[:, TW:]) * stat_ref[k, NBIN + b:NBIN + b + 1, :]
            power = total * total
            snr2 = (power[:, :TW] + power[:, TW:]) * stat_ref[k, 2 * NBIN:2 * NBIN + 1, :]
            reduced = chi / (2.0 * NBIN - 2.0)
            cube = (1.0 + reduced * reduced * reduced) * 0.5
            factor = jnp.where(reduced > 1.0, jnp.exp(jnp.log(cube) * (-1.0 / 3.0)), 1.0)
            new2 = snr2 * factor
            net2 = new2[:SEGS] + new2[SEGS:2 * SEGS] + new2[2 * SEGS:]
            best = jnp.where(stat_ref[k, 2 * NBIN + 1:2 * NBIN + 2, :] > 0.5, jnp.maximum(best, net2), best)
        best = jnp.sqrt(best)
        best_ref[...] = jnp.concatenate(
            [jnp.max(best[:, w * WIN:(w + 1) * WIN], axis=1, keepdims=True) for w in range(NWIN)], axis=1
        )
        for place in range(SEGS):
            out_ref[pl.ds(segment_at(place), 1), :] = best_ref[place:place + 1, :]


def add_bins(pieces, parts, shared, binned, stat=None):
    last = stat is not None
    operands = [*pieces, *shared] + ([stat] if last else []) + list(binned)
    first = len(operands) - SLOTS
    out_shape = list(BINNED)
    scratch = [
        pltpu.VMEM((JS * SLOTS * ROWS, 2 * FB), jnp.bfloat16),
    ]
    if last:
        out_shape.append(jax.ShapeDtypeStruct((SEGS, NWIN), jnp.float32))
        scratch.append(pltpu.VMEM((SEGS, NWIN), jnp.float32))
    flops = sum(part[1] for part in parts) * 2 * JS * SLOTS * ROWS * 2 * FB * 2 * TW
    return pl.pallas_call(
        functools.partial(bins_kernel, parts, last),
        out_shape=out_shape,
        in_specs=[whole()] * len(operands),
        out_specs=[whole()] * len(out_shape),
        scratch_shapes=scratch,
        input_output_aliases={first + k: k for k in range(SLOTS)},
        compiler_params=pltpu.CompilerParams(vmem_limit_bytes=VMEM),
        cost_estimate=pl.CostEstimate(flops=2 * flops, bytes_accessed=10**6, transcendentals=0),
        name="last_bins" if last else "add_bins",
    )(*operands)


def per_device(strain, templates, live_count, chi_edges, shifts):
    small = small_numbers(chi_edges, live_count, shifts)
    (bin_of, turned, table, turn), binned = prepare_tables(small)
    wide, stat = prepare_templates(templates, small)

    shard, even = lax.optimization_barrier((strain[0], lax.axis_index("dt") % 2 == 0))
    x = jnp.transpose(shard, (2, 1, 0, 3)).reshape(JS, 2 * NDET, 1, FB)
    got = {0: x}
    for dx in (2, 3, 1):
        got[dx] = swap_with(x, across(dx=dx))
    x = jnp.concatenate([got[dx] for dx in range(4)], axis=2)
    x, turned = lax.optimization_barrier((x, turned))
    got = swap_with(x, across(dy=1))
    x, got, wide = lax.optimization_barrier((x, got, wide))
    x = jnp.concatenate([jnp.where(even, x, got), jnp.where(even, got, x)], axis=2)
    shared = (bin_of, table, turn, wide, turned)

    def to_core(piece):
        return swap_with(piece, across(dcore=1))

    def after(value, binned):
        value, first = lax.optimization_barrier((value, binned[0]))
        return value, [first, *binned[1:]]

    p0 = x.reshape(1, JS, 2 * ROWS, FB)
    q0 = to_core(p0)
    p1 = swap_with(p0, step_move(0))
    p2 = swap_with(p0, step_move(1))
    binned = add_bins((p0, q0), ((0, 1, 0), (0, 1, 1)), shared, binned)
    (p1, p2), binned = after((p1, p2), binned)
    q1, q2 = to_core(p1), to_core(p2)
    p3 = swap_with(p1, step_move(1))
    p45 = swap_with(jnp.concatenate([p0, p1], axis=0), step_move(2))
    binned = add_bins((p1, q1), ((1, 1, 0), (1, 1, 1)), shared, binned)
    binned = add_bins((p2, q2), ((2, 1, 0), (2, 1, 1)), shared, binned)
    (p3, p45), binned = after((p3, p45), binned)
    p67 = swap_with(jnp.concatenate([p2, p3], axis=0), step_move(2))
    q3, q45 = to_core(p3), to_core(p45)
    binned = add_bins((p3, p45, q3, q45), ((3, 1, 0), (4, 2, 0), (3, 1, 1), (4, 2, 1)), shared, binned)
    p67, binned = after(p67, binned)
    q67 = to_core(p67)
    binned = add_bins((p67,), ((6, 2, 0),), shared, binned)
    best = add_bins((q67,), ((6, 2, 1),), shared, binned, stat)[-1]
    for move in (across(dcore=1), across(dz=1), across(dz=3), across(dy=2)):
        best = jnp.maximum(best, swap_with(best, move))
    return best[:, None, :]


def solution(mesh):
    in_specs = (
        P("dt", None, None, "tmpl", None),
        P(("dt", "tmpl"), None, None, None),
        P("dt", "tmpl"),
        P(("dt", "tmpl"), None),
        P(),
    )
    out_specs = P(None, "dt", None)
    return jax.shard_map(
        per_device, mesh=mesh, in_specs=in_specs, out_specs=out_specs, check_vma=False
    )
```
